32 devices in a mesh: fsdp: 4 (over z), ctx: 4 (over x, core), tp: 2 (over y).
Axes of the slice: x: 2, y: 2, z: 4, core: 2. Of those that a mesh axis runs over, the one named last changes fastest.
Arguments:
- tokens: bfloat16 [8192, 768], P(('fsdp', 'ctx')), may hold values from -6 to 6
- segments: int32 [4, 2048], P('fsdp'), may hold values from 0 to 23, never falling along the last dimension, each value on 1 to 1538 neighbouring positions
- experts: int32 [8192, 2], P(('fsdp', 'ctx')), may hold values from 0 to 15, all different within a row; in each aligned block of 512 rows (0 to 511, 512 to 1023, ...) at most 128 rows name the same one
- attn_gain: bfloat16 [768], P(('fsdp', 'ctx')), may hold values from 0.5 to 1.5
- qkv_proj: bfloat16 [3, 768, 768], P(None, ('fsdp', 'ctx'), 'tp'), may hold values from -0.3125 to 0.3125
- out_proj: bfloat16 [768, 768], P('tp', ('fsdp', 'ctx')), may hold values from -0.875 to 0.875
- ffn_gain: bfloat16 [768], P(('fsdp', 'ctx')), may hold values from 0.5 to 1.5
- router_proj: bfloat16 [768, 16], P(('fsdp', 'ctx')), may hold values from -0.15625 to 0.15625
- expert_gate_up: bfloat16 [16, 2, 768, 2048], P('ctx', None, 'fsdp', 'tp'), may hold values from -0.21875 to 0.21875
- expert_down: bfloat16 [16, 2048, 768], P('ctx', 'tp', 'fsdp'), may hold values from -2 to 2
- shared_gate_up: bfloat16 [2, 768, 2048], P(None, ('fsdp', 'ctx'), 'tp'), may hold values from -0.21875 to 0.21875
- shared_down: bfloat16 [2048, 768], P('tp', ('fsdp', 'ctx')), may hold values from -0.125 to 0.125
- cotangent: bfloat16 [8192, 768], P(('fsdp', 'ctx')), may hold values from -6 to 6
Outputs:
- layer_out: bfloat16 [8192, 768], P(('fsdp', 'ctx'))
- tokens_grad: float32 [8192, 768], P(('fsdp', 'ctx'))
- attn_gain_grad: float32 [768], P(('fsdp', 'ctx'))
- qkv_grad: float32 [3, 768, 768], P(None, ('fsdp', 'ctx'), 'tp')
- out_grad: float32 [768, 768], P('tp', ('fsdp', 'ctx'))
- ffn_gain_grad: float32 [768], P(('fsdp', 'ctx'))
- router_grad: float32 [768, 16], P(('fsdp', 'ctx'))
- expert_gate_up_grad: float32 [16, 2, 768, 2048], P('ctx', None, 'fsdp', 'tp')
- expert_down_grad: float32 [16, 2048, 768], P('ctx', 'tp', 'fsdp')
- shared_gate_up_grad: float32 [2, 768, 2048], P(None, ('fsdp', 'ctx'), 'tp')
- shared_down_grad: float32 [2048, 768], P('tp', ('fsdp', 'ctx'))
The draws below stay inside these ranges and needn't reach their ends.
Inputs may be any that keep to these rules, and one draw needn't show every extreme that they name: In each aligned block of 512 tokens (the tokens of one device) no expert is named by more than 128 tokens, and some expert reaches 128 in every draw; a token's two experts differ. `segments`: document numbers never fall along a sequence; one document of each sequence has exactly 1538 tokens.
All inputs are finite; a program needn't handle non-finite values.
Results may differ from the reference program's by a relative error of at most 0.015.
The reference program's roundings to bfloat16 on the way count: a program that leaves them out, or rounds other values in their place, can miss the bound.
Values may be sent and summed in bfloat16 or wider, within the bound.
No kernel may reach another device: no remote copies, remote signals or barrier semaphores. Data moves between devices by JAX's collectives and lax.ppermute only.
A program may use at most 192 MiB of HBM per device.

```python
import math
import jax
import jax.numpy as jnp
import numpy as np
from jax import lax

D = 768
H = 12
HD = 64
FF = 2048
FS = 2048
E = 16
ROWS = 512
CAP = 128
LEN = 2048
SEQS = 4
TOKENS = 8192
DOCS = 24


def level_of(stream_key, dims, cuts, smallest, high):
    gain = 1.0
    for axis_at, blocks in cuts:
        steps = jax.random.uniform(jax.random.fold_in(jax.random.fold_in(stream_key, 6), axis_at), (blocks,), jnp.float32, smallest / len(cuts), high / len(cuts))
        gain = gain * jnp.repeat(jnp.exp(steps), dims[axis_at] // blocks).reshape((-1,) + (1,) * (len(dims) - 1 - axis_at))
    return gain


def length_profile(count, total, limit, slope):
    portions = [(1 << 20) // math.isqrt(standing ** slope) + 1 for standing in range(2, count + 1)]
    spare, holding = total - limit - (count - 1), [1] * (count - 1)
    while spare > 0:
        candidates = [i for i in range(count - 1) if holding[i] < limit]
        whole, left = sum([portions[i] for i in candidates]), spare
        for i in candidates:
            more = min(limit - holding[i], max(1, left * portions[i] // whole), spare)
            holding[i] = holding[i] + more
            spare = spare - more
    return np.array([limit] + holding)


def uneven_parts(key, amount, total, most, lean):
    if amount == 2:
        one = jax.random.randint(key, (), max(1, total - most), min(most, total - 1) + 1)
        return jnp.stack([one, total - one])
    lengths = jnp.asarray(length_profile(amount, total, most, lean), jnp.int32)
    pairs = (amount - 1) // 2
    donor, sink = lengths[1:1 + 2 * pairs:2], lengths[2:2 + 2 * pairs:2]
    margin = jnp.minimum(donor - 1, most - sink)
    moved = jax.random.randint(jax.random.fold_in(key, 1), (pairs,), 0, 1 << 20) % (margin + 1)
    lengths = lengths.at[1:1 + 2 * pairs:2].set(donor - moved).at[2:2 + 2 * pairs:2].set(sink + moved)
    return lengths[jax.random.permutation(jax.random.fold_in(key, 2), amount)]


def deal_out(rng, own, number, rows, count, top, bound, skew):
    order = jax.random.permutation(rng, count)
    packed, usual = portions_of(count, rows * top, bound, skew, True), portions_of(count, rows * top, bound, skew, False)
    places = jnp.arange(count)

    def named(lengths, rotation):
        used = int((lengths > 0).sum())
        fixed = max(1, used // 4)
        shifted = fixed + (places - fixed + rotation * (used - fixed)) % max(1, count - fixed)
        return jnp.zeros((count,), jnp.int32).at[order[jnp.where(places < fixed, places, shifted)]].set(jnp.asarray(lengths, jnp.int32))

    lengths = jnp.where(number % 4 == 0, named(packed, number // 4), named(usual, number - number // 4 - 1))
    mixed = jax.random.permutation(jax.random.fold_in(own, 3), count)
    source_of, receiver = mixed[0:count // 2 * 2:2], mixed[1:count // 2 * 2:2]
    room = jnp.minimum(lengths[source_of] - 1, bound - lengths[receiver]) // 2
    room = jnp.where((source_of == order[0]) | (receiver == order[0]) | (lengths[receiver] == 0), 0, jnp.maximum(room, 0))
    shifted = jax.random.randint(jax.random.fold_in(own, 4), (count // 2,), 0, 1 << 20) % (room + 1)
    lengths = lengths.at[source_of].add(-shifted).at[receiver].add(shifted)
    members = jnp.searchsorted(jnp.cumsum(lengths), jnp.arange(rows * top), side="right").astype(jnp.int32)
    grid = members.reshape(top, rows).T
    grid = grid[jax.random.permutation(jax.random.fold_in(own, 1), rows)]
    rotation = jax.random.randint(jax.random.fold_in(own, 2), (rows, 1), 0, top)
    return jnp.take_along_axis(grid, (jnp.arange(top)[None, :] + rotation) % top, axis=1)


def portions_of(amount, total, bound, slope, full):
    weights = [(1 << 20) // math.isqrt(rank ** slope) + 1 for rank in range(1, amount + 1)]
    largest = bound if full else min(bound, max(-(-total // amount), total * weights[0] // sum(weights)))
    least = 1 if total - largest >= amount - 1 else 0
    given, surplus = [largest] + [least] * (amount - 1), total - largest - least * (amount - 1)
    while surplus > 0:
        candidates = [i for i in range(1, amount) if given[i] < largest] or [i for i in range(1, amount) if given[i] < bound]
        pool, remaining = sum([weights[i] for i in candidates]), surplus
        for i in candidates:
            more = min(bound - given[i], max(1, remaining * weights[i] // pool), surplus)
            given[i] = given[i] + more
            surplus = surplus - more
    return np.array(given)


def noise(key, shape, spread, reach, split=(), kind=jnp.bfloat16):
    values = spread * jax.random.normal(key, shape, jnp.float32)
    if split:
        values = values * level_of(key, shape, split, -0.22, 0.18)
    return jnp.clip(values, -reach, reach).astype(kind)


def setup_inputs(seed: int = 0) -> dict:
    key_list = jax.random.split(jax.random.key(seed), 14)
    tokens = noise(key_list[0], (TOKENS, D), 1.0, 6.0, ((0, 16),))
    segments = jax.vmap(lambda own: jnp.searchsorted(jnp.cumsum(uneven_parts(own, DOCS, LEN, 3 * ROWS + 2, 2)), jnp.arange(LEN), side="right"))(jax.random.split(key_list[1], SEQS)).reshape((SEQS, LEN)).astype(jnp.int32)
    experts_keys = jax.random.split(jax.random.fold_in(key_list[2], 1), TOKENS // ROWS)
    experts_turns = jax.random.permutation(jax.random.fold_in(key_list[2], 3), TOKENS // ROWS)
    experts = jax.vmap(lambda own, number: deal_out(jax.random.fold_in(key_list[2], 2), own, number, ROWS, E, 2, CAP, 2))(experts_keys, experts_turns).reshape((TOKENS, 2))
    attn_gain = jnp.clip(1.0 + 0.1 * jax.random.normal(key_list[3], (D,), jnp.float32), 0.5, 1.5).astype(jnp.bfloat16)
    qkv_proj = noise(key_list[4], (3, D, H * HD), (D // 2) ** -0.5, 0.3125, ((1, 16), (2, 2)))
    out_proj = noise(key_list[5], (H * HD, D), (H * HD // 16) ** -0.5, 0.875, ((0, 2), (1, 16)))
    ffn_gain = jnp.clip(1.0 + 0.1 * jax.random.normal(key_list[6], (D,), jnp.float32), 0.5, 1.5).astype(jnp.bfloat16)
    router_proj = noise(key_list[7], (D, E), 0.027, 0.15625, ((0, 16),))
    expert_gate_up = noise(key_list[8], (E, 2, D, FF), D ** -0.5, 0.21875, ((0, 4), (2, 4), (3, 2)))
    expert_down = noise(key_list[9], (E, FF, D), (max(FF // 256, 1)) ** -0.5, 2.0, ((0, 4), (1, 2), (2, 4)))
    shared_gate_up = noise(key_list[10], (2, D, FS), D ** -0.5, 0.21875, ((1, 16), (2, 2)))
    shared_down = noise(key_list[11], (FS, D), FS ** -0.5, 0.125, ((0, 2), (1, 16)))
    cotangent = noise(key_list[12], (TOKENS, D), 1.0, 6.0, ((0, 16),))
    return {"tokens": tokens, "segments": segments, "experts": experts, "attn_gain": attn_gain, "qkv_proj": qkv_proj, "out_proj": out_proj, "ffn_gain": ffn_gain, "router_proj": router_proj, "expert_gate_up": expert_gate_up, "expert_down": expert_down, "shared_gate_up": shared_gate_up, "shared_down": shared_down, "cotangent": cotangent}


eps = 1e-06

@jax.custom_vjp
def low(v):
    return lax.optimization_barrier(v.astype(jnp.bfloat16)).astype(jnp.float32)

@jax.custom_vjp
def low_back(v):
    return v

def low_keep(v):
    return (low(v), None)

def low_pass(kept, grad):
    return (grad,)

def back_keep(v):
    return (v, None)

def back_low(kept, grad):
    return (low(grad),)
low.defvjp(low_keep, low_pass)
low_back.defvjp(back_keep, back_low)

def rotary(values, positions, direction):
    half_dim = values.shape[-1] // 2
    frequency = 10000.0 ** (-jnp.arange(half_dim, dtype=jnp.float32) / half_dim)
    angles = direction * positions.astype(jnp.float32)[:, None] * frequency[None, :]
    cosine = jnp.cos(angles)[:, None, :]
    sine_part = jnp.sin(angles)[:, None, :]
    first = values[..., :half_dim]
    second = values[..., half_dim:]
    return jnp.concatenate([first * cosine - second * sine_part, second * cosine + first * sine_part], axis=-1)

def attend_sequence(inputs):
    queries, key_block, value_block, seq_ids = inputs
    seq_len = queries.shape[0]
    block_size = min(512, seq_len)
    positions = jnp.arange(seq_len, dtype=jnp.int32)

    def one_block(start):
        start = start.astype(jnp.int32)
        q_block = lax.dynamic_slice_in_dim(queries, start, block_size, 0)
        q_pos = lax.dynamic_slice_in_dim(positions, start, block_size, 0)
        q_ids = lax.dynamic_slice_in_dim(seq_ids, start, block_size, 0)
        scores = low_back(jnp.einsum('qhc,khc->hqk', q_block, key_block, precision=lax.Precision.HIGHEST) * HD ** (-0.5))
        allowed = (q_pos[:, None] >= positions[None, :]) & (q_ids[:, None] == seq_ids[None, :])
        weights = jax.nn.softmax(jnp.where(allowed[None], scores, -jnp.inf), axis=-1)
        return jnp.einsum('hqk,khc->qhc', low(weights), value_block, precision=lax.Precision.HIGHEST)
    starts = jnp.arange(seq_len // block_size, dtype=jnp.int32) * block_size
    outputs = lax.map(jax.checkpoint(one_block), starts)
    return outputs.reshape(seq_len, queries.shape[1], queries.shape[2])

def apply_expert(inputs):
    tok_rows, gate_up, down_proj = inputs
    gate_pair = low_back(jnp.einsum('md,jdf->mjf', tok_rows, gate_up, precision=lax.Precision.HIGHEST))
    hidden = low(jax.nn.silu(gate_pair[:, 0]) * gate_pair[:, 1])
    return low_back(jnp.dot(hidden, down_proj, precision=lax.Precision.HIGHEST))

def dispatch_tables(experts):
    total_rows = experts.shape[0]
    blocks = total_rows // ROWS
    expert_ids = experts.reshape(blocks, 2 * ROWS).astype(jnp.int32)
    onehot = (expert_ids[:, :, None] == jnp.arange(E, dtype=jnp.int32)[None, None, :]).astype(jnp.int32)
    slot_index = lax.optimization_barrier(jnp.sum((jnp.cumsum(onehot, axis=1) - onehot) * onehot, axis=2)).astype(jnp.int32)
    block_ids = jnp.arange(blocks, dtype=jnp.int32)[:, None]
    slot_target = (expert_ids * (blocks * CAP) + block_ids * CAP + slot_index).reshape(-1).astype(jnp.int32)
    slot_table = jnp.full((E * blocks * CAP,), 2 * total_rows, jnp.int32).at[slot_target].set(jnp.arange(2 * total_rows, dtype=jnp.int32))
    token_index = jnp.where(slot_table < 2 * total_rows, slot_table // 2, total_rows).astype(jnp.int32)
    return (slot_target, token_index)

def reference(tokens, segments, experts, attn_gain, qkv_proj, out_proj, ffn_gain, router_proj, expert_gate_up, expert_down, shared_gate_up, shared_down, cotangent):
    slot_target, token_index = dispatch_tables(experts)
    seq_len = segments.shape[1]

    def forward(residual, gain_one, qkv_w, out_w, gain_two, router_w, gate_up_w, down_w, shared_gu, shared_dn):
        total_rows = residual.shape[0]
        scale_one = lax.rsqrt(lax.optimization_barrier(jnp.mean(residual * residual, axis=-1, keepdims=True)) + eps)
        normed_one = low(residual * scale_one * gain_one)
        projected = low_back(jnp.einsum('td,jdc->tjc', normed_one, qkv_w, precision=lax.Precision.HIGHEST))
        positions = jnp.arange(total_rows, dtype=jnp.int32) % seq_len
        shaped = projected.reshape(total_rows, 3, H, HD)
        queries = low(rotary(shaped[:, 0], positions, 1.0))
        key_rows = low(rotary(shaped[:, 1], positions, 1.0))
        value_rows = low(shaped[:, 2])
        attended = lax.map(attend_sequence, (queries.reshape(-1, seq_len, H, HD), key_rows.reshape(-1, seq_len, H, HD), value_rows.reshape(-1, seq_len, H, HD), segments))
        mixed = low(low_back(attended.reshape(total_rows, H * HD)))
        middle = residual + low_back(jnp.dot(mixed, out_w, precision=lax.Precision.HIGHEST))
        scale_two = lax.rsqrt(lax.optimization_barrier(jnp.mean(middle * middle, axis=-1, keepdims=True)) + eps)
        normed_two = low(middle * scale_two * gain_two)
        router_probs = jax.nn.softmax(jnp.dot(normed_two, router_w, precision=lax.Precision.HIGHEST), axis=-1)
        gate_values = jnp.take_along_axis(router_probs, experts, axis=1)
        shared_pair = low_back(jnp.einsum('td,jdf->tjf', normed_two, shared_gu, precision=lax.Precision.HIGHEST))
        shared_hidden = low(jax.nn.silu(shared_pair[:, 0]) * shared_pair[:, 1])
        shared_out = low_back(jnp.dot(shared_hidden, shared_dn, precision=lax.Precision.HIGHEST))
        padded = jnp.concatenate([normed_two, jnp.zeros((1, D), jnp.float32)], axis=0)
        expert_rows = padded[token_index].reshape(E, -1, D)
        expert_out = lax.map(jax.checkpoint(apply_expert), (expert_rows, gate_up_w, down_w))
        picked_rows = expert_out.reshape(-1, D)[slot_target].reshape(total_rows, 2, D)
        return middle + shared_out + lax.optimization_barrier(jnp.sum(gate_values[:, :, None] * picked_rows, axis=1))
    floats = tuple((item.astype(jnp.float32) for item in (tokens, attn_gain, qkv_proj, out_proj, ffn_gain, router_proj, expert_gate_up, expert_down, shared_gate_up, shared_down)))
    result, pullback = jax.vjp(forward, *floats)
    grads = pullback(cotangent.astype(jnp.float32))
    return (result.astype(jnp.bfloat16), grads[0], grads[1], grads[2], grads[3], grads[4], grads[5], grads[6], grads[7], grads[8], grads[9])
```

```python
import functools

import jax
import jax.numpy as jnp
from jax import lax
from jax.experimental import pallas as pl
from jax.experimental.pallas import tpu as pltpu
from jax.sharding import PartitionSpec as P

D = 768
HALF = D // 2
HD = 64
E = 16
ROWS = 512
CAP = 128
NEG = -1e30
eps = 1e-06
bf16 = jnp.bfloat16
f32 = jnp.float32
VMEM_LIMIT = 56 * 1024 * 1024


def mm(a, b):
    return lax.dot_general(a, b, (((1,), (0,)), ((), ())), preferred_element_type=f32)


def mm_t(a, b):
    return lax.dot_general(a, b, (((1,), (1,)), ((), ())), preferred_element_type=f32)


def t_mm(a, b):
    return lax.dot_general(a, b, (((0,), (0,)), ((), ())), preferred_element_type=f32)


def sds(shape, dtype):
    return jax.ShapeDtypeStruct(shape, dtype)


SMEM = pl.BlockSpec(memory_space=pltpu.SMEM)
VM = pl.BlockSpec(memory_space=pltpu.VMEM)


def call(body, outs, scratch=(), flops=0, moved=0, name=None):
    def run(scalars, *args):
        return pl.pallas_call(
            body,
            out_shape=outs,
            in_specs=[SMEM] + [VM] * len(args),
            out_specs=jax.tree.map(lambda _: VM, outs),
            scratch_shapes=list(scratch),
            compiler_params=pltpu.CompilerParams(vmem_limit_bytes=VMEM_LIMIT),
            cost_estimate=pl.CostEstimate(flops=flops, bytes_accessed=moved, transcendentals=0),
            name=name,
        )(scalars, *args)

    return run


def partner(v, lane):
    return jnp.where(lane % 64 < 32, pltpu.roll(v, 96, 1), pltpu.roll(v, 32, 1))


def lane_id(rows):
    return lax.broadcasted_iota(jnp.int32, (rows, 128), 1)


def qkv_body(sc, tok, gain, w, cos, sin, a_o, q_o, kv_o):
    x = tok[...].astype(f32)
    scale = lax.rsqrt(jnp.mean(x * x, axis=1, keepdims=True) + eps)
    a = (x * scale * gain[...]).astype(bf16)
    a_o[...] = a
    n = w.shape[1] // 3
    lane = lane_id(ROWS)
    for g in range(3 * n // 128):
        v = mm(a, w[:, g * 128 : (g + 1) * 128])
        lo = g * 128
        if lo < n:
            r = v * cos[...] + partner(v, lane) * sin[...]
            q_o[:, lo : lo + 128] = (r.astype(bf16).astype(f32) * (HD**-0.5)).astype(bf16)
        elif lo < 2 * n:
            r = v * cos[...] + partner(v, lane) * sin[...]
            kv_o[:, lo - n : lo - n + 128] = r.astype(bf16)
        else:
            kv_o[:, lo - n : lo - n + 128] = v.astype(bf16)


def block_bias(c, kb, segc, segq):
    off = pl.multiple_of(kb * ROWS, ROWS)
    kpos = off + lax.broadcasted_iota(jnp.int32, (ROWS, ROWS), 0)
    qpos = c * ROWS + lax.broadcasted_iota(jnp.int32, (ROWS, ROWS), 1)
    ok = (segc[pl.ds(off, ROWS), :] == segq[...]) & (kpos <= qpos)
    return jnp.where(ok, 0.0, NEG)


def attn_body(sc, q, k0, k1, k2, k3, segc, segq, wo, o_o, zown_o, zoth_o, lse_o, kvs, bias, st, ot):
    c, y = sc[0], sc[1]
    nb = c + 1
    n = q.shape[1]
    for r, ref in enumerate((k0, k1, k2, k3)):
        kvs[pl.ds(pl.multiple_of((c ^ r) * ROWS, ROWS), ROWS), :] = ref[...]

    def bias_step(kb, carry):
        bias[pl.ds(pl.multiple_of(kb * ROWS, ROWS), ROWS), :] = block_bias(c, kb, segc, segq)
        return carry

    lax.fori_loop(0, nb, bias_step, 0)
    for h in range(n // HD):
        lo = h * HD
        qh = q[:, lo : lo + HD]

        def score_step(kb, m, lo=lo, qh=qh):
            rows = pl.ds(pl.multiple_of(kb * ROWS, ROWS), ROWS)
            s = mm_t(kvs[rows, lo : lo + HD], qh) + bias[rows, :]
            st[rows, :] = s
            return jnp.maximum(m, jnp.max(s, axis=0, keepdims=True))

        m = lax.fori_loop(0, nb, score_step, jnp.full((1, ROWS), NEG, f32))

        def value_step(kb, carry, lo=lo, m=m):
            total, acc = carry
            rows = pl.ds(pl.multiple_of(kb * ROWS, ROWS), ROWS)
            p = jnp.exp(st[rows, :] - m)
            total = total + jnp.sum(p, axis=0, keepdims=True)
            return total, acc + t_mm(kvs[rows, n + lo : n + lo + HD], p.astype(bf16))

        total, acc = lax.fori_loop(
            0, nb, value_step, (jnp.zeros((1, ROWS), f32), jnp.zeros((HD, ROWS), f32))
        )
        ot[lo : lo + HD, :] = acc / total
        lse_o[h : h + 1, :] = m + jnp.log(total)
    o = ot[...].T.astype(bf16)
    o_o[...] = o
    own = pl.ds(pl.multiple_of(y * HALF, HALF), HALF)
    oth = pl.ds(pl.multiple_of((1 - y) * HALF, HALF), HALF)
    zoth_o[...] = mm_t(o, wo[oth, :]).astype(bf16)
    zown_o[...] = mm_t(o, wo[own, :])


def attn_back_body(
    sc, q, k0, k1, k2, k3, segc, segq, lse, o, zown, zoth, wo, cos, sin, dq_o, dkv_o,
    kvs, bias, do_s, delta, dqt,
):
    c, y = sc[0], sc[1]
    nb = c + 1
    n = q.shape[1]
    heads = n // HD
    for r, ref in enumerate((k0, k1, k2, k3)):
        kvs[pl.ds(pl.multiple_of((c ^ r) * ROWS, ROWS), ROWS), :] = ref[...]

    def bias_step(kb, carry):
        bias[pl.ds(pl.multiple_of(kb * ROWS, ROWS), ROWS), :] = block_bias(c, kb, segc, segq)
        return carry

    lax.fori_loop(0, nb, bias_step, 0)
    own = pl.ds(pl.multiple_of(y * HALF, HALF), HALF)
    oth = pl.ds(pl.multiple_of((1 - y) * HALF, HALF), HALF)
    do = (mm(zown[...], wo[own, :]) + mm(zoth[...], wo[oth, :])).astype(bf16)
    do_s[...] = do
    pick = (
        lax.broadcasted_iota(jnp.int32, (8, n), 1) // HD
        == lax.broadcasted_iota(jnp.int32, (8, n), 0)
    ).astype(f32)
    delta[...] = lax.dot_general(
        pick,
        do.astype(f32) * o[...].astype(f32),
        (((1,), (1,)), ((), ())),
        precision=lax.Precision.HIGHEST,
        preferred_element_type=f32,
    )

    def zero_step(kb, carry):
        dkv_o[kb ^ c] = jnp.zeros((ROWS, 2 * n), bf16)
        return carry

    lax.fori_loop(nb, 4, zero_step, 0)
    for pair in range(heads // 2):
        at = pair * 128

        def step(kb, carry, at=at, pair=pair):
            rows = pl.ds(pl.multiple_of(kb * ROWS, ROWS), ROWS)
            dks, dvs, dqs = [], [], []
            for i in range(2):
                lo = at + i * HD
                h = 2 * pair + i
                kh = kvs[rows, lo : lo + HD]
                vh = kvs[rows, n + lo : n + lo + HD]
                qh = q[:, lo : lo + HD]
                dh = do_s[:, lo : lo + HD]
                p = jnp.exp(mm_t(kh, qh) + bias[rows, :] - lse[h : h + 1, :])
                ds = (p * (mm_t(vh, dh) - delta[h : h + 1, :])).astype(bf16)
                dvs.append(mm(p.astype(bf16), dh))
                dks.append(mm(ds, qh))
                dqs.append(carry[i] + t_mm(kh, ds))
            at_k = kb ^ c
            dkv_o[at_k, :, at : at + 128] = jnp.concatenate(dks, axis=1).astype(bf16)
            dkv_o[at_k, :, n + at : n + at + 128] = jnp.concatenate(dvs, axis=1).astype(bf16)
            return tuple(dqs)

        zero = jnp.zeros((HD, ROWS), f32)
        dqs = lax.fori_loop(0, nb, step, (zero, zero))
        dqt[at : at + HD, :] = dqs[0]
        dqt[at + HD : at + 128, :] = dqs[1]
    lane = lane_id(ROWS)
    for g in range(n // 128):
        v = dqt[g * 128 : (g + 1) * 128, :].T * (HD**-0.5)
        dq_o[:, g * 128 : (g + 1) * 128] = (v * cos[...] - partner(v, lane) * sin[...]).astype(bf16)


def proj_back_body(sc, dq, keep, recv, w, cos, sin, dp_o, own_o, oth_o):
    y = sc[1]
    n = dq.shape[1]
    lane = lane_id(ROWS)
    dp_o[:, :n] = dq[...]
    for g in range(2 * n // 128):
        cols = slice(g * 128, (g + 1) * 128)
        v = keep[:, cols].astype(f32) + recv[:, cols].astype(f32)
        if g < n // 128:
            v = v * cos[...] - partner(v, lane) * sin[...]
        dp_o[:, n + g * 128 : n + (g + 1) * 128] = v.astype(bf16)
    own = pl.ds(pl.multiple_of(y * HALF, HALF), HALF)
    oth = pl.ds(pl.multiple_of((1 - y) * HALF, HALF), HALF)
    oth_o[...] = mm_t(dp_o[...], w[oth, :]).astype(bf16)
    own_o[...] = mm_t(dp_o[...], w[own, :])


def slots_onehot(ids, r):
    i = lax.broadcasted_iota(jnp.int32, (4 * CAP, ROWS), 0)
    hit = (i == ids[2 * r : 2 * r + 1, :]) | (i == ids[2 * r + 1 : 2 * r + 2, :])
    return jnp.where(hit, 1.0, 0.0).astype(bf16)


def pack_body(sc, ids, b0, b1, b2, b3, p0, p1, p2, p3):
    for r, ref in enumerate((b0, b1, b2, b3)):
        rows = mm(slots_onehot(ids, r), ref[...]).astype(bf16)
        for s, out in enumerate((p0, p1, p2, p3)):
            out[r * CAP : (r + 1) * CAP, :] = rows[s * CAP : (s + 1) * CAP, :]


def unpack_body(sc, ids, p0, p1, p2, p3, keep_o, send_o):
    for r in range(4):
        rows = jnp.concatenate(
            [p[r * CAP : (r + 1) * CAP, :] for p in (p0, p1, p2, p3)], axis=0
        )
        tok = t_mm(slots_onehot(ids, r), rows).astype(bf16)
        if r % 2 == 0:
            keep_o[r // 2] = tok
        else:
            send_o[r // 2] = tok


def halves(y, a, b):
    first = y == 0
    return jnp.concatenate([jnp.where(first, a, b), jnp.where(first, b, a)], axis=1)


def ffn_body(routed, sc, xa, xb, wa, wb, gu, dt, rt, *refs):
    if routed:
        refs = refs[len(refs) - 9 :]
        out_o, db_o, rg_o, dgu_o, y_o, x_o, de_o, acc_o, acc_b = refs
    else:
        out_o, db_o, dgu_o, y_o, acc_o, acc_b = refs
    y, e = sc[1], sc[2]
    x = halves(y, xa[...], xb[...])
    w = halves(y, wa[...], wb[...])
    hidden = dt.shape[1]
    if routed:
        lane = lane_id(ROWS)
        logits = jnp.where(lane < E, mm(x, rt[...]), NEG)
        ex = jnp.exp(logits - jnp.max(logits, axis=1, keepdims=True))
        probs = ex / jnp.sum(ex, axis=1, keepdims=True)
        gate = jnp.sum(jnp.where(lane == e, probs, 0.0), axis=1, keepdims=True)
        x_o[0] = x
        de_o[0] = (w.astype(f32) * gate).astype(bf16)
    acc_o[...] = jnp.zeros_like(acc_o)
    acc_b[...] = jnp.zeros_like(acc_b)
    tile = 256

    def step(j, dots):
        lo = pl.multiple_of(j * tile, tile)
        hi = pl.multiple_of(hidden + j * tile, tile)
        g = mm(x, gu[:, pl.ds(lo, tile)])
        u = mm(x, gu[:, pl.ds(hi, tile)])
        h = mm(w, dt[:, pl.ds(lo, tile)])
        sg = 1.0 / (1.0 + jnp.exp(-g))
        act = g * sg
        yv = (act * u).astype(bf16)
        if routed:
            dots = dots + jnp.sum(yv.astype(f32) * h, axis=1, keepdims=True)
            h = h * gate
        dg = (h * u * (sg + act * (1.0 - sg))).astype(bf16)
        du = (h * act).astype(bf16)
        y_o[0, :, pl.ds(lo, tile)] = yv
        dgu_o[0, :, pl.ds(lo, tile)] = dg
        dgu_o[0, :, pl.ds(hi, tile)] = du
        acc_o[...] += mm_t(yv, dt[:, pl.ds(lo, tile)])
        acc_b[...] += mm_t(dg, gu[:, pl.ds(lo, tile)]) + mm_t(du, gu[:, pl.ds(hi, tile)])
        return dots

    dots = lax.fori_loop(0, hidden // tile, step, jnp.zeros((ROWS, 1), f32))
    if routed:
        coef = (dots * gate) * (jnp.where(lane == e, 1.0, 0.0) - probs)
        coef = jnp.where(lane < E, coef, 0.0).astype(bf16)
        acc_b[...] += mm_t(coef, rt[...])
        rg_o[...] = t_mm(x, coef)
    for i, at in enumerate((y, 1 - y)):
        cols = pl.ds(pl.multiple_of(at * HALF, HALF), HALF)
        out = acc_o[:, cols]
        if routed:
            out = out * gate
        out_o[i] = out.astype(bf16)
        db_o[i] = acc_b[:, cols].astype(bf16)


def ffn(scalars, s, groups, xa, xb, wa, wb, gu, dt, rt, prev):
    routed = rt is not None
    hidden = dt.shape[1]
    full = lambda shape: pl.BlockSpec(shape, lambda i, n=len(shape): (0,) * n)
    part = lambda width: pl.BlockSpec((1, ROWS, width), lambda i: (s, 0, 0))
    two = (2, ROWS, HALF)
    outs = [sds(two, bf16), sds(two, bf16)]
    out_specs = [full(two), full(two)]
    if routed:
        outs.append(sds((D, 128), f32))
        out_specs.append(full((D, 128)))
    widths = [2 * hidden, hidden] + ([D, D] if routed else [])
    base = len(outs)
    for width in widths:
        outs.append(sds((groups, ROWS, width), bf16))
        out_specs.append(part(width))
    args = [xa, xb, wa, wb, gu, dt] + ([rt] if routed else [])
    in_specs = [SMEM] + [full(a.shape) for a in args]
    aliases = {}
    if not routed:
        args.append(dt[:16, :128])
        in_specs.append(full((16, 128)))
    if prev is not None:
        for i, arr in enumerate(prev):
            aliases[1 + len(args)] = base + i
            args.append(arr)
            in_specs.append(pl.BlockSpec(memory_space=pl.ANY))
    return pl.pallas_call(
        functools.partial(ffn_body, routed),
        grid=(1,),
        out_shape=outs,
        in_specs=in_specs,
        out_specs=out_specs,
        scratch_shapes=[pltpu.VMEM((ROWS, D), f32), pltpu.VMEM((ROWS, D), f32)],
        input_output_aliases=aliases,
        compiler_params=pltpu.CompilerParams(vmem_limit_bytes=VMEM_LIMIT),
        cost_estimate=pl.CostEstimate(
            flops=2 * ROWS * D * hidden * 6, bytes_accessed=16 << 20, transcendentals=0
        ),
        name="expert_ffn" if routed else "shared_ffn",
    )(scalars, *args)


def dense_assemble(scalars, offs, st, xs, co, widths):
    rows = st.shape[1]

    def body(sc, st, xs, co, *outs):
        for rc in range(4):
            for s in range(4):
                piece = (st, co.at[0], xs, co.at[1])[rc]
                at = pl.ds(pl.multiple_of(sc[rc * 4 + s], 16), rows)
                lo = 0
                for out, width in zip(outs, widths):
                    out[at, :] = piece[s, :, lo : lo + width]
                    lo += width

    outs = [sds((16 * rows, width), bf16) for width in widths]
    return call(body, outs, moved=4 * 16 * rows * sum(widths), name="dense_assemble")(offs, st, xs, co)


def dense_split(offs, full, rows):
    def body(sc, full, out):
        for k in range(16):
            at = pl.ds(pl.multiple_of(sc[k], 16), rows)
            out[k] = full[at, :]

    n = full.shape[1]
    return call(body, sds((16, rows, n), bf16), moved=64 * rows * n, name="dense_split")(offs, full)


def expert_assemble(offs, gus, dts):
    rows = dts[0].shape[0]
    hidden = dts[0].shape[1]

    def body(sc, g0, g1, g2, g3, d0, d1, d2, d3, gu_o, dt_o):
        for s, (g, d) in enumerate(((g0, d0), (g1, d1), (g2, d2), (g3, d3))):
            at = pl.ds(pl.multiple_of(sc[s], 16), rows)
            gu_o[at, :hidden] = g[0]
            gu_o[at, hidden:] = g[1]
            dt_o[at, :] = d[...]

    outs = [sds((4 * rows, 2 * hidden), bf16), sds((4 * rows, hidden), bf16)]
    return call(body, outs, moved=4 * 4 * rows * 3 * hidden, name="expert_assemble")(offs, *gus, *dts)


def grads_place(order, gus, dts):
    rows, hidden = dts[0].shape

    def body(sc, g0, g1, g2, g3, d0, d1, d2, d3, gu_o, dt_o):
        for s, (g, d) in enumerate(((g0, d0), (g1, d1), (g2, d2), (g3, d3))):
            gu_o[sc[s], 0] = g[:, :hidden].astype(f32)
            gu_o[sc[s], 1] = g[:, hidden:].astype(f32)
            dt_o[sc[s]] = d[...].astype(f32).T

    outs = [sds((4, 2, rows, hidden), f32), sds((4, hidden, rows), f32)]
    return call(body, outs, moved=6 * 4 * rows * 3 * hidden, name="grads_place")(order, *gus, *dts)


def per_device(
    tokens,
    segments,
    experts,
    attn_gain,
    qkv_proj,
    out_proj,
    ffn_gain,
    router_proj,
    expert_gate_up,
    expert_down,
    shared_gate_up,
    shared_down,
    cotangent,
):
    F, C = lax.axis_size("fsdp"), lax.axis_size("ctx")
    f, c, y = lax.axis_index("fsdp"), lax.axis_index("ctx"), lax.axis_index("tp")
    EL = expert_gate_up.shape[0]
    small = F == EL and C == 4
    heads_width = qkv_proj.shape[2]
    hidden = expert_down.shape[1]
    shared_hidden = shared_down.shape[0]
    zi = f % EL
    i32 = jnp.int32

    def yx(v):
        return lax.ppermute(v, "tp", [(0, 1), (1, 0)])

    def cx(v, flip):
        return lax.ppermute(v, "ctx", [(i, i ^ flip) for i in range(C)])

    def zs(v, s):
        return lax.ppermute(
            v, "fsdp", [(i, i // EL * EL + (i % EL + s) % EL) for i in range(F)]
        )

    scalars = jnp.stack([c, y, EL * c + zi]).astype(i32)
    rows_own = D // (F * C)
    rc = jnp.arange(4, dtype=i32)
    if small:
        dense_offs = (
            (((f - rc)[None, :] % 4) * 4 + (c ^ rc)[:, None]).reshape(16) * rows_own
        ).astype(i32)
        back_offs = (
            (((f + rc)[None, :] % 4) * 4 + (c ^ rc)[:, None]).reshape(16) * rows_own
        ).astype(i32)

    def dense_gather(shard, widths):
        if small:
            st = jnp.stack([shard] + [zs(shard, s) for s in (1, 2, 3)])
            xs = cx(st, 2)
            co = cx(jnp.stack([st, xs]), 1)
            return dense_assemble(scalars, dense_offs, st, xs, co, widths)
        full = lax.all_gather(shard, ("fsdp", "ctx"), axis=0, tiled=True)
        cuts, lo = [], 0
        for width in widths:
            cuts.append(full[:, lo : lo + width])
            lo += width
        return cuts

    def reduce_blocks(blocks):
        kind = blocks.dtype
        part = blocks[0::2].astype(f32) + cx(blocks[1::2], 1).astype(f32)
        part = part[0] + cx(part[1].astype(kind), 2).astype(f32)
        total = part[0]
        for s in (1, 2, 3):
            total = total + zs(part[s].astype(kind), s).astype(f32)
        return total

    def dense_reduce(full):
        n = full.shape[1]
        if small:
            blocks = dense_split(back_offs, full.astype(bf16), rows_own)
            return reduce_blocks(blocks.reshape(4, 4, rows_own, n))
        return lax.psum_scatter(
            full.astype(f32), ("fsdp", "ctx"), scatter_dimension=0, tiled=True
        )

    def half(v, which):
        return lax.dynamic_slice_in_dim(v, which * HALF, HALF, v.ndim - 1)

    qkv_shard = jnp.concatenate(
        [
            qkv_proj.transpose(1, 0, 2).reshape(rows_own, 3 * heads_width),
            router_proj,
            attn_gain[:, None],
            ffn_gain[:, None],
            jnp.zeros((rows_own, 128 - E - 2), bf16),
        ],
        axis=1,
    )
    qkv_w, extra = dense_gather(qkv_shard, (3 * heads_width, 128))
    rest_shard = jnp.concatenate(
        [
            out_proj.T,
            shared_gate_up.transpose(1, 0, 2).reshape(rows_own, 2 * shared_hidden),
            shared_down.T,
        ],
        axis=1,
    )
    out_w, shared_gu, shared_dt = dense_gather(
        rest_shard, (heads_width, 2 * shared_hidden, shared_hidden)
    )
    gains = extra[:, E : E + 2].astype(f32)
    gain_one, gain_two = gains[:, 0], gains[:, 1]
    gain_two_h = half(gain_two, y)
    gain_one_h = half(gain_one, y)

    if small:
        gus, dts = [], []
        for s in range(4):
            j = (zi + s) % EL
            gu = lax.dynamic_index_in_dim(expert_gate_up, j, 0, keepdims=False)
            dt = lax.dynamic_index_in_dim(expert_down, j, 0, keepdims=False).T
            gus.append(gu if s == 0 else zs(gu, s))
            dts.append(dt if s == 0 else zs(dt, s))
        expert_offs = (((zi - rc) % 4) * (D // 4)).astype(i32)
        expert_gu, expert_dt = expert_assemble(expert_offs, gus, dts)
    else:
        inner = [[g * EL + i for i in range(EL)] for g in range(F // EL)]
        outer = [[g * EL + i for g in range(F // EL)] for i in range(EL)]
        mine = lax.all_to_all(
            jnp.concatenate(
                [expert_gate_up[:, 0], expert_gate_up[:, 1], expert_down.transpose(0, 2, 1)], axis=2
            ),
            "fsdp", 0, 0, axis_index_groups=inner, tiled=True,
        )
        mine = lax.all_gather(mine, "fsdp", axis=0, axis_index_groups=outer, tiled=True)
        mine = mine.reshape(D, 3 * hidden)
        expert_gu, expert_dt = mine[:, : 2 * hidden], mine[:, 2 * hidden :]

    lanes = jnp.arange(E, dtype=i32)[None, :]
    named = [(experts[:, k : k + 1] == lanes) for k in range(2)]
    both = (named[0] | named[1]).astype(bf16)
    before = (jnp.arange(ROWS)[:, None] > jnp.arange(ROWS)[None, :]).astype(bf16)
    counts = jnp.dot(before, both, preferred_element_type=f32)
    code = jnp.stack(
        [
            experts[:, k] * CAP + jnp.sum(jnp.where(named[k], counts, 0.0), axis=1).astype(i32)
            for k in range(2)
        ]
    )
    code_two = jnp.stack([code, cx(code, 2)])
    code_core = cx(code_two, 1)
    codes = jnp.concatenate([code_two[0], code_core[0], code_two[1], code_core[1]], axis=0)
    which, rank = codes // CAP, codes % CAP
    ids = jnp.where(which // EL == c, ((which - zi) % EL) * CAP + rank, -1).astype(i32)

    def dispatch(own):
        far = cx(own, 2)
        near = cx(own, 1)
        both_far = cx(far, 1)
        packs = call(
            pack_body, [sds((4 * CAP, HALF), bf16)] * 4, flops=8 * ROWS * ROWS * HALF,
            moved=6 << 20, name="pack",
        )(scalars, ids, own, near, far, both_far)
        mine = [packs[0]] + [zs(packs[s], s) for s in (1, 2, 3)]
        return [(m, yx(m)) for m in mine]

    def give_back(parts):
        rows = []
        for s, two in enumerate(parts):
            total = (two[0].astype(f32) + yx(two[1]).astype(f32)).astype(bf16)
            rows.append(total if s == 0 else zs(total, EL - s))
        rows = [rows[0], rows[1], rows[2], rows[3]]
        keep, send = call(
            unpack_body, [sds((2, ROWS, HALF), bf16)] * 2, flops=8 * ROWS * ROWS * HALF,
            moved=6 << 20, name="unpack",
        )(scalars, ids, *rows)
        got = cx(send, 1)
        far = (keep[1].astype(f32) + got[1].astype(f32)).astype(bf16)
        return keep[0].astype(f32) + got[0].astype(f32) + cx(far, 2).astype(f32)

    cot_h, cot_o = half(cotangent, y), half(cotangent, 1 - y)
    cot_chunks = dispatch(cot_h)

    positions = (c * ROWS + jnp.arange(ROWS, dtype=i32)).astype(f32)
    table = jnp.arange(128, dtype=i32)
    frequency = 10000.0 ** (-(table % 32).astype(f32) / 32)
    angles = positions[:, None] * frequency[None, :]
    cos = jnp.cos(angles)
    sin = jnp.sin(angles) * jnp.where(table % 64 < 32, -1.0, 1.0)[None, :]
    normed_one, queries, kv = call(
        qkv_body,
        [sds((ROWS, D), bf16), sds((ROWS, heads_width), bf16), sds((ROWS, 2 * heads_width), bf16)],
        flops=2 * ROWS * D * 3 * heads_width, moved=6 << 20, name="qkv",
    )(scalars, tokens, gain_one[None, :], qkv_w, cos, sin)
    kv_far = cx(kv, 2)
    kv_near = cx(kv, 1)
    kv_both = cx(kv_far, 1)
    kvs = (kv, kv_near, kv_far, kv_both)
    seq_ids = segments[0]
    seg_col = seq_ids[:, None]
    seg_row = lax.dynamic_slice_in_dim(seq_ids, c * ROWS, ROWS, 0)[None, :]
    attended, z_own, z_oth, lse = call(
        attn_body,
        [
            sds((ROWS, heads_width), bf16),
            sds((ROWS, HALF), f32),
            sds((ROWS, HALF), bf16),
            sds((8, ROWS), f32),
        ],
        scratch=[
            pltpu.VMEM((4 * ROWS, 2 * heads_width), bf16),
            pltpu.VMEM((4 * ROWS, ROWS), f32),
            pltpu.VMEM((4 * ROWS, ROWS), f32),
            pltpu.VMEM((heads_width, ROWS), f32),
        ],
        flops=16 * ROWS * ROWS * heads_width * 4, moved=8 << 20, name="attn",
    )(scalars, queries, *kvs, seg_col, seg_row, out_w)
    tok_h = half(tokens, y).astype(f32)
    middle = tok_h + z_own + yx(z_oth).astype(f32)

    def both_halves(sums):
        return sums + yx(sums)

    square = both_halves(jnp.sum(middle * middle, axis=1))
    scale_two = lax.rsqrt(square / D + eps)[:, None]
    normal_two = middle * scale_two
    normed_two = (normal_two * gain_two_h[None, :]).astype(bf16)

    chunks = dispatch(normed_two)
    normed_two_oth = yx(normed_two)
    sh_out, sh_db, sh_dgu, sh_y = ffn(
        scalars, 0, 1, normed_two, normed_two_oth, cot_h, cot_o, shared_gu, shared_dt, None, None
    )
    saved, outs, backs, router_part = None, [], [], 0.0
    for s in range(4):
        res = ffn(
            scalars, s, 4, *chunks[s], *cot_chunks[s], expert_gu, expert_dt, extra, saved
        )
        outs.append(res[0])
        backs.append(res[1])
        router_part = router_part + res[2][:, :E]
        saved = res[3:]
    ex_dgu, ex_y, ex_x, ex_de = [v.reshape(4 * ROWS, -1) for v in saved]
    sh_db_recv = yx(sh_db[1])
    sh_out_recv = yx(sh_out[1])
    back_h = give_back(backs) + sh_db[0].astype(f32) + sh_db_recv.astype(f32)

    scaled = back_h * gain_two_h[None, :]
    mean_two = both_halves(jnp.sum(scaled * normal_two, axis=1))[:, None] / D
    ffn_gain_part = jnp.sum(back_h * normal_two, axis=0)
    middle_grad = cot_h.astype(f32) + scale_two * (scaled - normal_two * mean_two)
    dz_own = middle_grad.astype(bf16)
    dz_oth = yx(dz_own)
    dq, dkv = call(
        attn_back_body,
        [sds((ROWS, heads_width), bf16), sds((4, ROWS, 2 * heads_width), bf16)],
        scratch=[
            pltpu.VMEM((4 * ROWS, 2 * heads_width), bf16),
            pltpu.VMEM((4 * ROWS, ROWS), f32),
            pltpu.VMEM((ROWS, heads_width), bf16),
            pltpu.VMEM((8, ROWS), f32),
            pltpu.VMEM((heads_width, ROWS), f32),
        ],
        flops=40 * ROWS * ROWS * heads_width * 4, moved=10 << 20, name="attn_back",
    )(
        scalars, queries, *kvs, seg_col, seg_row, lse, attended, dz_own, dz_oth, out_w, cos, sin
    )
    kv_part = dkv[0::2].astype(f32) + cx(dkv[1::2], 1).astype(f32)
    kv_recv = cx(kv_part[1].astype(bf16), 2)
    dp, da_own, da_oth = call(
        proj_back_body,
        [sds((ROWS, 3 * heads_width), bf16), sds((ROWS, HALF), f32), sds((ROWS, HALF), bf16)],
        flops=2 * ROWS * D * 3 * heads_width, moved=8 << 20, name="proj_back",
    )(scalars, dq, kv_part[0], kv_recv, qkv_w, cos, sin)
    da_h = da_own + yx(da_oth).astype(f32)
    tok_full = tokens.astype(f32)
    scale_one = lax.rsqrt(jnp.mean(tok_full * tok_full, axis=1, keepdims=True) + eps)
    normal_one = tok_h * scale_one
    scaled_one = da_h * gain_one_h[None, :]
    mean_one = both_halves(jnp.sum(scaled_one * normal_one, axis=1))[:, None] / D
    attn_gain_part = jnp.sum(da_h * normal_one, axis=0)
    tokens_grad_h = middle_grad + scale_one * (scaled_one - normal_one * mean_one)

    def whole_rows(own):
        return halves(y, own, yx(own))

    tokens_grad = whole_rows(tokens_grad_h.astype(bf16)).astype(f32)

    grad_gu = lax.dot_general(
        ex_x, ex_dgu, (((0,), (0,)), ((), ())), preferred_element_type=f32
    )
    grad_dt = lax.dot_general(ex_de, ex_y, (((0,), (0,)), ((), ())), preferred_element_type=f32)
    if small:
        grad_gu, grad_dt = grad_gu.astype(bf16), grad_dt.astype(bf16)
        ggs, gds = [], []
        for s in range(4):
            at = ((zi + s) % 4) * (D // 4)
            gg = lax.dynamic_slice_in_dim(grad_gu, at, D // 4, 0)
            gd = lax.dynamic_slice_in_dim(grad_dt, at, D // 4, 0)
            ggs.append(gg if s == 0 else zs(gg, s))
            gds.append(gd if s == 0 else zs(gd, s))
        expert_gate_up_grad, expert_down_grad = grads_place(
            ((zi - rc) % 4).astype(i32), ggs, gds
        )
    else:
        both_grads = jnp.concatenate([grad_gu, grad_dt], axis=1)
        both_grads = both_grads.reshape(F // EL * EL, D // F, 3 * hidden)
        both_grads = lax.psum_scatter(
            both_grads, "fsdp", scatter_dimension=0, axis_index_groups=outer, tiled=True
        )
        both_grads = lax.all_to_all(
            both_grads, "fsdp", 0, 0, axis_index_groups=inner, tiled=True
        )
        expert_gate_up_grad = jnp.stack(
            [both_grads[:, :, :hidden], both_grads[:, :, hidden : 2 * hidden]], axis=1
        )
        expert_down_grad = both_grads[:, :, 2 * hidden :].transpose(0, 2, 1)

    layer_h = middle + give_back(outs) + sh_out[0].astype(f32) + sh_out_recv.astype(f32)
    layer_out = whole_rows(layer_h.astype(bf16))

    dz_full = halves(y, dz_own, dz_oth)
    normed_full = halves(y, normed_two, normed_two_oth)

    def grad_of(a, b):
        return lax.dot_general(a, b, (((0,), (0,)), ((), ())), preferred_element_type=f32).astype(
            bf16
        )

    rest_grad = jnp.concatenate(
        [grad_of(dz_full, attended), grad_of(normed_full, sh_dgu[0]), grad_of(cotangent, sh_y[0])],
        axis=1,
    )
    rest_grad = dense_reduce(rest_grad)
    qkv_grad = dense_reduce(grad_of(normed_one, dp))
    qkv_grad = qkv_grad.reshape(rows_own, 3, heads_width).transpose(1, 0, 2)
    out_grad = rest_grad[:, :heads_width].T
    shared_gate_up_grad = jnp.stack(
        [
            rest_grad[:, heads_width : heads_width + shared_hidden],
            rest_grad[:, heads_width + shared_hidden : heads_width + 2 * shared_hidden],
        ]
    )
    shared_down_grad = rest_grad[:, heads_width + 2 * shared_hidden :].T

    def placed(part):
        first = y == 0
        return jnp.concatenate([jnp.where(first, part, 0.0), jnp.where(first, 0.0, part)])

    tail = jnp.concatenate(
        [router_part, placed(attn_gain_part)[:, None], placed(ffn_gain_part)[:, None]], axis=1
    )
    if small:
        order = back_offs // rows_own
        blocks = tail.reshape(16, rows_own * (E + 2))[order]
        tail = reduce_blocks(blocks.reshape(4, 4, rows_own * (E + 2)))
        tail = tail.reshape(rows_own, E + 2)
    else:
        tail = lax.psum_scatter(tail, ("fsdp", "ctx"), scatter_dimension=0, tiled=True)
    tail = tail + yx(tail)
    return (
        layer_out,
        tokens_grad,
        tail[:, E],
        qkv_grad,
        out_grad,
        tail[:, E + 1],
        tail[:, :E],
        expert_gate_up_grad,
        expert_down_grad,
        shared_gate_up_grad,
        shared_down_grad,
    )


def solution(mesh):
    return jax.shard_map(
        per_device,
        mesh=mesh,
        in_specs=(
            P(("fsdp", "ctx"), None),
            P("fsdp", None),
            P(("fsdp", "ctx"), None),
            P(("fsdp", "ctx")),
            P(None, ("fsdp", "ctx"), "tp"),
            P("tp", ("fsdp", "ctx")),
            P(("fsdp", "ctx")),
            P(("fsdp", "ctx"), None),
            P("ctx", None, "fsdp", "tp"),
            P("ctx", "tp", "fsdp"),
            P(None, ("fsdp", "ctx"), "tp"),
            P("tp", ("fsdp", "ctx")),
            P(("fsdp", "ctx"), None),
        ),
        out_specs=(
            P(("fsdp", "ctx"), None),
            P(("fsdp", "ctx"), None),
            P(("fsdp", "ctx")),
            P(None, ("fsdp", "ctx"), "tp"),
            P("tp", ("fsdp", "ctx")),
            P(("fsdp", "ctx")),
            P(("fsdp", "ctx"), None),
            P("ctx", None, "fsdp", "tp"),
            P("ctx", "tp", "fsdp"),
            P(None, ("fsdp", "ctx"), "tp"),
            P("tp", ("fsdp", "ctx")),
        ),
        check_vma=False,
    )
```

```python
import functools

import jax
import jax.numpy as jnp
from jax import lax
from jax.experimental import pallas as pl
from jax.experimental.pallas import tpu as pltpu
from jax.sharding import PartitionSpec as P

D = 768
HALF = D // 2
HD = 64
E = 16
ROWS = 512
CAP = 128
NEG = -1e30
eps = 1e-06
bf16 = jnp.bfloat16
f32 = jnp.float32
VMEM_LIMIT = 56 * 1024 * 1024


def mm(a, b):
    return lax.dot_general(a, b, (((1,), (0,)), ((), ())), preferred_element_type=f32)


def mm_t(a, b):
    return lax.dot_general(a, b, (((1,), (1,)), ((), ())), preferred_element_type=f32)


def t_mm(a, b):
    return lax.dot_general(a, b, (((0,), (0,)), ((), ())), preferred_element_type=f32)


def sds(shape, dtype):
    return jax.ShapeDtypeStruct(shape, dtype)


SMEM = pl.BlockSpec(memory_space=pltpu.SMEM)
VM = pl.BlockSpec(memory_space=pltpu.VMEM)


def call(body, outs, scratch=(), us=1.0, name=None):
    def run(scalars, *args, deps=()):
        count = 1 + len(args)

        def inner(*refs):
            body(*refs[:count], *refs[count + len(deps) :])

        return pl.pallas_call(
            inner,
            out_shape=outs,
            in_specs=[SMEM] + [VM] * len(args) + [pl.BlockSpec(memory_space=pl.ANY)] * len(deps),
            out_specs=jax.tree.map(lambda _: VM, outs),
            scratch_shapes=list(scratch),
            compiler_params=pltpu.CompilerParams(vmem_limit_bytes=VMEM_LIMIT),
            cost_estimate=pl.CostEstimate(
                flops=int(us * 1e9), bytes_accessed=0, transcendentals=0
            ),
            name=name,
        )(scalars, *args, *deps)

    return run


def after(v, *deps):
    return lax.optimization_barrier((v,) + deps)[0]


def partner(v, lane):
    return jnp.where(lane % 64 < 32, pltpu.roll(v, 96, 1), pltpu.roll(v, 32, 1))


def lane_id(rows):
    return lax.broadcasted_iota(jnp.int32, (rows, 128), 1)


def qkv_body(sc, tok, gain, w, cos, sin, a_o, q_o, kv_o):
    x = tok[...].astype(f32)
    scale = lax.rsqrt(jnp.mean(x * x, axis=1, keepdims=True) + eps)
    a = (x * scale * gain[...]).astype(bf16)
    a_o[...] = a
    n = q_o.shape[1]
    lane = lane_id(ROWS)
    for g in range(3 * n // 128):
        v = mm(a, w[:, g * 128 : (g + 1) * 128])
        lo = g * 128
        if lo < n:
            r = v * cos[...] + partner(v, lane) * sin[...]
            q_o[:, lo : lo + 128] = (r.astype(bf16).astype(f32) * (HD**-0.5)).astype(bf16)
        elif lo < 2 * n:
            r = v * cos[...] + partner(v, lane) * sin[...]
            kv_o[:, lo - n : lo - n + 128] = r.astype(bf16)
        else:
            kv_o[:, lo - n : lo - n + 128] = v.astype(bf16)


def block_bias(c, kb, segc, segq):
    off = pl.multiple_of(kb * ROWS, ROWS)
    kpos = off + lax.broadcasted_iota(jnp.int32, (ROWS, ROWS), 0)
    qpos = c * ROWS + lax.broadcasted_iota(jnp.int32, (ROWS, ROWS), 1)
    ok = (segc[pl.ds(off, ROWS), :] == segq[...]) & (kpos <= qpos)
    return jnp.where(ok, 0.0, NEG)


def attn_body(sc, q, k0, k1, k2, k3, segc, segq, wo, o_o, zown_o, zoth_o, lse_o, kvs, bias, st, ot):
    c, y = sc[0], sc[1]
    nb = c + 1
    n = q.shape[1]
    for r, ref in enumerate((k0, k1, k2, k3)):
        kvs[pl.ds(pl.multiple_of((c ^ r) * ROWS, ROWS), ROWS), :] = ref[...]

    def bias_step(kb, carry):
        bias[pl.ds(pl.multiple_of(kb * ROWS, ROWS), ROWS), :] = block_bias(c, kb, segc, segq)
        return carry

    lax.fori_loop(0, nb, bias_step, 0)
    for h in range(n // HD):
        lo = h * HD
        qh = q[:, lo : lo + HD]

        def score_step(kb, m, lo=lo, qh=qh):
            rows = pl.ds(pl.multiple_of(kb * ROWS, ROWS), ROWS)
            s = mm_t(kvs[rows, lo : lo + HD], qh) + bias[rows, :]
            st[rows, :] = s
            return jnp.maximum(m, jnp.max(s, axis=0, keepdims=True))

        m = lax.fori_loop(0, nb, score_step, jnp.full((1, ROWS), NEG, f32))

        def value_step(kb, carry, lo=lo, m=m):
            total, acc = carry
            rows = pl.ds(pl.multiple_of(kb * ROWS, ROWS), ROWS)
            p = jnp.exp(st[rows, :] - m)
            total = total + jnp.sum(p, axis=0, keepdims=True)
            return total, acc + t_mm(kvs[rows, n + lo : n + lo + HD], p.astype(bf16))

        total, acc = lax.fori_loop(
            0, nb, value_step, (jnp.zeros((1, ROWS), f32), jnp.zeros((HD, ROWS), f32))
        )
        ot[lo : lo + HD, :] = acc / total
        lse_o[h : h + 1, :] = m + jnp.log(total)
    o = ot[...].T.astype(bf16)
    o_o[...] = o
    own = pl.ds(pl.multiple_of(y * HALF, HALF), HALF)
    oth = pl.ds(pl.multiple_of((1 - y) * HALF, HALF), HALF)
    zoth_o[...] = mm_t(o, wo[oth, :]).astype(bf16)
    zown_o[...] = mm_t(o, wo[own, :])


def attn_back_body(
    sc, q, k0, k1, k2, k3, segc, segq, lse, o, zown, zoth, wo, cos, sin, dq_o, keep_o, send_o,
    kvs, bias, do_s, delta, dqt,
):
    c, y = sc[0], sc[1]
    nb = c + 1
    n = q.shape[1]
    heads = n // HD
    for r, ref in enumerate((k0, k1, k2, k3)):
        kvs[pl.ds(pl.multiple_of((c ^ r) * ROWS, ROWS), ROWS), :] = ref[...]

    def bias_step(kb, carry):
        bias[pl.ds(pl.multiple_of(kb * ROWS, ROWS), ROWS), :] = block_bias(c, kb, segc, segq)
        return carry

    lax.fori_loop(0, nb, bias_step, 0)
    own = pl.ds(pl.multiple_of(y * HALF, HALF), HALF)
    oth = pl.ds(pl.multiple_of((1 - y) * HALF, HALF), HALF)
    do = (mm(zown[...], wo[own, :]) + mm(zoth[...], wo[oth, :])).astype(bf16)
    do_s[...] = do
    pick = (
        lax.broadcasted_iota(jnp.int32, (8, n), 1) // HD
        == lax.broadcasted_iota(jnp.int32, (8, n), 0)
    ).astype(f32)
    delta[...] = lax.dot_general(
        pick,
        do.astype(f32) * o[...].astype(f32),
        (((1,), (1,)), ((), ())),
        precision=lax.Precision.HIGHEST,
        preferred_element_type=f32,
    )

    def put(kb, cols, value):
        at = kb ^ c

        @pl.when(at % 2 == 0)
        def _():
            keep_o[at // 2, :, cols] = value

        @pl.when(at % 2 == 1)
        def _():
            send_o[at // 2, :, cols] = value

    def zero_step(kb, carry):
        put(kb, slice(None), jnp.zeros((ROWS, 2 * n), bf16))
        return carry

    lax.fori_loop(nb, 4, zero_step, 0)
    for pair in range(heads // 2):
        at = pair * 128

        def step(kb, carry, at=at, pair=pair):
            rows = pl.ds(pl.multiple_of(kb * ROWS, ROWS), ROWS)
            dks, dvs, dqs = [], [], []
            for i in range(2):
                lo = at + i * HD
                h = 2 * pair + i
                kh = kvs[rows, lo : lo + HD]
                vh = kvs[rows, n + lo : n + lo + HD]
                qh = q[:, lo : lo + HD]
                dh = do_s[:, lo : lo + HD]
                p = jnp.exp(mm_t(kh, qh) + bias[rows, :] - lse[h : h + 1, :])
                ds = (p * (mm_t(vh, dh) - delta[h : h + 1, :])).astype(bf16)
                dvs.append(mm(p.astype(bf16), dh))
                dks.append(mm(ds, qh))
                dqs.append(carry[i] + t_mm(kh, ds))
            put(kb, slice(at, at + 128), jnp.concatenate(dks, axis=1).astype(bf16))
            put(kb, slice(n + at, n + at + 128), jnp.concatenate(dvs, axis=1).astype(bf16))
            return tuple(dqs)

        zero = jnp.zeros((HD, ROWS), f32)
        dqs = lax.fori_loop(0, nb, step, (zero, zero))
        dqt[at : at + HD, :] = dqs[0]
        dqt[at + HD : at + 128, :] = dqs[1]
    lane = lane_id(ROWS)
    for g in range(n // 128):
        v = dqt[g * 128 : (g + 1) * 128, :].T * (HD**-0.5)
        dq_o[:, g * 128 : (g + 1) * 128] = (v * cos[...] - partner(v, lane) * sin[...]).astype(bf16)


def proj_back_body(sc, dq, keep, near, recv, w, cos, sin, dp_o, own_o, oth_o):
    y = sc[1]
    n = dq.shape[1]
    lane = lane_id(ROWS)
    dp_o[:, :n] = dq[...]
    for g in range(2 * n // 128):
        cols = slice(g * 128, (g + 1) * 128)
        v = keep[0, :, cols].astype(f32) + near[0, :, cols].astype(f32) + recv[:, cols].astype(f32)
        if g < n // 128:
            v = v * cos[...] - partner(v, lane) * sin[...]
        dp_o[:, n + g * 128 : n + (g + 1) * 128] = v.astype(bf16)
    own = pl.ds(pl.multiple_of(y * HALF, HALF), HALF)
    oth = pl.ds(pl.multiple_of((1 - y) * HALF, HALF), HALF)
    oth_o[...] = mm_t(dp_o[...], w[oth, : 3 * n]).astype(bf16)
    own_o[...] = mm_t(dp_o[...], w[own, : 3 * n])


def slots_onehot(ids, r):
    i = lax.broadcasted_iota(jnp.int32, (4 * CAP, ROWS), 0)
    hit = (i == ids[2 * r : 2 * r + 1, :]) | (i == ids[2 * r + 1 : 2 * r + 2, :])
    return jnp.where(hit, 1.0, 0.0).astype(bf16)


def pack_body(sc, ids, b0, b1, b2, b3, p0, p1, p2, p3):
    for r, ref in enumerate((b0, b1, b2, b3)):
        rows = mm(slots_onehot(ids, r), ref[...]).astype(bf16)
        for s, out in enumerate((p0, p1, p2, p3)):
            out[r * CAP : (r + 1) * CAP, :] = rows[s * CAP : (s + 1) * CAP, :]


def unpack_body(sc, ids, p0, p1, p2, p3, keep_b, send_b, keep_o, send_o):
    for r in (1, 3, 0, 2):
        rows = jnp.concatenate(
            [p[r * CAP : (r + 1) * CAP, :] for p in (p0, p1, p2, p3)], axis=0
        )
        tok = t_mm(slots_onehot(ids, r), rows).astype(bf16)
        for at, pair in ((0, (keep_b, send_b)), (HALF, (keep_o, send_o))):
            pair[r % 2][r // 2] = tok[:, at : at + HALF]


def halves(y, a, b):
    first = y == 0
    return jnp.concatenate([jnp.where(first, a, b), jnp.where(first, b, a)], axis=1)


def ffn_body(routed, sc, xa, xb, wa, wb, weights, rt, *refs):
    if routed:
        refs = refs[len(refs) - 8 :]
        back_o, rg_o, dgu_o, y_o, x_o, de_o, acc_o, acc_b = refs
    else:
        back_o, dgu_o, y_o, acc_o, acc_b = refs[len(refs) - 5 :]
    y, e = sc[1], sc[2]
    x = halves(y, xa[...], xb[...])
    w = halves(y, wa[...], wb[...])
    hidden = weights.shape[3]
    if routed:
        lane = lane_id(ROWS)
        logits = jnp.where(lane < E, mm(x, rt[...]), NEG)
        ex = jnp.exp(logits - jnp.max(logits, axis=1, keepdims=True))
        probs = ex / jnp.sum(ex, axis=1, keepdims=True)
        gate = jnp.sum(jnp.where(lane == e, probs, 0.0), axis=1, keepdims=True)
        x_o[0] = x
        de_o[0] = (w.astype(f32) * gate).astype(bf16)
    acc_o[...] = jnp.zeros_like(acc_o)
    acc_b[...] = jnp.zeros_like(acc_b)
    tile = 256

    def columns(which, lo):
        cols = pl.ds(pl.multiple_of(lo, tile), tile)
        return jnp.concatenate(
            [weights[j, which, :, cols] for j in range(weights.shape[0])], axis=0
        )

    def step(j, dots):
        lo = pl.multiple_of(j * tile, tile)
        hi = pl.multiple_of(hidden + j * tile, tile)
        g = mm(x, columns(0, lo))
        u = mm(x, columns(1, lo))
        h = mm(w, columns(2, lo))
        sg = 1.0 / (1.0 + jnp.exp(-g))
        act = g * sg
        yv = (act * u).astype(bf16)
        if routed:
            dots = dots + jnp.sum(yv.astype(f32) * h, axis=1, keepdims=True)
            h = h * gate
        dg = (h * u * (sg + act * (1.0 - sg))).astype(bf16)
        du = (h * act).astype(bf16)
        y_o[0, :, pl.ds(lo, tile)] = yv
        dgu_o[0, :, pl.ds(lo, tile)] = dg
        dgu_o[0, :, pl.ds(hi, tile)] = du
        acc_o[...] += mm_t(yv, columns(2, lo))
        acc_b[...] += mm_t(dg, columns(0, lo)) + mm_t(du, columns(1, lo))
        return dots

    dots = lax.fori_loop(0, hidden // tile, step, jnp.zeros((ROWS, 1), f32))
    if routed:
        coef = (dots * gate) * (jnp.where(lane == e, 1.0, 0.0) - probs)
        coef = jnp.where(lane < E, coef, 0.0).astype(bf16)
        acc_b[...] += mm_t(coef, rt[...])
        rg_o[...] = t_mm(x, coef)
    for i, at in enumerate((y, 1 - y)):
        cols = pl.ds(pl.multiple_of(at * HALF, HALF), HALF)
        out = acc_o[:, cols]
        if routed:
            out = out * gate
        back_o[i, :, :HALF] = acc_b[:, cols].astype(bf16)
        back_o[i, :, HALF:] = out.astype(bf16)


def ffn(scalars, s, groups, xa, xb, wa, wb, weights, rt, prev, deps=()):
    routed = rt is not None
    hidden = weights.shape[3]
    full = lambda shape: pl.BlockSpec(shape, lambda i, n=len(shape): (0,) * n)
    part = lambda width: pl.BlockSpec((1, ROWS, width), lambda i: (s, 0, 0))
    two = (2, ROWS, D)
    outs = [sds(two, bf16)]
    out_specs = [full(two)]
    if routed:
        outs.append(sds((D, 128), f32))
        out_specs.append(full((D, 128)))
    widths = [2 * hidden, hidden] + ([D, D] if routed else [])
    base = len(outs)
    for width in widths:
        outs.append(sds((groups, ROWS, width), bf16))
        out_specs.append(part(width))
    args = [xa, xb, wa, wb, weights] + ([rt] if routed else [])
    in_specs = [SMEM] + [full(a.shape) for a in args]
    aliases = {}
    if not routed:
        args.append(scalars)
        in_specs.append(SMEM)
    for arr in deps:
        args.append(arr)
        in_specs.append(pl.BlockSpec(memory_space=pl.ANY))
    if prev is not None:
        for i, arr in enumerate(prev):
            aliases[1 + len(args)] = base + i
            args.append(arr)
            in_specs.append(pl.BlockSpec(memory_space=pl.ANY))
    return pl.pallas_call(
        functools.partial(ffn_body, routed),
        grid=(1,),
        out_shape=outs,
        in_specs=in_specs,
        out_specs=out_specs,
        scratch_shapes=[pltpu.VMEM((ROWS, D), f32), pltpu.VMEM((ROWS, D), f32)],
        input_output_aliases=aliases,
        compiler_params=pltpu.CompilerParams(vmem_limit_bytes=VMEM_LIMIT),
        cost_estimate=pl.CostEstimate(flops=int(6e9), bytes_accessed=0, transcendentals=0),
        name="expert_ffn" if routed else "shared_ffn",
    )(scalars, *args)


def grad_blocks(offs, rows, pairs):
    tile = 384
    total = sum(b.shape[1] for _, b in pairs)

    def body(sc, *refs):
        keep, send, acc = refs[-3:]
        lo = 0
        for i in range(len(pairs)):
            a, b = refs[2 * i], refs[2 * i + 1]
            turned = a[...].T
            for j in range(0, b.shape[1], tile):
                width = min(tile, b.shape[1] - j)
                acc[:, :width] = mm(turned, b[:, j : j + width])
                for k in range(16):
                    at = pl.ds(pl.multiple_of(sc[k], 16), rows)
                    out = send if (k // 4) % 2 else keep
                    out[k // 8, k % 4, :, lo : lo + width] = acc[at, :width].astype(bf16)
                lo += width

    shape = sds((2, 4, rows, total), bf16)
    args = [m for pair in pairs for m in pair]
    return call(body, [shape, shape], scratch=[pltpu.VMEM((D, tile), f32)], us=3.0, name="grad_blocks")(
        offs, *args
    )


def per_device(
    tokens,
    segments,
    experts,
    attn_gain,
    qkv_proj,
    out_proj,
    ffn_gain,
    router_proj,
    expert_gate_up,
    expert_down,
    shared_gate_up,
    shared_down,
    cotangent,
):
    F, C = lax.axis_size("fsdp"), lax.axis_size("ctx")
    f, c, y = lax.axis_index("fsdp"), lax.axis_index("ctx"), lax.axis_index("tp")
    EL = expert_gate_up.shape[0]
    small = F == EL and C == 4
    heads_width = qkv_proj.shape[2]
    hidden = expert_down.shape[1]
    shared_hidden = shared_down.shape[0]
    zi = f % EL
    i32 = jnp.int32

    def yx(v):
        return lax.ppermute(v, "tp", [(0, 1), (1, 0)])

    def cx(v, flip):
        return lax.ppermute(v, "ctx", [(i, i ^ flip) for i in range(C)])

    def zs(v, s):
        return lax.ppermute(
            v, "fsdp", [(i, i // EL * EL + (i % EL + s) % EL) for i in range(F)]
        )

    scalars = jnp.stack([c, y, EL * c + zi]).astype(i32)
    rows_own = D // (F * C)
    rc = jnp.arange(4, dtype=i32)
    if small:
        dense_offs = (
            (((f - rc)[None, :] % 4) * 4 + (c ^ rc)[:, None]).reshape(16) * rows_own
        ).astype(i32)
        back_offs = (
            (((f + rc)[None, :] % 4) * 4 + (c ^ rc)[:, None]).reshape(16) * rows_own
        ).astype(i32)

    def gathered(shard, axis=0):
        return lax.all_gather(shard, ("fsdp", "ctx"), axis=axis, tiled=True)

    def reduce_near(keep, send):
        kind = keep.dtype
        near = cx(send, 1)
        far = cx((keep[1].astype(f32) + near[1].astype(f32)).astype(kind), 2)
        return keep[0].astype(f32) + near[0].astype(f32) + far.astype(f32)

    def reduce_far(part, kind, z_after=None, sum_after=None):
        pieces = [part[s].astype(kind) for s in (1, 2, 3)]
        if z_after is not None:
            pieces = [after(piece, z_after) for piece in pieces]
        total = part[0] if sum_after is None else after(part[0], sum_after)
        for s, piece in zip((1, 2, 3), pieces):
            total = total + zs(piece, s).astype(f32)
        return total

    def grad_of(a, b):
        return lax.dot_general(a, b, (((0,), (0,)), ((), ())), preferred_element_type=f32)

    def dense_reduce(pairs):
        full = jnp.concatenate([grad_of(a, b) for a, b in pairs], axis=1)
        return lax.psum_scatter(full, ("fsdp", "ctx"), scatter_dimension=0, tiled=True)

    def half(v, which):
        return lax.dynamic_slice_in_dim(v, which * HALF, HALF, v.ndim - 1)

    qkv_shard = jnp.concatenate(
        [
            qkv_proj.transpose(1, 0, 2).reshape(rows_own, 3 * heads_width),
            router_proj,
            attn_gain[:, None],
            ffn_gain[:, None],
            jnp.zeros((rows_own, 128 - E - 2), bf16),
        ],
        axis=1,
    )
    first = gathered(jnp.concatenate([qkv_shard, out_proj.T], axis=1))
    extra = first[:, 3 * heads_width : 3 * heads_width + 128]
    out_w = first[:, 3 * heads_width + 128 :]
    gains = extra[:, E : E + 2].astype(f32)
    gain_one, gain_two = gains[:, 0], gains[:, 1]
    gain_two_h = half(gain_two, y)
    gain_one_h = half(gain_one, y)
    shared_shard = jnp.concatenate([shared_gate_up, shared_down.T[None]])
    expert_local = jnp.concatenate(
        [expert_gate_up, expert_down.transpose(0, 2, 1)[:, None]], axis=1
    )
    if small:
        expert_w = None
    else:
        inner = [[g * EL + i for i in range(EL)] for g in range(F // EL)]
        outer = [[g * EL + i for g in range(F // EL)] for i in range(EL)]
        mine = lax.all_to_all(
            expert_local, "fsdp", 0, 0, axis_index_groups=inner, tiled=True
        )
        mine = lax.all_gather(mine, "fsdp", axis=0, axis_index_groups=outer, tiled=True)
        expert_w = mine.transpose(1, 0, 2, 3).reshape(1, 3, D, hidden)

    lanes = jnp.arange(E, dtype=i32)[None, :]
    named = [(experts[:, k : k + 1] == lanes) for k in range(2)]
    both = (named[0] | named[1]).astype(bf16)
    before = (jnp.arange(ROWS)[:, None] > jnp.arange(ROWS)[None, :]).astype(bf16)
    counts = jnp.dot(before, both, preferred_element_type=f32)
    code = jnp.stack(
        [
            experts[:, k] * CAP + jnp.sum(jnp.where(named[k], counts, 0.0), axis=1).astype(i32)
            for k in range(2)
        ]
    )
    code_two = jnp.stack([code, cx(code, 2)])
    code_core = cx(code_two, 1)
    codes = jnp.concatenate([code_two[0], code_core[0], code_two[1], code_core[1]], axis=0)
    which, rank = codes // CAP, codes % CAP
    ids = jnp.where(which // EL == c, ((which - zi) % EL) * CAP + rank, -1).astype(i32)

    def dispatch(own, dep=None):
        far = cx(own, 2)
        near = cx(own, 1)
        both_far = cx(far, 1)
        packs = call(
            pack_body, [sds((4 * CAP, HALF), bf16)] * 4, name="pack"
        )(scalars, ids if dep is None else after(ids, *dep), own, near, far, both_far)
        return [packs[0]] + [zs(packs[s], s) for s in (1, 2, 3)]

    def sum_pieces(pieces, dep=None):
        total = pieces[0]
        if dep is not None:
            total = after(total, dep)
        for piece in pieces[1:]:
            total = total + piece.astype(f32)
        return total

    def over_tp(two):
        return (two[0].astype(f32) + yx(two[1]).astype(f32)).astype(bf16)

    def home(s, total):
        return total if s == 0 else zs(total, EL - s)

    def over_ctx(keep, send):
        got = cx(send, 1)
        far = (keep[1].astype(f32) + got[1].astype(f32)).astype(bf16)
        return keep[0].astype(f32) + got[0].astype(f32) + cx(far, 2).astype(f32)

    cot_h, cot_o = half(cotangent, y), half(cotangent, 1 - y)
    cot_rows = dispatch(cot_h)
    cot_pairs = [(rows, yx(rows)) for rows in cot_rows]

    positions = (c * ROWS + jnp.arange(ROWS, dtype=i32)).astype(f32)
    table = jnp.arange(128, dtype=i32)
    frequency = 10000.0 ** (-(table % 32).astype(f32) / 32)
    angles = positions[:, None] * frequency[None, :]
    cos = jnp.cos(angles)
    sin = jnp.sin(angles) * jnp.where(table % 64 < 32, -1.0, 1.0)[None, :]
    normed_one, queries, kv = call(
        qkv_body,
        [sds((ROWS, D), bf16), sds((ROWS, heads_width), bf16), sds((ROWS, 2 * heads_width), bf16)],
        us=3.0, name="qkv",
    )(
        scalars, tokens, gain_one[None, :], first, cos, sin,
        deps=[cot_pairs[0][1], *cot_rows[1:], expert_local],
    )
    kv_far = cx(kv, 2)
    kv_near = cx(kv, 1)
    kv_both = cx(kv_far, 1)
    kvs = (kv, kv_near, kv_far, kv_both)
    if small:
        expert_w = lax.all_to_all(
            after(expert_local, kv_near), "fsdp", 0, 0, tiled=True
        )
    before_attn = [cot_pairs[1][1], cot_pairs[2][1]]
    seq_ids = segments[0]
    seg_col = seq_ids[:, None]
    seg_row = lax.dynamic_slice_in_dim(seq_ids, c * ROWS, ROWS, 0)[None, :]
    attended, z_own, z_oth, lse = call(
        attn_body,
        [
            sds((ROWS, heads_width), bf16),
            sds((ROWS, HALF), f32),
            sds((ROWS, HALF), bf16),
            sds((8, ROWS), f32),
        ],
        scratch=[
            pltpu.VMEM((4 * ROWS, 2 * heads_width), bf16),
            pltpu.VMEM((4 * ROWS, ROWS), f32),
            pltpu.VMEM((4 * ROWS, ROWS), f32),
            pltpu.VMEM((heads_width, ROWS), f32),
        ],
        us=9.0, name="attn",
    )(scalars, queries, *kvs, seg_col, seg_row, out_w, deps=before_attn)
    tok_h = half(tokens, y).astype(f32)
    middle = tok_h + z_own + yx(z_oth).astype(f32)

    def whole_rows(own):
        return halves(y, own, yx(own))

    def both_halves(sums):
        return sums + yx(sums)

    square = both_halves(jnp.sum(middle * middle, axis=1))
    scale_two = lax.rsqrt(square / D + eps)[:, None]
    normal_two = middle * scale_two
    normed_two = (normal_two * gain_two_h[None, :]).astype(bf16)

    normed_two_oth = yx(normed_two)
    rows_in = dispatch(normed_two, [cot_pairs[3][1]])
    shared_w = gathered(after(shared_shard, rows_in[3]), 1)[None]
    saved, backs, sums, router_part = None, [], [], 0.0
    pairs = [(rows, yx(rows)) for rows in rows_in]
    for s in range(4):
        deps = [rows_in[1:], [pairs[2][1], pairs[3][1]], sums[:1], sums[1:2]][s]
        res = ffn(scalars, s, 4, *pairs[s], *cot_pairs[s], expert_w, extra, saved, deps)
        sums.append(over_tp(res[0]))
        backs.append(home(s, sums[s]))
        router_part = router_part + res[1][:, :E]
        saved = res[2:]
    ex_dgu, ex_y, ex_x, ex_de = [v.reshape(4 * ROWS, -1) for v in saved]

    grad_w = [
        lax.dot_general(a, b, (((0,), (0,)), ((), ())), preferred_element_type=f32)
        for a, b in ((ex_x, ex_dgu[:, :hidden]), (ex_x, ex_dgu[:, hidden:]), (ex_de, ex_y))
    ]
    if small:
        grad_w = [g.astype(bf16).reshape(4, D // 4, hidden) for g in grad_w]
        grad_w = grad_ready = jnp.stack(grad_w, axis=1)
        grad_w = lax.all_to_all(
            grad_w, "fsdp", 0, 0, tiled=True
        )
    else:
        grad_ready = saved[0]
        grad_w = jnp.stack([g.reshape(F, D // F, hidden) for g in grad_w], axis=1)
        grad_w = lax.psum_scatter(
            grad_w, "fsdp", scatter_dimension=0, axis_index_groups=outer, tiled=True
        )
        grad_w = lax.all_to_all(grad_w, "fsdp", 0, 0, axis_index_groups=inner, tiled=True)

    sh_back, sh_dgu, sh_y = ffn(
        scalars, 0, 1, normed_two, normed_two_oth, cot_h, cot_o, shared_w, None, None, [grad_ready]
    )
    sh_sum = sh_back[0].astype(f32) + yx(sh_back[1]).astype(f32)
    normed_full = halves(y, normed_two, normed_two_oth)
    shared_full = jnp.concatenate(
        [grad_of(normed_full, sh_dgu[0]), grad_of(cotangent, sh_y[0])], axis=1
    )
    shared_grad = lax.psum_scatter(
        shared_full.astype(bf16) if small else shared_full,
        ("fsdp", "ctx"), scatter_dimension=0, tiled=True,
    ).astype(f32)

    keep_b, send_b, keep_o, send_o = call(
        unpack_body, [sds((2, ROWS, HALF), bf16)] * 4, us=3.0, name="unpack"
    )(scalars, ids, *backs, deps=[sh_sum])
    back_h = over_ctx(keep_b, send_b) + sh_sum[:, :HALF]
    scaled = back_h * gain_two_h[None, :]
    mean_two = both_halves(jnp.sum(scaled * normal_two, axis=1))[:, None] / D
    ffn_gain_part = jnp.sum(back_h * normal_two, axis=0)
    middle_grad = cot_h.astype(f32) + scale_two * (scaled - normal_two * mean_two)
    dz_own = middle_grad.astype(bf16)
    dz_oth = yx(dz_own)
    dq, dkv_keep, dkv_send = call(
        attn_back_body,
        [sds((ROWS, heads_width), bf16)] + [sds((2, ROWS, 2 * heads_width), bf16)] * 2,
        scratch=[
            pltpu.VMEM((4 * ROWS, 2 * heads_width), bf16),
            pltpu.VMEM((4 * ROWS, ROWS), f32),
            pltpu.VMEM((ROWS, heads_width), bf16),
            pltpu.VMEM((8, ROWS), f32),
            pltpu.VMEM((heads_width, ROWS), f32),
        ],
        us=11.0, name="attn_back",
    )(
        scalars, queries, *kvs, seg_col, seg_row, lse, attended, dz_own, dz_oth, out_w, cos, sin,
    )
    dkv_near = cx(dkv_send, 1)
    kv_recv = cx((dkv_keep[1].astype(f32) + dkv_near[1].astype(f32)).astype(bf16), 2)
    dp, da_own, da_oth = call(
        proj_back_body,
        [sds((ROWS, 3 * heads_width), bf16), sds((ROWS, HALF), f32), sds((ROWS, HALF), bf16)],
        us=3.0, name="proj_back",
    )(scalars, dq, dkv_keep, dkv_near, kv_recv, first, cos, sin, deps=[grad_w])
    dense_pairs = [(normed_one, dp), (halves(y, dz_own, dz_oth), attended)]
    if small:
        dense_keep, dense_send = grad_blocks(back_offs, rows_own, dense_pairs)
    else:
        dense_keep = dp
    da_h = after(da_own, dense_keep) + yx(da_oth).astype(f32)
    tok_full = tokens.astype(f32)
    scale_one = lax.rsqrt(jnp.mean(tok_full * tok_full, axis=1, keepdims=True) + eps)
    normal_one = tok_h * scale_one
    scaled_one = da_h * gain_one_h[None, :]
    mean_one = both_halves(jnp.sum(scaled_one * normal_one, axis=1))[:, None] / D
    attn_gain_part = jnp.sum(da_h * normal_one, axis=0)
    tokens_grad_h = middle_grad + scale_one * (scaled_one - normal_one * mean_one)

    tokens_grad = whole_rows(tokens_grad_h.astype(bf16)).astype(f32)

    layer_h = middle + over_ctx(keep_o, send_o) + sh_sum[:, HALF:]
    layer_out = whole_rows(layer_h.astype(bf16))
    grad_w = after(grad_w, tokens_grad_h)
    expert_gate_up_grad = grad_w[:, :2].astype(f32)
    expert_down_grad = grad_w[:, 2].astype(f32).transpose(0, 2, 1)
    if small:
        dense_grad = reduce_far(reduce_near(dense_keep, dense_send), bf16, None, tokens_grad_h)
    else:
        dense_grad = dense_reduce(dense_pairs)
    qkv_grad = dense_grad[:, : 3 * heads_width].reshape(rows_own, 3, heads_width).transpose(1, 0, 2)
    out_grad = dense_grad[:, 3 * heads_width :].T
    shared_gate_up_grad = jnp.stack(
        [shared_grad[:, :shared_hidden], shared_grad[:, shared_hidden : 2 * shared_hidden]]
    )
    shared_down_grad = shared_grad[:, 2 * shared_hidden :].T

    def placed(part):
        first = y == 0
        return jnp.concatenate([jnp.where(first, part, 0.0), jnp.where(first, 0.0, part)])

    tail = jnp.concatenate(
        [router_part, placed(attn_gain_part)[:, None], placed(ffn_gain_part)[:, None]], axis=1
    )
    if small:
        order = back_offs // rows_own
        blocks = tail.reshape(16, rows_own * (E + 2))[order].reshape(2, 2, 4, rows_own * (E + 2))
        tail = reduce_far(reduce_near(blocks[:, 0], blocks[:, 1]), f32)
        tail = tail.reshape(rows_own, E + 2)
    else:
        tail = lax.psum_scatter(tail, ("fsdp", "ctx"), scatter_dimension=0, tiled=True)
    tail = tail + yx(tail)
    return (
        layer_out,
        tokens_grad,
        tail[:, E],
        qkv_grad,
        out_grad,
        tail[:, E + 1],
        tail[:, :E],
        expert_gate_up_grad,
        expert_down_grad,
        shared_gate_up_grad,
        shared_down_grad,
    )


def solution(mesh):
    return jax.shard_map(
        per_device,
        mesh=mesh,
        in_specs=(
            P(("fsdp", "ctx"), None),
            P("fsdp", None),
            P(("fsdp", "ctx"), None),
            P(("fsdp", "ctx")),
            P(None, ("fsdp", "ctx"), "tp"),
            P("tp", ("fsdp", "ctx")),
            P(("fsdp", "ctx")),
            P(("fsdp", "ctx"), None),
            P("ctx", None, "fsdp", "tp"),
            P("ctx", "tp", "fsdp"),
            P(None, ("fsdp", "ctx"), "tp"),
            P("tp", ("fsdp", "ctx")),
            P(("fsdp", "ctx"), None),
        ),
        out_specs=(
            P(("fsdp", "ctx"), None),
            P(("fsdp", "ctx"), None),
            P(("fsdp", "ctx")),
            P(None, ("fsdp", "ctx"), "tp"),
            P("tp", ("fsdp", "ctx")),
            P(("fsdp", "ctx")),
            P(("fsdp", "ctx"), None),
            P("ctx", None, "fsdp", "tp"),
            P("ctx", "tp", "fsdp"),
            P(None, ("fsdp", "ctx"), "tp"),
            P("tp", ("fsdp", "ctx")),
        ),
        check_vma=False,
    )
```

```python
import functools

import jax
import jax.numpy as jnp
from jax import lax
from jax.experimental import pallas as pl
from jax.experimental.pallas import tpu as pltpu
from jax.sharding import PartitionSpec as P

D = 768
HALF = D // 2
HD = 64
E = 16
ROWS = 512
CAP = 128
NEG = -1e30
eps = 1e-06
bf16 = jnp.bfloat16
f32 = jnp.float32
VMEM_LIMIT = 56 * 1024 * 1024


def mm(a, b):
    return lax.dot_general(a, b, (((1,), (0,)), ((), ())), preferred_element_type=f32)


def mm_t(a, b):
    return lax.dot_general(a, b, (((1,), (1,)), ((), ())), preferred_element_type=f32)


def t_mm(a, b):
    return lax.dot_general(a, b, (((0,), (0,)), ((), ())), preferred_element_type=f32)


def sds(shape, dtype):
    return jax.ShapeDtypeStruct(shape, dtype)


SMEM = pl.BlockSpec(memory_space=pltpu.SMEM)
VM = pl.BlockSpec(memory_space=pltpu.VMEM)


def call(body, outs, scratch=(), us=1.0, name=None):
    def run(scalars, *args, deps=()):
        count = 1 + len(args)

        def inner(*refs):
            body(*refs[:count], *refs[count + len(deps) :])

        return pl.pallas_call(
            inner,
            out_shape=outs,
            in_specs=[SMEM] + [VM] * len(args) + [pl.BlockSpec(memory_space=pl.ANY)] * len(deps),
            out_specs=jax.tree.map(lambda _: VM, outs),
            scratch_shapes=list(scratch),
            compiler_params=pltpu.CompilerParams(vmem_limit_bytes=VMEM_LIMIT),
            cost_estimate=pl.CostEstimate(
                flops=int(us * 1.1e9), bytes_accessed=0, transcendentals=0
            ),
            name=name,
        )(scalars, *args, *deps)

    return run


def after(v, *deps):
    return lax.optimization_barrier((v,) + deps)[0]


def partner(v, lane):
    return jnp.where(lane % 64 < 32, pltpu.roll(v, 96, 1), pltpu.roll(v, 32, 1))


def lane_id(rows):
    return lax.broadcasted_iota(jnp.int32, (rows, 128), 1)


def qkv_body(sc, tok, gain, w, cos, sin, a_o, q_o, kv_o):
    x = tok[...].astype(f32)
    scale = lax.rsqrt(jnp.mean(x * x, axis=1, keepdims=True) + eps)
    a = (x * scale * gain[...]).astype(bf16)
    a_o[...] = a
    n = q_o.shape[1]
    lane = lane_id(ROWS)
    for g in range(3 * n // 128):
        v = mm(a, w[:, g * 128 : (g + 1) * 128])
        lo = g * 128
        if lo < n:
            r = v * cos[...] + partner(v, lane) * sin[...]
            q_o[:, lo : lo + 128] = (r.astype(bf16).astype(f32) * (HD**-0.5)).astype(bf16)
        elif lo < 2 * n:
            r = v * cos[...] + partner(v, lane) * sin[...]
            kv_o[:, lo - n : lo - n + 128] = r.astype(bf16)
        else:
            kv_o[:, lo - n : lo - n + 128] = v.astype(bf16)


def block_bias(c, kb, segc, segq):
    off = pl.multiple_of(kb * ROWS, ROWS)
    kpos = off + lax.broadcasted_iota(jnp.int32, (ROWS, ROWS), 0)
    qpos = c * ROWS + lax.broadcasted_iota(jnp.int32, (ROWS, ROWS), 1)
    ok = (segc[pl.ds(off, ROWS), :] == segq[...]) & (kpos <= qpos)
    return jnp.where(ok, 0.0, NEG)


def attn_body(sc, q, k0, k1, k2, k3, segc, segq, wo, o_o, zown_o, zoth_o, lse_o, kvs, bias, st, ot):
    c, y = sc[0], sc[1]
    nb = c + 1
    n = q.shape[1]
    for r, ref in enumerate((k0, k1, k2, k3)):
        kvs[pl.ds(pl.multiple_of((c ^ r) * ROWS, ROWS), ROWS), :] = ref[...]

    def bias_step(kb, carry):
        bias[pl.ds(pl.multiple_of(kb * ROWS, ROWS), ROWS), :] = block_bias(c, kb, segc, segq)
        return carry

    lax.fori_loop(0, nb, bias_step, 0)
    for h in range(n // HD):
        lo = h * HD
        qh = q[:, lo : lo + HD]

        def score_step(kb, m, lo=lo, qh=qh):
            rows = pl.ds(pl.multiple_of(kb * ROWS, ROWS), ROWS)
            s = mm_t(kvs[rows, lo : lo + HD], qh) + bias[rows, :]
            st[rows, :] = s
            return jnp.maximum(m, jnp.max(s, axis=0, keepdims=True))

        m = lax.fori_loop(0, nb, score_step, jnp.full((1, ROWS), NEG, f32))

        def value_step(kb, carry, lo=lo, m=m):
            total, acc = carry
            rows = pl.ds(pl.multiple_of(kb * ROWS, ROWS), ROWS)
            p = jnp.exp(st[rows, :] - m)
            total = total + jnp.sum(p, axis=0, keepdims=True)
            return total, acc + t_mm(kvs[rows, n + lo : n + lo + HD], p.astype(bf16))

        total, acc = lax.fori_loop(
            0, nb, value_step, (jnp.zeros((1, ROWS), f32), jnp.zeros((HD, ROWS), f32))
        )
        ot[lo : lo + HD, :] = acc / total
        lse_o[h : h + 1, :] = m + jnp.log(total)
    o = ot[...].T.astype(bf16)
    o_o[...] = o
    own = pl.ds(pl.multiple_of(y * HALF, HALF), HALF)
    oth = pl.ds(pl.multiple_of((1 - y) * HALF, HALF), HALF)
    zoth_o[...] = mm_t(o, wo[oth, :]).astype(bf16)
    zown_o[...] = mm_t(o, wo[own, :])


def attn_back_body(
    sc, q, k0, k1, k2, k3, segc, segq, lse, o, zown, zoth, wo, cos, sin, dq_o, keep_o, send_o,
    kvs, bias, do_s, delta, dqt,
):
    c, y = sc[0], sc[1]
    nb = c + 1
    n = q.shape[1]
    heads = n // HD
    for r, ref in enumerate((k0, k1, k2, k3)):
        kvs[pl.ds(pl.multiple_of((c ^ r) * ROWS, ROWS), ROWS), :] = ref[...]

    def bias_step(kb, carry):
        bias[pl.ds(pl.multiple_of(kb * ROWS, ROWS), ROWS), :] = block_bias(c, kb, segc, segq)
        return carry

    lax.fori_loop(0, nb, bias_step, 0)
    own = pl.ds(pl.multiple_of(y * HALF, HALF), HALF)
    oth = pl.ds(pl.multiple_of((1 - y) * HALF, HALF), HALF)
    do = (mm(zown[...], wo[own, :]) + mm(zoth[...], wo[oth, :])).astype(bf16)
    do_s[...] = do
    pick = (
        lax.broadcasted_iota(jnp.int32, (8, n), 1) // HD
        == lax.broadcasted_iota(jnp.int32, (8, n), 0)
    ).astype(f32)
    delta[...] = lax.dot_general(
        pick,
        do.astype(f32) * o[...].astype(f32),
        (((1,), (1,)), ((), ())),
        precision=lax.Precision.HIGHEST,
        preferred_element_type=f32,
    )

    def put(kb, cols, value):
        at = kb ^ c

        @pl.when(at % 2 == 0)
        def _():
            keep_o[at // 2, :, cols] = value

        @pl.when(at % 2 == 1)
        def _():
            send_o[at // 2, :, cols] = value

    def zero_step(kb, carry):
        put(kb, slice(None), jnp.zeros((ROWS, 2 * n), bf16))
        return carry

    lax.fori_loop(nb, 4, zero_step, 0)
    for pair in range(heads // 2):
        at = pair * 128

        def step(kb, carry, at=at, pair=pair):
            rows = pl.ds(pl.multiple_of(kb * ROWS, ROWS), ROWS)
            dks, dvs, dqs = [], [], []
            for i in range(2):
                lo = at + i * HD
                h = 2 * pair + i
                kh = kvs[rows, lo : lo + HD]
                vh = kvs[rows, n + lo : n + lo + HD]
                qh = q[:, lo : lo + HD]
                dh = do_s[:, lo : lo + HD]
                p = jnp.exp(mm_t(kh, qh) + bias[rows, :] - lse[h : h + 1, :])
                ds = (p * (mm_t(vh, dh) - delta[h : h + 1, :])).astype(bf16)
                dvs.append(mm(p.astype(bf16), dh))
                dks.append(mm(ds, qh))
                dqs.append(carry[i] + t_mm(kh, ds))
            put(kb, slice(at, at + 128), jnp.concatenate(dks, axis=1).astype(bf16))
            put(kb, slice(n + at, n + at + 128), jnp.concatenate(dvs, axis=1).astype(bf16))
            return tuple(dqs)

        zero = jnp.zeros((HD, ROWS), f32)
        dqs = lax.fori_loop(0, nb, step, (zero, zero))
        dqt[at : at + HD, :] = dqs[0]
        dqt[at + HD : at + 128, :] = dqs[1]
    lane = lane_id(ROWS)
    for g in range(n // 128):
        v = dqt[g * 128 : (g + 1) * 128, :].T * (HD**-0.5)
        dq_o[:, g * 128 : (g + 1) * 128] = (v * cos[...] - partner(v, lane) * sin[...]).astype(bf16)


def proj_back_body(sc, dq, keep, near, recv, w, cos, sin, dp_o, own_o, oth_o):
    y = sc[1]
    n = dq.shape[1]
    lane = lane_id(ROWS)
    dp_o[:, :n] = dq[...]
    for g in range(2 * n // 128):
        cols = slice(g * 128, (g + 1) * 128)
        v = keep[0, :, cols].astype(f32) + near[0, :, cols].astype(f32) + recv[:, cols].astype(f32)
        if g < n // 128:
            v = v * cos[...] - partner(v, lane) * sin[...]
        dp_o[:, n + g * 128 : n + (g + 1) * 128] = v.astype(bf16)
    own = pl.ds(pl.multiple_of(y * HALF, HALF), HALF)
    oth = pl.ds(pl.multiple_of((1 - y) * HALF, HALF), HALF)
    oth_o[...] = mm_t(dp_o[...], w[oth, : 3 * n]).astype(bf16)
    own_o[...] = mm_t(dp_o[...], w[own, : 3 * n])


def slots_onehot(ids, r):
    i = lax.broadcasted_iota(jnp.int32, (4 * CAP, ROWS), 0)
    hit = (i == ids[2 * r : 2 * r + 1, :]) | (i == ids[2 * r + 1 : 2 * r + 2, :])
    return jnp.where(hit, 1.0, 0.0).astype(bf16)


def pack_body(sc, ids, b0, b1, b2, b3, p0, p1, p2, p3):
    for r, ref in enumerate((b0, b1, b2, b3)):
        rows = mm(slots_onehot(ids, r), ref[...]).astype(bf16)
        for s, out in enumerate((p0, p1, p2, p3)):
            out[r * CAP : (r + 1) * CAP, :] = rows[s * CAP : (s + 1) * CAP, :]


def unpack_body(sc, ids, p0, p1, p2, p3, keep_b, send_b, keep_o, send_o):
    for r in (1, 3, 0, 2):
        rows = jnp.concatenate(
            [p[r * CAP : (r + 1) * CAP, :] for p in (p0, p1, p2, p3)], axis=0
        )
        tok = t_mm(slots_onehot(ids, r), rows).astype(bf16)
        for at, pair in ((0, (keep_b, send_b)), (HALF, (keep_o, send_o))):
            pair[r % 2][r // 2] = tok[:, at : at + HALF]


def halves(y, a, b):
    first = y == 0
    return jnp.concatenate([jnp.where(first, a, b), jnp.where(first, b, a)], axis=1)


def ffn_body(routed, sc, xa, xb, wa, wb, weights, rt, *refs):
    if routed:
        refs = refs[len(refs) - 8 :]
        back_o, rg_o, dgu_o, y_o, x_o, de_o, acc_o, acc_b = refs
    else:
        back_o, dgu_o, y_o, acc_o, acc_b = refs[len(refs) - 5 :]
    y, e = sc[1], sc[2]
    x = halves(y, xa[...], xb[...])
    w = halves(y, wa[...], wb[...])
    hidden = weights.shape[3]
    if routed:
        lane = lane_id(ROWS)
        logits = jnp.where(lane < E, mm(x, rt[...]), NEG)
        ex = jnp.exp(logits - jnp.max(logits, axis=1, keepdims=True))
        probs = ex / jnp.sum(ex, axis=1, keepdims=True)
        gate = jnp.sum(jnp.where(lane == e, probs, 0.0), axis=1, keepdims=True)
        x_o[0] = x
        de_o[0] = (w.astype(f32) * gate).astype(bf16)
    acc_o[...] = jnp.zeros_like(acc_o)
    acc_b[...] = jnp.zeros_like(acc_b)
    tile = 256

    def columns(which, lo):
        cols = pl.ds(pl.multiple_of(lo, tile), tile)
        return jnp.concatenate(
            [weights[j, which, :, cols] for j in range(weights.shape[0])], axis=0
        )

    def step(j, dots):
        lo = pl.multiple_of(j * tile, tile)
        hi = pl.multiple_of(hidden + j * tile, tile)
        g = mm(x, columns(0, lo))
        u = mm(x, columns(1, lo))
        h = mm(w, columns(2, lo))
        sg = 1.0 / (1.0 + jnp.exp(-g))
        act = g * sg
        yv = (act * u).astype(bf16)
        if routed:
            dots = dots + jnp.sum(yv.astype(f32) * h, axis=1, keepdims=True)
            h = h * gate
        dg = (h * u * (sg + act * (1.0 - sg))).astype(bf16)
        du = (h * act).astype(bf16)
        y_o[0, :, pl.ds(lo, tile)] = yv
        dgu_o[0, :, pl.ds(lo, tile)] = dg
        dgu_o[0, :, pl.ds(hi, tile)] = du
        acc_o[...] += mm_t(yv, columns(2, lo))
        acc_b[...] += mm_t(dg, columns(0, lo)) + mm_t(du, columns(1, lo))
        return dots

    dots = lax.fori_loop(0, hidden // tile, step, jnp.zeros((ROWS, 1), f32))
    if routed:
        coef = (dots * gate) * (jnp.where(lane == e, 1.0, 0.0) - probs)
        coef = jnp.where(lane < E, coef, 0.0).astype(bf16)
        acc_b[...] += mm_t(coef, rt[...])
        rg_o[...] = t_mm(x, coef)
    for i, at in enumerate((y, 1 - y)):
        cols = pl.ds(pl.multiple_of(at * HALF, HALF), HALF)
        out = acc_o[:, cols]
        if routed:
            out = out * gate
        back_o[i, :, :HALF] = acc_b[:, cols].astype(bf16)
        back_o[i, :, HALF:] = out.astype(bf16)


def ffn(scalars, s, groups, xa, xb, wa, wb, weights, rt, prev, deps=()):
    routed = rt is not None
    hidden = weights.shape[3]
    full = lambda shape: pl.BlockSpec(shape, lambda i, n=len(shape): (0,) * n)
    part = lambda width: pl.BlockSpec((1, ROWS, width), lambda i: (s, 0, 0))
    two = (2, ROWS, D)
    outs = [sds(two, bf16)]
    out_specs = [full(two)]
    if routed:
        outs.append(sds((D, 128), f32))
        out_specs.append(full((D, 128)))
    widths = [2 * hidden, hidden] + ([D, D] if routed else [])
    base = len(outs)
    for width in widths:
        outs.append(sds((groups, ROWS, width), bf16))
        out_specs.append(part(width))
    args = [xa, xb, wa, wb, weights] + ([rt] if routed else [])
    in_specs = [SMEM] + [full(a.shape) for a in args]
    aliases = {}
    if not routed:
        args.append(scalars)
        in_specs.append(SMEM)
    for arr in deps:
        args.append(arr)
        in_specs.append(pl.BlockSpec(memory_space=pl.ANY))
    if prev is not None:
        for i, arr in enumerate(prev):
            aliases[1 + len(args)] = base + i
            args.append(arr)
            in_specs.append(pl.BlockSpec(memory_space=pl.ANY))
    return pl.pallas_call(
        functools.partial(ffn_body, routed),
        grid=(1,),
        out_shape=outs,
        in_specs=in_specs,
        out_specs=out_specs,
        scratch_shapes=[pltpu.VMEM((ROWS, D), f32), pltpu.VMEM((ROWS, D), f32)],
        input_output_aliases=aliases,
        compiler_params=pltpu.CompilerParams(vmem_limit_bytes=VMEM_LIMIT),
        cost_estimate=pl.CostEstimate(flops=int(16e9) if routed else 0, bytes_accessed=0, transcendentals=0),
        name="expert_ffn" if routed else "shared_ffn",
    )(scalars, *args)


def grad_blocks(offs, rows, pairs):
    tile = 384
    total = sum(b.shape[1] for _, b in pairs)

    def body(sc, *refs):
        keep, send, acc = refs[-3:]
        lo = 0
        for i in range(len(pairs)):
            a, b = refs[2 * i], refs[2 * i + 1]
            turned = a[...].T
            for j in range(0, b.shape[1], tile):
                width = min(tile, b.shape[1] - j)
                acc[:, :width] = mm(turned, b[:, j : j + width])
                for k in range(16):
                    at = pl.ds(pl.multiple_of(sc[k], 16), rows)
                    out = send if (k // 4) % 2 else keep
                    out[k // 8, k % 4, :, lo : lo + width] = acc[at, :width].astype(bf16)
                lo += width

    shape = sds((2, 4, rows, total), bf16)
    args = [m for pair in pairs for m in pair]
    return call(body, [shape, shape], scratch=[pltpu.VMEM((D, tile), f32)], us=3.0, name="grad_blocks")(
        offs, *args
    )


def per_device(
    tokens,
    segments,
    experts,
    attn_gain,
    qkv_proj,
    out_proj,
    ffn_gain,
    router_proj,
    expert_gate_up,
    expert_down,
    shared_gate_up,
    shared_down,
    cotangent,
):
    F, C = lax.axis_size("fsdp"), lax.axis_size("ctx")
    f, c, y = lax.axis_index("fsdp"), lax.axis_index("ctx"), lax.axis_index("tp")
    EL = expert_gate_up.shape[0]
    small = F == EL and C == 4
    heads_width = qkv_proj.shape[2]
    hidden = expert_down.shape[1]
    shared_hidden = shared_down.shape[0]
    zi = f % EL
    i32 = jnp.int32

    def yx(v):
        return lax.ppermute(v, "tp", [(0, 1), (1, 0)])

    def cx(v, flip):
        return lax.ppermute(v, "ctx", [(i, i ^ flip) for i in range(C)])

    def zs(v, s):
        return lax.ppermute(
            v, "fsdp", [(i, i // EL * EL + (i % EL + s) % EL) for i in range(F)]
        )

    scalars = jnp.stack([c, y, EL * c + zi]).astype(i32)
    rows_own = D // (F * C)
    rc = jnp.arange(4, dtype=i32)
    if small:
        dense_offs = (
            (((f - rc)[None, :] % 4) * 4 + (c ^ rc)[:, None]).reshape(16) * rows_own
        ).astype(i32)
        back_offs = (
            (((f + rc)[None, :] % 4) * 4 + (c ^ rc)[:, None]).reshape(16) * rows_own
        ).astype(i32)

    def gathered(shard, axis=0):
        return lax.all_gather(shard, ("fsdp", "ctx"), axis=axis, tiled=True)

    def reduce_near(keep, send):
        kind = keep.dtype
        near = cx(send, 1)
        far = cx((keep[1].astype(f32) + near[1].astype(f32)).astype(kind), 2)
        return keep[0].astype(f32) + near[0].astype(f32) + far.astype(f32)

    def reduce_far(part, kind, z_after=None, sum_after=None):
        pieces = [part[s].astype(kind) for s in (1, 2, 3)]
        if z_after is not None:
            pieces = [after(piece, z_after) for piece in pieces]
        total = part[0] if sum_after is None else after(part[0], sum_after)
        for s, piece in zip((1, 2, 3), pieces):
            total = total + zs(piece, s).astype(f32)
        return total

    def grad_of(a, b):
        return lax.dot_general(a, b, (((0,), (0,)), ((), ())), preferred_element_type=f32)

    def dense_reduce(pairs):
        full = jnp.concatenate([grad_of(a, b) for a, b in pairs], axis=1)
        return lax.psum_scatter(full, ("fsdp", "ctx"), scatter_dimension=0, tiled=True)

    def half(v, which):
        return lax.dynamic_slice_in_dim(v, which * HALF, HALF, v.ndim - 1)

    qkv_shard = jnp.concatenate(
        [
            qkv_proj.transpose(1, 0, 2).reshape(rows_own, 3 * heads_width),
            router_proj,
            attn_gain[:, None],
            ffn_gain[:, None],
            jnp.zeros((rows_own, 128 - E - 2), bf16),
        ],
        axis=1,
    )
    first = gathered(jnp.concatenate([qkv_shard, out_proj.T], axis=1))
    extra = first[:, 3 * heads_width : 3 * heads_width + 128]
    out_w = first[:, 3 * heads_width + 128 :]
    gains = extra[:, E : E + 2].astype(f32)
    gain_one, gain_two = gains[:, 0], gains[:, 1]
    gain_two_h = half(gain_two, y)
    gain_one_h = half(gain_one, y)
    shared_shard = jnp.concatenate([shared_gate_up, shared_down.T[None]])
    expert_local = jnp.concatenate(
        [expert_gate_up, expert_down.transpose(0, 2, 1)[:, None]], axis=1
    )
    if small:
        expert_w = None
    else:
        inner = [[g * EL + i for i in range(EL)] for g in range(F // EL)]
        outer = [[g * EL + i for g in range(F // EL)] for i in range(EL)]
        mine = lax.all_to_all(
            expert_local, "fsdp", 0, 0, axis_index_groups=inner, tiled=True
        )
        mine = lax.all_gather(mine, "fsdp", axis=0, axis_index_groups=outer, tiled=True)
        expert_w = mine.transpose(1, 0, 2, 3).reshape(1, 3, D, hidden)

    lanes = jnp.arange(E, dtype=i32)[None, :]
    named = [(experts[:, k : k + 1] == lanes) for k in range(2)]
    both = (named[0] | named[1]).astype(bf16)
    before = (jnp.arange(ROWS)[:, None] > jnp.arange(ROWS)[None, :]).astype(bf16)
    counts = jnp.dot(before, both, preferred_element_type=f32)
    code = jnp.stack(
        [
            experts[:, k] * CAP + jnp.sum(jnp.where(named[k], counts, 0.0), axis=1).astype(i32)
            for k in range(2)
        ]
    )
    code_two = jnp.stack([code, cx(code, 2)])
    code_core = cx(code_two, 1)
    codes = jnp.concatenate([code_two[0], code_core[0], code_two[1], code_core[1]], axis=0)
    which, rank = codes // CAP, codes % CAP
    ids = jnp.where(which // EL == c, ((which - zi) % EL) * CAP + rank, -1).astype(i32)

    def dispatch(own, dep=None):
        far = cx(own, 2)
        near = cx(own, 1)
        both_far = cx(far, 1)
        packs = call(
            pack_body, [sds((4 * CAP, HALF), bf16)] * 4, name="pack"
        )(scalars, ids if dep is None else after(ids, *dep), own, near, far, both_far)
        return [packs[0]] + [zs(packs[s], s) for s in (1, 2, 3)]

    def sum_pieces(pieces, dep=None):
        total = pieces[0]
        if dep is not None:
            total = after(total, dep)
        for piece in pieces[1:]:
            total = total + piece.astype(f32)
        return total

    def over_tp(two):
        return (two[0].astype(f32) + yx(two[1]).astype(f32)).astype(bf16)

    def home(s, total):
        return total if s == 0 else zs(total, EL - s)

    def over_ctx(keep, send):
        got = cx(send, 1)
        far = (keep[1].astype(f32) + got[1].astype(f32)).astype(bf16)
        return keep[0].astype(f32) + got[0].astype(f32) + cx(far, 2).astype(f32)

    cot_h, cot_o = half(cotangent, y), half(cotangent, 1 - y)
    cot_rows = dispatch(cot_h)
    cot_pairs = [(rows, yx(rows)) for rows in cot_rows]

    positions = (c * ROWS + jnp.arange(ROWS, dtype=i32)).astype(f32)
    table = jnp.arange(128, dtype=i32)
    frequency = 10000.0 ** (-(table % 32).astype(f32) / 32)
    angles = positions[:, None] * frequency[None, :]
    cos = jnp.cos(angles)
    sin = jnp.sin(angles) * jnp.where(table % 64 < 32, -1.0, 1.0)[None, :]
    normed_one, queries, kv = call(
        qkv_body,
        [sds((ROWS, D), bf16), sds((ROWS, heads_width), bf16), sds((ROWS, 2 * heads_width), bf16)],
        us=5.0, name="qkv",
    )(
        scalars, tokens, gain_one[None, :], first, cos, sin,
        deps=[cot_pairs[0][1], *cot_rows[1:], expert_local],
    )
    kv_far = cx(kv, 2)
    kv_near = cx(kv, 1)
    kv_both = cx(kv_far, 1)
    kvs = (kv, kv_near, kv_far, kv_both)
    if small:
        expert_w = lax.all_to_all(
            after(expert_local, kv_near), "fsdp", 0, 0, tiled=True
        )
    before_attn = []
    seq_ids = segments[0]
    seg_col = seq_ids[:, None]
    seg_row = lax.dynamic_slice_in_dim(seq_ids, c * ROWS, ROWS, 0)[None, :]
    attended, z_own, z_oth, lse = call(
        attn_body,
        [
            sds((ROWS, heads_width), bf16),
            sds((ROWS, HALF), f32),
            sds((ROWS, HALF), bf16),
            sds((8, ROWS), f32),
        ],
        scratch=[
            pltpu.VMEM((4 * ROWS, 2 * heads_width), bf16),
            pltpu.VMEM((4 * ROWS, ROWS), f32),
            pltpu.VMEM((4 * ROWS, ROWS), f32),
            pltpu.VMEM((heads_width, ROWS), f32),
        ],
        us=17.0, name="attn",
    )(scalars, queries, *kvs, seg_col, seg_row, out_w, deps=before_attn)
    tok_h = half(tokens, y).astype(f32)
    middle = tok_h + z_own + yx(z_oth).astype(f32)

    def whole_rows(own):
        return halves(y, own, yx(own))

    def both_halves(sums):
        return sums + yx(sums)

    square = both_halves(jnp.sum(middle * middle, axis=1))
    scale_two = lax.rsqrt(square / D + eps)[:, None]
    normal_two = middle * scale_two
    normed_two = (normal_two * gain_two_h[None, :]).astype(bf16)

    normed_two_oth = yx(normed_two)
    rows_in = dispatch(normed_two, [normed_two_oth])
    shared_w = gathered(after(shared_shard, rows_in[3]), 1)[None]
    saved, backs, sums, router_part = None, [None] * 4, [], 0.0
    tied = [rows_in[0]] + [after(rows, *[pair[1] for pair in cot_pairs]) for rows in rows_in[1:]]
    pairs = [(rows, yx(rows)) for rows in tied]
    for i, s in enumerate((2, 1, 3, 0)):
        deps = [rows_in[1:], [pairs[3][1], pairs[0][1]], sums[:1], sums[1:2]][i]
        res = ffn(scalars, s, 4, *pairs[s], *cot_pairs[s], expert_w, extra, saved, deps)
        sums.append(over_tp(res[0]))
        backs[s] = home(s, sums[i])
        router_part = router_part + res[1][:, :E]
        saved = res[2:]
    ex_dgu, ex_y, ex_x, ex_de = [v.reshape(4 * ROWS, -1) for v in saved]
    ex_x = after(ex_x, backs[2])

    grad_w = [
        lax.dot_general(a, b, (((0,), (0,)), ((), ())), preferred_element_type=f32)
        for a, b in ((ex_x, ex_dgu[:, :hidden]), (ex_x, ex_dgu[:, hidden:]), (ex_de, ex_y))
    ]
    if small:
        grad_w = [g.astype(bf16).reshape(4, D // 4, hidden) for g in grad_w]
        grad_w = grad_ready = jnp.stack(grad_w, axis=1)
        grad_w = lax.all_to_all(
            grad_w, "fsdp", 0, 0, tiled=True
        )
    else:
        grad_ready = saved[0]
        grad_w = jnp.stack([g.reshape(F, D // F, hidden) for g in grad_w], axis=1)
        grad_w = lax.psum_scatter(
            grad_w, "fsdp", scatter_dimension=0, axis_index_groups=outer, tiled=True
        )
        grad_w = lax.all_to_all(grad_w, "fsdp", 0, 0, axis_index_groups=inner, tiled=True)

    sh_back, sh_dgu, sh_y = ffn(
        scalars, 0, 1, normed_two, normed_two_oth, cot_h, cot_o, shared_w, None, None,
        [grad_ready, backs[1], backs[3]],
    )
    sh_sum = sh_back[0].astype(f32) + yx(sh_back[1]).astype(f32)
    normed_full = halves(y, normed_two, normed_two_oth)
    shared_full = jnp.concatenate(
        [grad_of(normed_full, sh_dgu[0]), grad_of(cotangent, sh_y[0])], axis=1
    )
    shared_full = shared_full.astype(bf16) if small else shared_full
    shared_grad = lax.psum_scatter(
        shared_full,
        ("fsdp", "ctx"), scatter_dimension=0, tiled=True,
    ).astype(f32)

    keep_b, send_b, keep_o, send_o = call(
        unpack_body, [sds((2, ROWS, HALF), bf16)] * 4, us=0.0, name="unpack"
    )(scalars, ids, *backs, deps=[sh_sum])
    back_h = over_ctx(keep_b, send_b) + sh_sum[:, :HALF]
    scaled = back_h * gain_two_h[None, :]
    mean_two = both_halves(jnp.sum(scaled * normal_two, axis=1))[:, None] / D
    ffn_gain_part = jnp.sum(back_h * normal_two, axis=0)
    middle_grad = cot_h.astype(f32) + scale_two * (scaled - normal_two * mean_two)
    dz_own = middle_grad.astype(bf16)
    dz_oth = yx(dz_own)
    dq, dkv_keep, dkv_send = call(
        attn_back_body,
        [sds((ROWS, heads_width), bf16)] + [sds((2, ROWS, 2 * heads_width), bf16)] * 2,
        scratch=[
            pltpu.VMEM((4 * ROWS, 2 * heads_width), bf16),
            pltpu.VMEM((4 * ROWS, ROWS), f32),
            pltpu.VMEM((ROWS, heads_width), bf16),
            pltpu.VMEM((8, ROWS), f32),
            pltpu.VMEM((heads_width, ROWS), f32),
        ],
        us=0.0, name="attn_back",
    )(
        scalars, queries, *kvs, seg_col, seg_row, lse, attended, dz_own, dz_oth, out_w, cos, sin,
        deps=[shared_full],
    )
    layer_h = middle + over_ctx(keep_o, after(send_o, dz_oth)) + sh_sum[:, HALF:]
    dkv_near = cx(dkv_send, 1)
    kv_recv = cx((dkv_keep[1].astype(f32) + dkv_near[1].astype(f32)).astype(bf16), 2)
    dp, da_own, da_oth = call(
        proj_back_body,
        [sds((ROWS, 3 * heads_width), bf16), sds((ROWS, HALF), f32), sds((ROWS, HALF), bf16)],
        us=5.0, name="proj_back",
    )(scalars, dq, dkv_keep, dkv_near, kv_recv, first, cos, sin, deps=[grad_w, layer_h])
    dense_pairs = [(normed_one, dp), (halves(y, dz_own, dz_oth), attended)]
    if small:
        dense_keep, dense_send = grad_blocks(back_offs, rows_own, dense_pairs)
        dense_part = reduce_near(dense_keep, dense_send)
    else:
        dense_keep = dense_part = dp
    da_h = after(da_own, dense_keep) + yx(da_oth).astype(f32)
    tok_full = tokens.astype(f32)
    scale_one = lax.rsqrt(jnp.mean(tok_full * tok_full, axis=1, keepdims=True) + eps)
    normal_one = tok_h * scale_one
    scaled_one = da_h * gain_one_h[None, :]
    mean_one = both_halves(jnp.sum(scaled_one * normal_one, axis=1))[:, None] / D
    attn_gain_part = jnp.sum(after(da_h, mean_one) * normal_one, axis=0)
    tokens_grad_h = middle_grad + scale_one * (scaled_one - normal_one * mean_one)

    tokens_grad = whole_rows(tokens_grad_h.astype(bf16)).astype(f32)

    layer_out = whole_rows(after(layer_h, mean_one).astype(bf16))
    grad_w = after(grad_w, tokens_grad_h, dense_part)
    expert_gate_up_grad = grad_w[:, :2].astype(f32)
    expert_down_grad = grad_w[:, 2].astype(f32).transpose(0, 2, 1)
    if small:
        dense_grad = reduce_far(dense_part, bf16, None, tokens_grad_h)
    else:
        dense_grad = dense_reduce(dense_pairs)
    qkv_grad = dense_grad[:, : 3 * heads_width].reshape(rows_own, 3, heads_width).transpose(1, 0, 2)
    out_grad = dense_grad[:, 3 * heads_width :].T
    shared_gate_up_grad = jnp.stack(
        [shared_grad[:, :shared_hidden], shared_grad[:, shared_hidden : 2 * shared_hidden]]
    )
    shared_down_grad = shared_grad[:, 2 * shared_hidden :].T

    def placed(part):
        first = y == 0
        return jnp.concatenate([jnp.where(first, part, 0.0), jnp.where(first, 0.0, part)])

    tail = jnp.concatenate(
        [router_part, placed(attn_gain_part)[:, None], placed(ffn_gain_part)[:, None]], axis=1
    )
    if small:
        order = back_offs // rows_own
        blocks = tail.reshape(16, rows_own * (E + 2))[order].reshape(2, 2, 4, rows_own * (E + 2))
        tail = reduce_far(reduce_near(blocks[:, 0], blocks[:, 1]), f32)
        tail = tail.reshape(rows_own, E + 2)
    else:
        tail = lax.psum_scatter(tail, ("fsdp", "ctx"), scatter_dimension=0, tiled=True)
    tail = tail + yx(tail)
    return (
        layer_out,
        tokens_grad,
        tail[:, E],
        qkv_grad,
        out_grad,
        tail[:, E + 1],
        tail[:, :E],
        expert_gate_up_grad,
        expert_down_grad,
        shared_gate_up_grad,
        shared_down_grad,
    )


def solution(mesh):
    return jax.shard_map(
        per_device,
        mesh=mesh,
        in_specs=(
            P(("fsdp", "ctx"), None),
            P("fsdp", None),
            P(("fsdp", "ctx"), None),
            P(("fsdp", "ctx")),
            P(None, ("fsdp", "ctx"), "tp"),
            P("tp", ("fsdp", "ctx")),
            P(("fsdp", "ctx")),
            P(("fsdp", "ctx"), None),
            P("ctx", None, "fsdp", "tp"),
            P("ctx", "tp", "fsdp"),
            P(None, ("fsdp", "ctx"), "tp"),
            P("tp", ("fsdp", "ctx")),
            P(("fsdp", "ctx"), None),
        ),
        out_specs=(
            P(("fsdp", "ctx"), None),
            P(("fsdp", "ctx"), None),
            P(("fsdp", "ctx")),
            P(None, ("fsdp", "ctx"), "tp"),
            P("tp", ("fsdp", "ctx")),
            P(("fsdp", "ctx")),
            P(("fsdp", "ctx"), None),
            P("ctx", None, "fsdp", "tp"),
            P("ctx", "tp", "fsdp"),
            P(None, ("fsdp", "ctx"), "tp"),
            P("tp", ("fsdp", "ctx")),
        ),
        check_vma=False,
    )
```

```python
import functools

import jax
import jax.numpy as jnp
from jax import lax
from jax.experimental import pallas as pl
from jax.experimental.pallas import tpu as pltpu
from jax.sharding import PartitionSpec as P

D = 768
HALF = D // 2
HD = 64
E = 16
ROWS = 512
CAP = 128
NEG = -1e30
eps = 1e-06
bf16 = jnp.bfloat16
f32 = jnp.float32
VMEM_LIMIT = 56 * 1024 * 1024


def mm(a, b):
    return lax.dot_general(a, b, (((1,), (0,)), ((), ())), preferred_element_type=f32)


def mm_t(a, b):
    return lax.dot_general(a, b, (((1,), (1,)), ((), ())), preferred_element_type=f32)


def t_mm(a, b):
    return lax.dot_general(a, b, (((0,), (0,)), ((), ())), preferred_element_type=f32)


def sds(shape, dtype):
    return jax.ShapeDtypeStruct(shape, dtype)


SMEM = pl.BlockSpec(memory_space=pltpu.SMEM)
VM = pl.BlockSpec(memory_space=pltpu.VMEM)


def call(body, outs, scratch=(), us=1.0, name=None):
    def run(scalars, *args, deps=()):
        count = 1 + len(args)

        def inner(*refs):
            body(*refs[:count], *refs[count + len(deps) :])

        return pl.pallas_call(
            inner,
            out_shape=outs,
            in_specs=[SMEM] + [VM] * len(args) + [pl.BlockSpec(memory_space=pl.ANY)] * len(deps),
            out_specs=jax.tree.map(lambda _: VM, outs),
            scratch_shapes=list(scratch),
            compiler_params=pltpu.CompilerParams(vmem_limit_bytes=VMEM_LIMIT),
            cost_estimate=pl.CostEstimate(
                flops=int(us * 1.1e9), bytes_accessed=0, transcendentals=0
            ),
            name=name,
        )(scalars, *args, *deps)

    return run


def after(v, *deps):
    return lax.optimization_barrier((v,) + deps)[0]


def partner(v, lane):
    return jnp.where(lane % 64 < 32, pltpu.roll(v, 96, 1), pltpu.roll(v, 32, 1))


def lane_id(rows):
    return lax.broadcasted_iota(jnp.int32, (rows, 128), 1)


def qkv_body(sc, tok, gain, w, cos, sin, a_o, q_o, kv_o):
    x = tok[...].astype(f32)
    scale = lax.rsqrt(jnp.mean(x * x, axis=1, keepdims=True) + eps)
    a = (x * scale * gain[...]).astype(bf16)
    a_o[...] = a
    n = q_o.shape[1]
    lane = lane_id(ROWS)
    for g in range(3 * n // 128):
        v = mm(a, w[:, g * 128 : (g + 1) * 128])
        lo = g * 128
        if lo < n:
            r = v * cos[...] + partner(v, lane) * sin[...]
            q_o[:, lo : lo + 128] = (r.astype(bf16).astype(f32) * (HD**-0.5)).astype(bf16)
        elif lo < 2 * n:
            r = v * cos[...] + partner(v, lane) * sin[...]
            kv_o[:, lo - n : lo - n + 128] = r.astype(bf16)
        else:
            kv_o[:, lo - n : lo - n + 128] = v.astype(bf16)


def block_bias(c, kb, segc, segq):
    off = pl.multiple_of(kb * ROWS, ROWS)
    kpos = off + lax.broadcasted_iota(jnp.int32, (ROWS, ROWS), 0)
    qpos = c * ROWS + lax.broadcasted_iota(jnp.int32, (ROWS, ROWS), 1)
    ok = (segc[pl.ds(off, ROWS), :] == segq[...]) & (kpos <= qpos)
    return jnp.where(ok, 0.0, NEG)


def attn_body(sc, q, k0, k1, k2, k3, segc, segq, wo, o_o, zown_o, zoth_o, lse_o, kvs, bias, st, ot):
    c, y = sc[0], sc[1]
    nb = c + 1
    n = q.shape[1]
    for r, ref in enumerate((k0, k1, k2, k3)):
        kvs[pl.ds(pl.multiple_of((c ^ r) * ROWS, ROWS), ROWS), :] = ref[...]

    def bias_step(kb, carry):
        bias[pl.ds(pl.multiple_of(kb * ROWS, ROWS), ROWS), :] = block_bias(c, kb, segc, segq)
        return carry

    lax.fori_loop(0, nb, bias_step, 0)
    for h in range(n // HD):
        lo = h * HD
        qh = q[:, lo : lo + HD]

        def score_step(kb, m, lo=lo, qh=qh):
            rows = pl.ds(pl.multiple_of(kb * ROWS, ROWS), ROWS)
            s = mm_t(kvs[rows, lo : lo + HD], qh) + bias[rows, :]
            st[rows, :] = s
            return jnp.maximum(m, jnp.max(s, axis=0, keepdims=True))

        m = lax.fori_loop(0, nb, score_step, jnp.full((1, ROWS), NEG, f32))

        def value_step(kb, carry, lo=lo, m=m):
            total, acc = carry
            rows = pl.ds(pl.multiple_of(kb * ROWS, ROWS), ROWS)
            p = jnp.exp(st[rows, :] - m)
            total = total + jnp.sum(p, axis=0, keepdims=True)
            return total, acc + t_mm(kvs[rows, n + lo : n + lo + HD], p.astype(bf16))

        total, acc = lax.fori_loop(
            0, nb, value_step, (jnp.zeros((1, ROWS), f32), jnp.zeros((HD, ROWS), f32))
        )
        ot[lo : lo + HD, :] = acc / total
        lse_o[h : h + 1, :] = m + jnp.log(total)
    o = ot[...].T.astype(bf16)
    o_o[...] = o
    own = pl.ds(pl.multiple_of(y * HALF, HALF), HALF)
    oth = pl.ds(pl.multiple_of((1 - y) * HALF, HALF), HALF)
    zoth_o[...] = mm_t(o, wo[oth, :]).astype(bf16)
    zown_o[...] = mm_t(o, wo[own, :])


def attn_back_body(
    sc, q, k0, k1, k2, k3, segc, segq, lse, o, zown, zoth, wo, cos, sin, dq_o, keep_o, send_o,
    kvs, bias, do_s, delta, dqt,
):
    c, y = sc[0], sc[1]
    nb = c + 1
    n = q.shape[1]
    heads = n // HD
    for r, ref in enumerate((k0, k1, k2, k3)):
        kvs[pl.ds(pl.multiple_of((c ^ r) * ROWS, ROWS), ROWS), :] = ref[...]

    def bias_step(kb, carry):
        bias[pl.ds(pl.multiple_of(kb * ROWS, ROWS), ROWS), :] = block_bias(c, kb, segc, segq)
        return carry

    lax.fori_loop(0, nb, bias_step, 0)
    own = pl.ds(pl.multiple_of(y * HALF, HALF), HALF)
    oth = pl.ds(pl.multiple_of((1 - y) * HALF, HALF), HALF)
    do = (mm(zown[...], wo[own, :]) + mm(zoth[...], wo[oth, :])).astype(bf16)
    do_s[...] = do
    pick = (
        lax.broadcasted_iota(jnp.int32, (8, n), 1) // HD
        == lax.broadcasted_iota(jnp.int32, (8, n), 0)
    ).astype(f32)
    delta[...] = lax.dot_general(
        pick,
        do.astype(f32) * o[...].astype(f32),
        (((1,), (1,)), ((), ())),
        precision=lax.Precision.HIGHEST,
        preferred_element_type=f32,
    )

    def put(kb, cols, value):
        at = kb ^ c

        @pl.when(at % 2 == 0)
        def _():
            keep_o[at // 2, :, cols] = value

        @pl.when(at % 2 == 1)
        def _():
            send_o[at // 2, :, cols] = value

    def zero_step(kb, carry):
        put(kb, slice(None), jnp.zeros((ROWS, 2 * n), bf16))
        return carry

    lax.fori_loop(nb, 4, zero_step, 0)
    for pair in range(heads // 2):
        at = pair * 128

        def step(kb, carry, at=at, pair=pair):
            rows = pl.ds(pl.multiple_of(kb * ROWS, ROWS), ROWS)
            dks, dvs, dqs = [], [], []
            for i in range(2):
                lo = at + i * HD
                h = 2 * pair + i
                kh = kvs[rows, lo : lo + HD]
                vh = kvs[rows, n + lo : n + lo + HD]
                qh = q[:, lo : lo + HD]
                dh = do_s[:, lo : lo + HD]
                p = jnp.exp(mm_t(kh, qh) + bias[rows, :] - lse[h : h + 1, :])
                ds = (p * (mm_t(vh, dh) - delta[h : h + 1, :])).astype(bf16)
                dvs.append(mm(p.astype(bf16), dh))
                dks.append(mm(ds, qh))
                dqs.append(carry[i] + t_mm(kh, ds))
            put(kb, slice(at, at + 128), jnp.concatenate(dks, axis=1).astype(bf16))
            put(kb, slice(n + at, n + at + 128), jnp.concatenate(dvs, axis=1).astype(bf16))
            return tuple(dqs)

        zero = jnp.zeros((HD, ROWS), f32)
        dqs = lax.fori_loop(0, nb, step, (zero, zero))
        dqt[at : at + HD, :] = dqs[0]
        dqt[at + HD : at + 128, :] = dqs[1]
    lane = lane_id(ROWS)
    for g in range(n // 128):
        v = dqt[g * 128 : (g + 1) * 128, :].T * (HD**-0.5)
        dq_o[:, g * 128 : (g + 1) * 128] = (v * cos[...] - partner(v, lane) * sin[...]).astype(bf16)


def proj_back_body(sc, dq, keep, near, recv, w, cos, sin, dp_o, own_o, oth_o):
    y = sc[1]
    n = dq.shape[1]
    lane = lane_id(ROWS)
    dp_o[:, :n] = dq[...]
    for g in range(2 * n // 128):
        cols = slice(g * 128, (g + 1) * 128)
        v = keep[0, :, cols].astype(f32) + near[0, :, cols].astype(f32) + recv[:, cols].astype(f32)
        if g < n // 128:
            v = v * cos[...] - partner(v, lane) * sin[...]
        dp_o[:, n + g * 128 : n + (g + 1) * 128] = v.astype(bf16)
    own = pl.ds(pl.multiple_of(y * HALF, HALF), HALF)
    oth = pl.ds(pl.multiple_of((1 - y) * HALF, HALF), HALF)
    oth_o[...] = mm_t(dp_o[...], w[oth, : 3 * n]).astype(bf16)
    own_o[...] = mm_t(dp_o[...], w[own, : 3 * n])


def slots_onehot(ids, r):
    i = lax.broadcasted_iota(jnp.int32, (4 * CAP, ROWS), 0)
    hit = (i == ids[2 * r : 2 * r + 1, :]) | (i == ids[2 * r + 1 : 2 * r + 2, :])
    return jnp.where(hit, 1.0, 0.0).astype(bf16)


def pack_body(sc, ids, b0, b1, b2, b3, p0, p1, p2, p3):
    for r, ref in enumerate((b0, b1, b2, b3)):
        rows = mm(slots_onehot(ids, r), ref[...]).astype(bf16)
        for s, out in enumerate((p0, p1, p2, p3)):
            out[r * CAP : (r + 1) * CAP, :] = rows[s * CAP : (s + 1) * CAP, :]


def unpack_body(sc, ids, p0, p1, p2, p3, keep_b, send_b, keep_o, send_o):
    for r in (1, 3, 0, 2):
        rows = jnp.concatenate(
            [p[r * CAP : (r + 1) * CAP, :] for p in (p0, p1, p2, p3)], axis=0
        )
        tok = t_mm(slots_onehot(ids, r), rows).astype(bf16)
        for at, pair in ((0, (keep_b, send_b)), (HALF, (keep_o, send_o))):
            pair[r % 2][r // 2] = tok[:, at : at + HALF]


def halves(y, a, b):
    first = y == 0
    return jnp.concatenate([jnp.where(first, a, b), jnp.where(first, b, a)], axis=1)


def ffn_body(routed, sc, xa, xb, wa, wb, weights, rt, *refs):
    if routed:
        refs = refs[len(refs) - 8 :]
        back_o, rg_o, dgu_o, y_o, x_o, de_o, acc_o, acc_b = refs
    else:
        back_o, dgu_o, y_o, acc_o, acc_b = refs[len(refs) - 5 :]
    y, e = sc[1], sc[2]
    x = halves(y, xa[...], xb[...])
    w = halves(y, wa[...], wb[...])
    hidden = weights.shape[3]
    if routed:
        lane = lane_id(ROWS)
        logits = jnp.where(lane < E, mm(x, rt[...]), NEG)
        ex = jnp.exp(logits - jnp.max(logits, axis=1, keepdims=True))
        probs = ex / jnp.sum(ex, axis=1, keepdims=True)
        gate = jnp.sum(jnp.where(lane == e, probs, 0.0), axis=1, keepdims=True)
        x_o[0] = x
        de_o[0] = (w.astype(f32) * gate).astype(bf16)
    acc_o[...] = jnp.zeros_like(acc_o)
    acc_b[...] = jnp.zeros_like(acc_b)
    tile = 256

    def columns(which, lo):
        cols = pl.ds(pl.multiple_of(lo, tile), tile)
        return jnp.concatenate(
            [weights[j, which, :, cols] for j in range(weights.shape[0])], axis=0
        )

    def step(j, dots):
        lo = pl.multiple_of(j * tile, tile)
        hi = pl.multiple_of(hidden + j * tile, tile)
        g = mm(x, columns(0, lo))
        u = mm(x, columns(1, lo))
        h = mm(w, columns(2, lo))
        sg = 1.0 / (1.0 + jnp.exp(-g))
        act = g * sg
        yv = (act * u).astype(bf16)
        if routed:
            dots = dots + jnp.sum(yv.astype(f32) * h, axis=1, keepdims=True)
            h = h * gate
        dg = (h * u * (sg + act * (1.0 - sg))).astype(bf16)
        du = (h * act).astype(bf16)
        y_o[0, :, pl.ds(lo, tile)] = yv
        dgu_o[0, :, pl.ds(lo, tile)] = dg
        dgu_o[0, :, pl.ds(hi, tile)] = du
        acc_o[...] += mm_t(yv, columns(2, lo))
        acc_b[...] += mm_t(dg, columns(0, lo)) + mm_t(du, columns(1, lo))
        return dots

    dots = lax.fori_loop(0, hidden // tile, step, jnp.zeros((ROWS, 1), f32))
    if routed:
        coef = (dots * gate) * (jnp.where(lane == e, 1.0, 0.0) - probs)
        coef = jnp.where(lane < E, coef, 0.0).astype(bf16)
        acc_b[...] += mm_t(coef, rt[...])
        rg_o[...] = t_mm(x, coef)
    for i, at in enumerate((y, 1 - y)):
        cols = pl.ds(pl.multiple_of(at * HALF, HALF), HALF)
        out = acc_o[:, cols]
        if routed:
            out = out * gate
        back_o[i, :, :HALF] = acc_b[:, cols].astype(bf16)
        back_o[i, :, HALF:] = out.astype(bf16)


def ffn(scalars, s, groups, xa, xb, wa, wb, weights, rt, prev, deps=()):
    routed = rt is not None
    hidden = weights.shape[3]
    full = lambda shape: pl.BlockSpec(shape, lambda i, n=len(shape): (0,) * n)
    part = lambda width: pl.BlockSpec((1, ROWS, width), lambda i: (s, 0, 0))
    two = (2, ROWS, D)
    outs = [sds(two, bf16)]
    out_specs = [full(two)]
    if routed:
        outs.append(sds((D, 128), f32))
        out_specs.append(full((D, 128)))
    widths = [2 * hidden, hidden] + ([D, D] if routed else [])
    base = len(outs)
    for width in widths:
        outs.append(sds((groups, ROWS, width), bf16))
        out_specs.append(part(width))
    args = [xa, xb, wa, wb, weights] + ([rt] if routed else [])
    in_specs = [SMEM] + [full(a.shape) for a in args]
    aliases = {}
    if not routed:
        args.append(scalars)
        in_specs.append(SMEM)
    for arr in deps:
        args.append(arr)
        in_specs.append(pl.BlockSpec(memory_space=pl.ANY))
    if prev is not None:
        for i, arr in enumerate(prev):
            aliases[1 + len(args)] = base + i
            args.append(arr)
            in_specs.append(pl.BlockSpec(memory_space=pl.ANY))
    return pl.pallas_call(
        functools.partial(ffn_body, routed),
        grid=(1,),
        out_shape=outs,
        in_specs=in_specs,
        out_specs=out_specs,
        scratch_shapes=[pltpu.VMEM((ROWS, D), f32), pltpu.VMEM((ROWS, D), f32)],
        input_output_aliases=aliases,
        compiler_params=pltpu.CompilerParams(vmem_limit_bytes=VMEM_LIMIT),
        cost_estimate=pl.CostEstimate(flops=int(16e9) if routed else 0, bytes_accessed=0, transcendentals=0),
        name="expert_ffn" if routed else "shared_ffn",
    )(scalars, *args)


def grad_blocks(offs, rows, pairs):
    tile = 384
    total = sum(b.shape[1] for _, b in pairs)

    def body(sc, *refs):
        keep, send, acc = refs[-3:]
        lo = 0
        for i in range(len(pairs)):
            a, b = refs[2 * i], refs[2 * i + 1]
            turned = a[...].T
            for j in range(0, b.shape[1], tile):
                width = min(tile, b.shape[1] - j)
                acc[:, :width] = mm(turned, b[:, j : j + width])
                for k in range(16):
                    at = pl.ds(pl.multiple_of(sc[k], 16), rows)
                    out = send if (k // 4) % 2 else keep
                    out[k // 8, k % 4, :, lo : lo + width] = acc[at, :width].astype(bf16)
                lo += width

    shape = sds((2, 4, rows, total), bf16)
    args = [m for pair in pairs for m in pair]
    return call(body, [shape, shape], scratch=[pltpu.VMEM((D, tile), f32)], us=3.0, name="grad_blocks")(
        offs, *args
    )


def per_device(
    tokens,
    segments,
    experts,
    attn_gain,
    qkv_proj,
    out_proj,
    ffn_gain,
    router_proj,
    expert_gate_up,
    expert_down,
    shared_gate_up,
    shared_down,
    cotangent,
):
    F, C = lax.axis_size("fsdp"), lax.axis_size("ctx")
    f, c, y = lax.axis_index("fsdp"), lax.axis_index("ctx"), lax.axis_index("tp")
    EL = expert_gate_up.shape[0]
    small = F == EL and C == 4
    heads_width = qkv_proj.shape[2]
    hidden = expert_down.shape[1]
    shared_hidden = shared_down.shape[0]
    zi = f % EL
    i32 = jnp.int32

    def yx(v):
        return lax.ppermute(v, "tp", [(0, 1), (1, 0)])

    def cx(v, flip):
        return lax.ppermute(v, "ctx", [(i, i ^ flip) for i in range(C)])

    def zs(v, s):
        return lax.ppermute(
            v, "fsdp", [(i, i // EL * EL + (i % EL + s) % EL) for i in range(F)]
        )

    scalars = jnp.stack([c, y, EL * c + zi]).astype(i32)
    rows_own = D // (F * C)
    rc = jnp.arange(4, dtype=i32)
    if small:
        dense_offs = (
            (((f - rc)[None, :] % 4) * 4 + (c ^ rc)[:, None]).reshape(16) * rows_own
        ).astype(i32)
        back_offs = (
            (((f + rc)[None, :] % 4) * 4 + (c ^ rc)[:, None]).reshape(16) * rows_own
        ).astype(i32)

    def gathered(shard, axis=0):
        return lax.all_gather(shard, ("fsdp", "ctx"), axis=axis, tiled=True)

    def reduce_near(keep, send):
        kind = keep.dtype
        near = cx(send, 1)
        far = cx((keep[1].astype(f32) + near[1].astype(f32)).astype(kind), 2)
        return keep[0].astype(f32) + near[0].astype(f32) + far.astype(f32)

    def reduce_far(part, kind, z_after=None, sum_after=None):
        pieces = [part[s].astype(kind) for s in (1, 2, 3)]
        if z_after is not None:
            pieces = [after(piece, z_after) for piece in pieces]
        total = part[0] if sum_after is None else after(part[0], sum_after)
        for s, piece in zip((1, 2, 3), pieces):
            total = total + zs(piece, s).astype(f32)
        return total

    def grad_of(a, b):
        return lax.dot_general(a, b, (((0,), (0,)), ((), ())), preferred_element_type=f32)

    def dense_reduce(pairs):
        full = jnp.concatenate([grad_of(a, b) for a, b in pairs], axis=1)
        return lax.psum_scatter(full, ("fsdp", "ctx"), scatter_dimension=0, tiled=True)

    def half(v, which):
        return lax.dynamic_slice_in_dim(v, which * HALF, HALF, v.ndim - 1)

    qkv_shard = jnp.concatenate(
        [
            qkv_proj.transpose(1, 0, 2).reshape(rows_own, 3 * heads_width),
            router_proj,
            attn_gain[:, None],
            ffn_gain[:, None],
            jnp.zeros((rows_own, 128 - E - 2), bf16),
        ],
        axis=1,
    )
    first = gathered(jnp.concatenate([qkv_shard, out_proj.T], axis=1))
    extra = first[:, 3 * heads_width : 3 * heads_width + 128]
    out_w = first[:, 3 * heads_width + 128 :]
    gains = extra[:, E : E + 2].astype(f32)
    gain_one, gain_two = gains[:, 0], gains[:, 1]
    gain_two_h = half(gain_two, y)
    gain_one_h = half(gain_one, y)
    shared_shard = jnp.concatenate([shared_gate_up, shared_down.T[None]])
    expert_local = jnp.concatenate(
        [expert_gate_up, expert_down.transpose(0, 2, 1)[:, None]], axis=1
    )
    if small:
        expert_w = None
    else:
        inner = [[g * EL + i for i in range(EL)] for g in range(F // EL)]
        outer = [[g * EL + i for g in range(F // EL)] for i in range(EL)]
        mine = lax.all_to_all(
            expert_local, "fsdp", 0, 0, axis_index_groups=inner, tiled=True
        )
        mine = lax.all_gather(mine, "fsdp", axis=0, axis_index_groups=outer, tiled=True)
        expert_w = mine.transpose(1, 0, 2, 3).reshape(1, 3, D, hidden)

    lanes = jnp.arange(E, dtype=i32)[None, :]
    named = [(experts[:, k : k + 1] == lanes) for k in range(2)]
    both = (named[0] | named[1]).astype(bf16)
    before = (jnp.arange(ROWS)[:, None] > jnp.arange(ROWS)[None, :]).astype(bf16)
    counts = jnp.dot(before, both, preferred_element_type=f32)
    code = jnp.stack(
        [
            experts[:, k] * CAP + jnp.sum(jnp.where(named[k], counts, 0.0), axis=1).astype(i32)
            for k in range(2)
        ]
    )
    code_two = jnp.stack([code, cx(code, 2)])
    code_core = cx(code_two, 1)
    codes = jnp.concatenate([code_two[0], code_core[0], code_two[1], code_core[1]], axis=0)
    which, rank = codes // CAP, codes % CAP
    ids = jnp.where(which // EL == c, ((which - zi) % EL) * CAP + rank, -1).astype(i32)

    def dispatch(own, dep=None):
        far = cx(own, 2)
        near = cx(own, 1)
        both_far = cx(far, 1)
        packs = call(
            pack_body, [sds((4 * CAP, HALF), bf16)] * 4, name="pack"
        )(scalars, ids if dep is None else after(ids, *dep), own, near, far, both_far)
        return [packs[0]] + [zs(packs[s], s) for s in (1, 2, 3)]

    def sum_pieces(pieces, dep=None):
        total = pieces[0]
        if dep is not None:
            total = after(total, dep)
        for piece in pieces[1:]:
            total = total + piece.astype(f32)
        return total

    def over_tp(two):
        return (two[0].astype(f32) + yx(two[1]).astype(f32)).astype(bf16)

    def home(s, total):
        return total if s == 0 else zs(total, EL - s)

    def over_ctx(keep, send):
        got = cx(send, 1)
        far = (keep[1].astype(f32) + got[1].astype(f32)).astype(bf16)
        return keep[0].astype(f32) + got[0].astype(f32) + cx(far, 2).astype(f32)

    cot_h, cot_o = half(cotangent, y), half(cotangent, 1 - y)
    cot_rows = dispatch(cot_h)
    cot_pairs = [(rows, yx(rows)) for rows in cot_rows]

    positions = (c * ROWS + jnp.arange(ROWS, dtype=i32)).astype(f32)
    table = jnp.arange(128, dtype=i32)
    frequency = 10000.0 ** (-(table % 32).astype(f32) / 32)
    angles = positions[:, None] * frequency[None, :]
    cos = jnp.cos(angles)
    sin = jnp.sin(angles) * jnp.where(table % 64 < 32, -1.0, 1.0)[None, :]
    normed_one, queries, kv = call(
        qkv_body,
        [sds((ROWS, D), bf16), sds((ROWS, heads_width), bf16), sds((ROWS, 2 * heads_width), bf16)],
        us=5.0, name="qkv",
    )(
        scalars, tokens, gain_one[None, :], first, cos, sin,
        deps=[cot_pairs[0][1], *cot_rows[1:], expert_local],
    )
    kv_far = cx(kv, 2)
    kv_near = cx(kv, 1)
    kv_both = cx(kv_far, 1)
    kvs = (kv, kv_near, kv_far, kv_both)
    if small:
        expert_w = lax.all_to_all(
            after(expert_local, kv_near), "fsdp", 0, 0, tiled=True
        )
    before_attn = []
    seq_ids = segments[0]
    seg_col = seq_ids[:, None]
    seg_row = lax.dynamic_slice_in_dim(seq_ids, c * ROWS, ROWS, 0)[None, :]
    attended, z_own, z_oth, lse = call(
        attn_body,
        [
            sds((ROWS, heads_width), bf16),
            sds((ROWS, HALF), f32),
            sds((ROWS, HALF), bf16),
            sds((8, ROWS), f32),
        ],
        scratch=[
            pltpu.VMEM((4 * ROWS, 2 * heads_width), bf16),
            pltpu.VMEM((4 * ROWS, ROWS), f32),
            pltpu.VMEM((4 * ROWS, ROWS), f32),
            pltpu.VMEM((heads_width, ROWS), f32),
        ],
        us=17.0, name="attn",
    )(scalars, queries, *kvs, seg_col, seg_row, out_w, deps=before_attn)
    tok_h = half(tokens, y).astype(f32)
    middle = tok_h + z_own + yx(z_oth).astype(f32)

    def whole_rows(own):
        return halves(y, own, yx(own))

    def both_halves(sums):
        return sums + yx(sums)

    square = both_halves(jnp.sum(middle * middle, axis=1))
    scale_two = lax.rsqrt(square / D + eps)[:, None]
    normal_two = middle * scale_two
    normed_two = (normal_two * gain_two_h[None, :]).astype(bf16)

    normed_two_oth = yx(normed_two)
    rows_in = dispatch(normed_two, [normed_two_oth])
    shared_w = gathered(after(shared_shard, rows_in[3]), 1)[None]
    saved, backs, sums, router_part = None, [None] * 4, [], 0.0
    tied = [rows_in[0]] + [after(rows, *[pair[1] for pair in cot_pairs]) for rows in rows_in[1:]]
    pairs = [(rows, yx(rows)) for rows in tied]
    for i, s in enumerate((2, 1, 3, 0)):
        deps = [rows_in[1:], [pairs[3][1], pairs[0][1]], sums[:1], sums[1:2]][i]
        res = ffn(scalars, s, 4, *pairs[s], *cot_pairs[s], expert_w, extra, saved, deps)
        sums.append(over_tp(res[0]))
        backs[s] = home(s, sums[i])
        router_part = router_part + res[1][:, :E]
        saved = res[2:]
    ex_dgu, ex_y, ex_x, ex_de = [v.reshape(4 * ROWS, -1) for v in saved]
    ex_x = after(ex_x, backs[2])

    grad_w = [
        lax.dot_general(a, b, (((0,), (0,)), ((), ())), preferred_element_type=f32)
        for a, b in ((ex_x, ex_dgu[:, :hidden]), (ex_x, ex_dgu[:, hidden:]), (ex_de, ex_y))
    ]
    if small:
        grad_w = [g.astype(bf16).reshape(4, D // 4, hidden) for g in grad_w]
        grad_w = grad_ready = jnp.stack(grad_w, axis=1)
        grad_w = lax.all_to_all(
            grad_w, "fsdp", 0, 0, tiled=True
        )
    else:
        grad_ready = saved[0]
        grad_w = jnp.stack([g.reshape(F, D // F, hidden) for g in grad_w], axis=1)
        grad_w = lax.psum_scatter(
            grad_w, "fsdp", scatter_dimension=0, axis_index_groups=outer, tiled=True
        )
        grad_w = lax.all_to_all(grad_w, "fsdp", 0, 0, axis_index_groups=inner, tiled=True)

    sh_back, sh_dgu, sh_y = ffn(
        scalars, 0, 1, normed_two, normed_two_oth, cot_h, cot_o, shared_w, None, None,
        [grad_ready, backs[1], backs[3]],
    )
    sh_sum = sh_back[0].astype(f32) + yx(sh_back[1]).astype(f32)
    normed_full = halves(y, normed_two, normed_two_oth)
    shared_full = jnp.concatenate(
        [grad_of(normed_full, sh_dgu[0]), grad_of(cotangent, sh_y[0])], axis=1
    )
    shared_full = shared_full.astype(bf16) if small else shared_full
    shared_grad = lax.psum_scatter(
        shared_full,
        ("fsdp", "ctx"), scatter_dimension=0, tiled=True,
    ).astype(f32)

    keep_b, send_b, keep_o, send_o = call(
        unpack_body, [sds((2, ROWS, HALF), bf16)] * 4, us=0.0, name="unpack"
    )(scalars, ids, *backs, deps=[sh_sum])
    back_h = over_ctx(keep_b, send_b) + sh_sum[:, :HALF]
    scaled = back_h * gain_two_h[None, :]
    mean_two = both_halves(jnp.sum(scaled * normal_two, axis=1))[:, None] / D
    ffn_gain_part = jnp.sum(back_h * normal_two, axis=0)
    middle_grad = cot_h.astype(f32) + scale_two * (scaled - normal_two * mean_two)
    dz_own = middle_grad.astype(bf16)
    dz_oth = yx(dz_own)
    dq, dkv_keep, dkv_send = call(
        attn_back_body,
        [sds((ROWS, heads_width), bf16)] + [sds((2, ROWS, 2 * heads_width), bf16)] * 2,
        scratch=[
            pltpu.VMEM((4 * ROWS, 2 * heads_width), bf16),
            pltpu.VMEM((4 * ROWS, ROWS), f32),
            pltpu.VMEM((ROWS, heads_width), bf16),
            pltpu.VMEM((8, ROWS), f32),
            pltpu.VMEM((heads_width, ROWS), f32),
        ],
        us=0.0, name="attn_back",
    )(
        scalars, queries, *kvs, seg_col, seg_row, lse, attended, dz_own, dz_oth, out_w, cos, sin,
        deps=[shared_full],
    )
    layer_h = middle + over_ctx(keep_o, after(send_o, dz_oth)) + sh_sum[:, HALF:]
    dkv_near = cx(dkv_send, 1)
    kv_recv = cx((dkv_keep[1].astype(f32) + dkv_near[1].astype(f32)).astype(bf16), 2)
    dp, da_own, da_oth = call(
        proj_back_body,
        [sds((ROWS, 3 * heads_width), bf16), sds((ROWS, HALF), f32), sds((ROWS, HALF), bf16)],
        us=5.0, name="proj_back",
    )(scalars, dq, dkv_keep, dkv_near, kv_recv, first, cos, sin, deps=[grad_w, layer_h])
    dense_pairs = [(normed_one, dp), (halves(y, dz_own, dz_oth), attended)]
    if small:
        dense_keep, dense_send = grad_blocks(back_offs, rows_own, dense_pairs)
        dense_part = reduce_near(dense_keep, dense_send)
    else:
        dense_keep = dense_part = dp
    da_h = after(da_own, dense_keep) + yx(da_oth).astype(f32)
    tok_full = tokens.astype(f32)
    scale_one = lax.rsqrt(jnp.mean(tok_full * tok_full, axis=1, keepdims=True) + eps)
    normal_one = tok_h * scale_one
    scaled_one = da_h * gain_one_h[None, :]
    mean_one = both_halves(jnp.sum(scaled_one * normal_one, axis=1))[:, None] / D
    attn_gain_part = jnp.sum(da_h * normal_one, axis=0)
    tokens_grad_h = middle_grad + scale_one * (scaled_one - normal_one * mean_one)

    tokens_grad = whole_rows(tokens_grad_h.astype(bf16)).astype(f32)

    layer_out = whole_rows(after(layer_h, tokens_grad_h).astype(bf16))
    grad_w = after(grad_w, tokens_grad_h)
    expert_gate_up_grad = grad_w[:, :2].astype(f32)
    expert_down_grad = grad_w[:, 2].astype(f32).transpose(0, 2, 1)
    if small:
        dense_grad = reduce_far(dense_part, bf16)
    else:
        dense_grad = dense_reduce(dense_pairs)
    qkv_grad = dense_grad[:, : 3 * heads_width].reshape(rows_own, 3, heads_width).transpose(1, 0, 2)
    out_grad = dense_grad[:, 3 * heads_width :].T
    shared_gate_up_grad = jnp.stack(
        [shared_grad[:, :shared_hidden], shared_grad[:, shared_hidden : 2 * shared_hidden]]
    )
    shared_down_grad = shared_grad[:, 2 * shared_hidden :].T

    def placed(part):
        first = y == 0
        return jnp.concatenate([jnp.where(first, part, 0.0), jnp.where(first, 0.0, part)])

    tail = jnp.concatenate(
        [router_part, placed(attn_gain_part)[:, None], placed(ffn_gain_part)[:, None]], axis=1
    )
    tail = after(tail, dense_part).reshape(F * C, rows_own * (E + 2))
    tail = jnp.sum(lax.all_to_all(tail, ("fsdp", "ctx"), 0, 0, tiled=True), axis=0)
    tail = after(tail, dense_grad, expert_gate_up_grad, expert_down_grad)
    tail = tail.reshape(rows_own, E + 2)
    tail = tail + yx(tail)
    return (
        layer_out,
        tokens_grad,
        tail[:, E],
        qkv_grad,
        out_grad,
        tail[:, E + 1],
        tail[:, :E],
        expert_gate_up_grad,
        expert_down_grad,
        shared_gate_up_grad,
        shared_down_grad,
    )


def solution(mesh):
    return jax.shard_map(
        per_device,
        mesh=mesh,
        in_specs=(
            P(("fsdp", "ctx"), None),
            P("fsdp", None),
            P(("fsdp", "ctx"), None),
            P(("fsdp", "ctx")),
            P(None, ("fsdp", "ctx"), "tp"),
            P("tp", ("fsdp", "ctx")),
            P(("fsdp", "ctx")),
            P(("fsdp", "ctx"), None),
            P("ctx", None, "fsdp", "tp"),
            P("ctx", "tp", "fsdp"),
            P(None, ("fsdp", "ctx"), "tp"),
            P("tp", ("fsdp", "ctx")),
            P(("fsdp", "ctx"), None),
        ),
        out_specs=(
            P(("fsdp", "ctx"), None),
            P(("fsdp", "ctx"), None),
            P(("fsdp", "ctx")),
            P(None, ("fsdp", "ctx"), "tp"),
            P("tp", ("fsdp", "ctx")),
            P(("fsdp", "ctx")),
            P(("fsdp", "ctx"), None),
            P("ctx", None, "fsdp", "tp"),
            P("ctx", "tp", "fsdp"),
            P(None, ("fsdp", "ctx"), "tp"),
            P("tp", ("fsdp", "ctx")),
        ),
        check_vma=False,
    )
```

```python
import functools

import jax
import jax.numpy as jnp
from jax import lax
from jax.experimental import pallas as pl
from jax.experimental.pallas import tpu as pltpu
from jax.sharding import PartitionSpec as P

D = 768
HALF = D // 2
HD = 64
E = 16
ROWS = 512
CAP = 128
NEG = -1e30
eps = 1e-06
bf16 = jnp.bfloat16
f32 = jnp.float32
VMEM_LIMIT = 56 * 1024 * 1024


def mm(a, b):
    return lax.dot_general(a, b, (((1,), (0,)), ((), ())), preferred_element_type=f32)


def mm_t(a, b):
    return lax.dot_general(a, b, (((1,), (1,)), ((), ())), preferred_element_type=f32)


def t_mm(a, b):
    return lax.dot_general(a, b, (((0,), (0,)), ((), ())), preferred_element_type=f32)


def sds(shape, dtype):
    return jax.ShapeDtypeStruct(shape, dtype)


SMEM = pl.BlockSpec(memory_space=pltpu.SMEM)
VM = pl.BlockSpec(memory_space=pltpu.VMEM)


def call(body, outs, scratch=(), us=1.0, name=None):
    def run(scalars, *args, deps=()):
        count = 1 + len(args)

        def inner(*refs):
            body(*refs[:count], *refs[count + len(deps) :])

        return pl.pallas_call(
            inner,
            out_shape=outs,
            in_specs=[SMEM] + [VM] * len(args) + [pl.BlockSpec(memory_space=pl.ANY)] * len(deps),
            out_specs=jax.tree.map(lambda _: VM, outs),
            scratch_shapes=list(scratch),
            compiler_params=pltpu.CompilerParams(vmem_limit_bytes=VMEM_LIMIT),
            cost_estimate=pl.CostEstimate(
                flops=int(us * 1.1e9), bytes_accessed=0, transcendentals=0
            ),
            name=name,
        )(scalars, *args, *deps)

    return run


def after(v, *deps):
    return lax.optimization_barrier((v,) + deps)[0]


def partner(v, lane):
    return jnp.where(lane % 64 < 32, pltpu.roll(v, 96, 1), pltpu.roll(v, 32, 1))


def lane_id(rows):
    return lax.broadcasted_iota(jnp.int32, (rows, 128), 1)


def qkv_body(sc, tok, gain, w, cos, sin, a_o, q_o, kv_o):
    x = tok[...].astype(f32)
    scale = lax.rsqrt(jnp.mean(x * x, axis=1, keepdims=True) + eps)
    a = (x * scale * gain[...]).astype(bf16)
    a_o[...] = a
    n = q_o.shape[1]
    lane = lane_id(ROWS)
    for g in range(3 * n // 128):
        v = mm(a, w[:, g * 128 : (g + 1) * 128])
        lo = g * 128
        if lo < n:
            r = v * cos[...] + partner(v, lane) * sin[...]
            q_o[:, lo : lo + 128] = (r.astype(bf16).astype(f32) * (HD**-0.5)).astype(bf16)
        elif lo < 2 * n:
            r = v * cos[...] + partner(v, lane) * sin[...]
            kv_o[:, lo - n : lo - n + 128] = r.astype(bf16)
        else:
            kv_o[:, lo - n : lo - n + 128] = v.astype(bf16)


def block_bias(c, kb, segc, segq):
    off = pl.multiple_of(kb * ROWS, ROWS)
    kpos = off + lax.broadcasted_iota(jnp.int32, (ROWS, ROWS), 0)
    qpos = c * ROWS + lax.broadcasted_iota(jnp.int32, (ROWS, ROWS), 1)
    ok = (segc[pl.ds(off, ROWS), :] == segq[...]) & (kpos <= qpos)
    return jnp.where(ok, 0.0, NEG)


def attn_body(sc, q, k0, k1, k2, k3, segc, segq, wo, o_o, zown_o, zoth_o, lse_o, kvs, bias, st, ot):
    c, y = sc[0], sc[1]
    nb = c + 1
    n = q.shape[1]
    for r, ref in enumerate((k0, k1, k2, k3)):
        kvs[pl.ds(pl.multiple_of((c ^ r) * ROWS, ROWS), ROWS), :] = ref[...]

    def bias_step(kb, carry):
        bias[pl.ds(pl.multiple_of(kb * ROWS, ROWS), ROWS), :] = block_bias(c, kb, segc, segq)
        return carry

    lax.fori_loop(0, nb, bias_step, 0)
    for h in range(n // HD):
        lo = h * HD
        qh = q[:, lo : lo + HD]

        def score_step(kb, m, lo=lo, qh=qh):
            rows = pl.ds(pl.multiple_of(kb * ROWS, ROWS), ROWS)
            s = mm_t(kvs[rows, lo : lo + HD], qh) + bias[rows, :]
            st[rows, :] = s
            return jnp.maximum(m, jnp.max(s, axis=0, keepdims=True))

        m = lax.fori_loop(0, nb, score_step, jnp.full((1, ROWS), NEG, f32))

        def value_step(kb, carry, lo=lo, m=m):
            total, acc = carry
            rows = pl.ds(pl.multiple_of(kb * ROWS, ROWS), ROWS)
            p = jnp.exp(st[rows, :] - m)
            total = total + jnp.sum(p, axis=0, keepdims=True)
            return total, acc + t_mm(kvs[rows, n + lo : n + lo + HD], p.astype(bf16))

        total, acc = lax.fori_loop(
            0, nb, value_step, (jnp.zeros((1, ROWS), f32), jnp.zeros((HD, ROWS), f32))
        )
        ot[lo : lo + HD, :] = acc / total
        lse_o[h : h + 1, :] = m + jnp.log(total)
    o = ot[...].T.astype(bf16)
    o_o[...] = o
    own = pl.ds(pl.multiple_of(y * HALF, HALF), HALF)
    oth = pl.ds(pl.multiple_of((1 - y) * HALF, HALF), HALF)
    zoth_o[...] = mm_t(o, wo[oth, :]).astype(bf16)
    zown_o[...] = mm_t(o, wo[own, :])


def attn_back_body(
    sc, q, k0, k1, k2, k3, segc, segq, lse, o, zown, zoth, wo, cos, sin, dq_o, keep_o, send_o,
    kvs, bias, do_s, delta, dqt,
):
    c, y = sc[0], sc[1]
    nb = c + 1
    n = q.shape[1]
    heads = n // HD
    for r, ref in enumerate((k0, k1, k2, k3)):
        kvs[pl.ds(pl.multiple_of((c ^ r) * ROWS, ROWS), ROWS), :] = ref[...]

    def bias_step(kb, carry):
        bias[pl.ds(pl.multiple_of(kb * ROWS, ROWS), ROWS), :] = block_bias(c, kb, segc, segq)
        return carry

    lax.fori_loop(0, nb, bias_step, 0)
    own = pl.ds(pl.multiple_of(y * HALF, HALF), HALF)
    oth = pl.ds(pl.multiple_of((1 - y) * HALF, HALF), HALF)
    do = (mm(zown[...], wo[own, :]) + mm(zoth[...], wo[oth, :])).astype(bf16)
    do_s[...] = do
    pick = (
        lax.broadcasted_iota(jnp.int32, (8, n), 1) // HD
        == lax.broadcasted_iota(jnp.int32, (8, n), 0)
    ).astype(f32)
    delta[...] = lax.dot_general(
        pick,
        do.astype(f32) * o[...].astype(f32),
        (((1,), (1,)), ((), ())),
        precision=lax.Precision.HIGHEST,
        preferred_element_type=f32,
    )

    def put(kb, cols, value):
        at = kb ^ c

        @pl.when(at % 2 == 0)
        def _():
            keep_o[at // 2, :, cols] = value

        @pl.when(at % 2 == 1)
        def _():
            send_o[at // 2, :, cols] = value

    def zero_step(kb, carry):
        put(kb, slice(None), jnp.zeros((ROWS, 2 * n), bf16))
        return carry

    lax.fori_loop(nb, 4, zero_step, 0)
    for pair in range(heads // 2):
        at = pair * 128

        def step(kb, carry, at=at, pair=pair):
            rows = pl.ds(pl.multiple_of(kb * ROWS, ROWS), ROWS)
            dks, dvs, dqs = [], [], []
            for i in range(2):
                lo = at + i * HD
                h = 2 * pair + i
                kh = kvs[rows, lo : lo + HD]
                vh = kvs[rows, n + lo : n + lo + HD]
                qh = q[:, lo : lo + HD]
                dh = do_s[:, lo : lo + HD]
                p = jnp.exp(mm_t(kh, qh) + bias[rows, :] - lse[h : h + 1, :])
                ds = (p * (mm_t(vh, dh) - delta[h : h + 1, :])).astype(bf16)
                dvs.append(mm(p.astype(bf16), dh))
                dks.append(mm(ds, qh))
                dqs.append(carry[i] + t_mm(kh, ds))
            put(kb, slice(at, at + 128), jnp.concatenate(dks, axis=1).astype(bf16))
            put(kb, slice(n + at, n + at + 128), jnp.concatenate(dvs, axis=1).astype(bf16))
            return tuple(dqs)

        zero = jnp.zeros((HD, ROWS), f32)
        dqs = lax.fori_loop(0, nb, step, (zero, zero))
        dqt[at : at + HD, :] = dqs[0]
        dqt[at + HD : at + 128, :] = dqs[1]
    lane = lane_id(ROWS)
    for g in range(n // 128):
        v = dqt[g * 128 : (g + 1) * 128, :].T * (HD**-0.5)
        dq_o[:, g * 128 : (g + 1) * 128] = (v * cos[...] - partner(v, lane) * sin[...]).astype(bf16)


def proj_back_body(sc, dq, keep, near, recv, w, cos, sin, dp_o, own_o, oth_o):
    y = sc[1]
    n = dq.shape[1]
    lane = lane_id(ROWS)
    dp_o[:, :n] = dq[...]
    for g in range(2 * n // 128):
        cols = slice(g * 128, (g + 1) * 128)
        v = keep[0, :, cols].astype(f32) + near[0, :, cols].astype(f32) + recv[:, cols].astype(f32)
        if g < n // 128:
            v = v * cos[...] - partner(v, lane) * sin[...]
        dp_o[:, n + g * 128 : n + (g + 1) * 128] = v.astype(bf16)
    own = pl.ds(pl.multiple_of(y * HALF, HALF), HALF)
    oth = pl.ds(pl.multiple_of((1 - y) * HALF, HALF), HALF)
    oth_o[...] = mm_t(dp_o[...], w[oth, : 3 * n]).astype(bf16)
    own_o[...] = mm_t(dp_o[...], w[own, : 3 * n])


def slots_onehot(ids, r):
    i = lax.broadcasted_iota(jnp.int32, (4 * CAP, ROWS), 0)
    hit = (i == ids[2 * r : 2 * r + 1, :]) | (i == ids[2 * r + 1 : 2 * r + 2, :])
    return jnp.where(hit, 1.0, 0.0).astype(bf16)


def pack_body(sc, ids, b0, b1, b2, b3, p0, p1, p2, p3):
    for r, ref in enumerate((b0, b1, b2, b3)):
        rows = mm(slots_onehot(ids, r), ref[...]).astype(bf16)
        for s, out in enumerate((p0, p1, p2, p3)):
            out[r * CAP : (r + 1) * CAP, :] = rows[s * CAP : (s + 1) * CAP, :]


def unpack_body(sc, ids, p0, p1, p2, p3, keep_b, send_b, keep_o, send_o):
    for r in (1, 3, 0, 2):
        rows = jnp.concatenate(
            [p[r * CAP : (r + 1) * CAP, :] for p in (p0, p1, p2, p3)], axis=0
        )
        tok = t_mm(slots_onehot(ids, r), rows).astype(bf16)
        for at, pair in ((0, (keep_b, send_b)), (HALF, (keep_o, send_o))):
            pair[r % 2][r // 2] = tok[:, at : at + HALF]


def halves(y, a, b):
    first = y == 0
    return jnp.concatenate([jnp.where(first, a, b), jnp.where(first, b, a)], axis=1)


def ffn_body(routed, sc, xa, xb, wa, wb, weights, rt, *refs):
    if routed:
        refs = refs[len(refs) - 8 :]
        back_o, rg_o, dgu_o, y_o, x_o, de_o, acc_o, acc_b = refs
    else:
        back_o, dgu_o, y_o, acc_o, acc_b = refs[len(refs) - 5 :]
    y, e = sc[1], sc[2]
    x = halves(y, xa[...], xb[...])
    w = halves(y, wa[...], wb[...])
    hidden = weights.shape[3]
    if routed:
        lane = lane_id(ROWS)
        logits = jnp.where(lane < E, mm(x, rt[...]), NEG)
        ex = jnp.exp(logits - jnp.max(logits, axis=1, keepdims=True))
        probs = ex / jnp.sum(ex, axis=1, keepdims=True)
        gate = jnp.sum(jnp.where(lane == e, probs, 0.0), axis=1, keepdims=True)
        x_o[0] = x
        de_o[0] = (w.astype(f32) * gate).astype(bf16)
    acc_o[...] = jnp.zeros_like(acc_o)
    acc_b[...] = jnp.zeros_like(acc_b)
    tile = 256

    def columns(which, lo):
        cols = pl.ds(pl.multiple_of(lo, tile), tile)
        return jnp.concatenate(
            [weights[j, which, :, cols] for j in range(weights.shape[0])], axis=0
        )

    def step(j, dots):
        lo = pl.multiple_of(j * tile, tile)
        hi = pl.multiple_of(hidden + j * tile, tile)
        g = mm(x, columns(0, lo))
        u = mm(x, columns(1, lo))
        h = mm(w, columns(2, lo))
        sg = 1.0 / (1.0 + jnp.exp(-g))
        act = g * sg
        yv = (act * u).astype(bf16)
        if routed:
            dots = dots + jnp.sum(yv.astype(f32) * h, axis=1, keepdims=True)
            h = h * gate
        dg = (h * u * (sg + act * (1.0 - sg))).astype(bf16)
        du = (h * act).astype(bf16)
        y_o[0, :, pl.ds(lo, tile)] = yv
        dgu_o[0, :, pl.ds(lo, tile)] = dg
        dgu_o[0, :, pl.ds(hi, tile)] = du
        acc_o[...] += mm_t(yv, columns(2, lo))
        acc_b[...] += mm_t(dg, columns(0, lo)) + mm_t(du, columns(1, lo))
        return dots

    dots = lax.fori_loop(0, hidden // tile, step, jnp.zeros((ROWS, 1), f32))
    if routed:
        coef = (dots * gate) * (jnp.where(lane == e, 1.0, 0.0) - probs)
        coef = jnp.where(lane < E, coef, 0.0).astype(bf16)
        acc_b[...] += mm_t(coef, rt[...])
        rg_o[...] = t_mm(x, coef)
    for i, at in enumerate((y, 1 - y)):
        cols = pl.ds(pl.multiple_of(at * HALF, HALF), HALF)
        out = acc_o[:, cols]
        if routed:
            out = out * gate
        back_o[i, :, :HALF] = acc_b[:, cols].astype(bf16)
        back_o[i, :, HALF:] = out.astype(bf16)


def ffn(scalars, s, groups, xa, xb, wa, wb, weights, rt, prev, deps=()):
    routed = rt is not None
    hidden = weights.shape[3]
    full = lambda shape: pl.BlockSpec(shape, lambda i, n=len(shape): (0,) * n)
    part = lambda width: pl.BlockSpec((1, ROWS, width), lambda i: (s, 0, 0))
    two = (2, ROWS, D)
    outs = [sds(two, bf16)]
    out_specs = [full(two)]
    if routed:
        outs.append(sds((D, 128), f32))
        out_specs.append(full((D, 128)))
    widths = [2 * hidden, hidden] + ([D, D] if routed else [])
    base = len(outs)
    for width in widths:
        outs.append(sds((groups, ROWS, width), bf16))
        out_specs.append(part(width))
    args = [xa, xb, wa, wb, weights] + ([rt] if routed else [])
    in_specs = [SMEM] + [full(a.shape) for a in args]
    aliases = {}
    if not routed:
        args.append(scalars)
        in_specs.append(SMEM)
    for arr in deps:
        args.append(arr)
        in_specs.append(pl.BlockSpec(memory_space=pl.ANY))
    if prev is not None:
        for i, arr in enumerate(prev):
            aliases[1 + len(args)] = base + i
            args.append(arr)
            in_specs.append(pl.BlockSpec(memory_space=pl.ANY))
    return pl.pallas_call(
        functools.partial(ffn_body, routed),
        grid=(1,),
        out_shape=outs,
        in_specs=in_specs,
        out_specs=out_specs,
        scratch_shapes=[pltpu.VMEM((ROWS, D), f32), pltpu.VMEM((ROWS, D), f32)],
        input_output_aliases=aliases,
        compiler_params=pltpu.CompilerParams(vmem_limit_bytes=VMEM_LIMIT),
        cost_estimate=pl.CostEstimate(flops=int(16e9) if routed else 0, bytes_accessed=0, transcendentals=0),
        name="expert_ffn" if routed else "shared_ffn",
    )(scalars, *args)


def grad_blocks(offs, rows, pairs):
    tile = 384
    total = sum(b.shape[1] for _, b in pairs)

    def body(sc, *refs):
        keep, send, acc = refs[-3:]
        lo = 0
        for i in range(len(pairs)):
            a, b = refs[2 * i], refs[2 * i + 1]
            turned = a[...].T
            for j in range(0, b.shape[1], tile):
                width = min(tile, b.shape[1] - j)
                acc[:, :width] = mm(turned, b[:, j : j + width])
                for k in range(16):
                    at = pl.ds(pl.multiple_of(sc[k], 16), rows)
                    out = send if (k // 4) % 2 else keep
                    out[k // 8, k % 4, :, lo : lo + width] = acc[at, :width].astype(bf16)
                lo += width

    shape = sds((2, 4, rows, total), bf16)
    args = [m for pair in pairs for m in pair]
    return call(body, [shape, shape], scratch=[pltpu.VMEM((D, tile), f32)], us=3.0, name="grad_blocks")(
        offs, *args
    )


def per_device(
    tokens,
    segments,
    experts,
    attn_gain,
    qkv_proj,
    out_proj,
    ffn_gain,
    router_proj,
    expert_gate_up,
    expert_down,
    shared_gate_up,
    shared_down,
    cotangent,
):
    F, C = lax.axis_size("fsdp"), lax.axis_size("ctx")
    f, c, y = lax.axis_index("fsdp"), lax.axis_index("ctx"), lax.axis_index("tp")
    EL = expert_gate_up.shape[0]
    small = F == EL and C == 4
    heads_width = qkv_proj.shape[2]
    hidden = expert_down.shape[1]
    shared_hidden = shared_down.shape[0]
    zi = f % EL
    i32 = jnp.int32

    def yx(v):
        return lax.ppermute(v, "tp", [(0, 1), (1, 0)])

    def cx(v, flip):
        return lax.ppermute(v, "ctx", [(i, i ^ flip) for i in range(C)])

    def zs(v, s):
        return lax.ppermute(
            v, "fsdp", [(i, i // EL * EL + (i % EL + s) % EL) for i in range(F)]
        )

    scalars = jnp.stack([c, y, EL * c + zi]).astype(i32)
    rows_own = D // (F * C)
    rc = jnp.arange(4, dtype=i32)
    if small:
        dense_offs = (
            (((f - rc)[None, :] % 4) * 4 + (c ^ rc)[:, None]).reshape(16) * rows_own
        ).astype(i32)
        back_offs = (
            (((f + rc)[None, :] % 4) * 4 + (c ^ rc)[:, None]).reshape(16) * rows_own
        ).astype(i32)

    def gathered(shard, axis=0):
        return lax.all_gather(shard, ("fsdp", "ctx"), axis=axis, tiled=True)

    def reduce_near(keep, send):
        kind = keep.dtype
        near = cx(send, 1)
        far = cx((keep[1].astype(f32) + near[1].astype(f32)).astype(kind), 2)
        return keep[0].astype(f32) + near[0].astype(f32) + far.astype(f32)

    def reduce_far(part, kind, z_after=None, sum_after=None):
        pieces = [part[s].astype(kind) for s in (1, 2, 3)]
        if z_after is not None:
            pieces = [after(piece, z_after) for piece in pieces]
        total = part[0] if sum_after is None else after(part[0], sum_after)
        for s, piece in zip((1, 2, 3), pieces):
            total = total + zs(piece, s).astype(f32)
        return total

    def grad_of(a, b):
        return lax.dot_general(a, b, (((0,), (0,)), ((), ())), preferred_element_type=f32)

    def dense_reduce(pairs):
        full = jnp.concatenate([grad_of(a, b) for a, b in pairs], axis=1)
        return lax.psum_scatter(full, ("fsdp", "ctx"), scatter_dimension=0, tiled=True)

    def half(v, which):
        return lax.dynamic_slice_in_dim(v, which * HALF, HALF, v.ndim - 1)

    qkv_shard = jnp.concatenate(
        [
            qkv_proj.transpose(1, 0, 2).reshape(rows_own, 3 * heads_width),
            router_proj,
            attn_gain[:, None],
            ffn_gain[:, None],
            jnp.zeros((rows_own, 128 - E - 2), bf16),
        ],
        axis=1,
    )
    first = gathered(jnp.concatenate([qkv_shard, out_proj.T], axis=1))
    extra = first[:, 3 * heads_width : 3 * heads_width + 128]
    out_w = first[:, 3 * heads_width + 128 :]
    gains = extra[:, E : E + 2].astype(f32)
    gain_one, gain_two = gains[:, 0], gains[:, 1]
    gain_two_h = half(gain_two, y)
    gain_one_h = half(gain_one, y)
    shared_shard = jnp.concatenate([shared_gate_up, shared_down.T[None]])
    expert_local = jnp.concatenate(
        [expert_gate_up, expert_down.transpose(0, 2, 1)[:, None]], axis=1
    )
    if small:
        expert_w = None
    else:
        inner = [[g * EL + i for i in range(EL)] for g in range(F // EL)]
        outer = [[g * EL + i for g in range(F // EL)] for i in range(EL)]
        mine = lax.all_to_all(
            expert_local, "fsdp", 0, 0, axis_index_groups=inner, tiled=True
        )
        mine = lax.all_gather(mine, "fsdp", axis=0, axis_index_groups=outer, tiled=True)
        expert_w = mine.transpose(1, 0, 2, 3).reshape(1, 3, D, hidden)

    lanes = jnp.arange(E, dtype=i32)[None, :]
    named = [(experts[:, k : k + 1] == lanes) for k in range(2)]
    both = (named[0] | named[1]).astype(bf16)
    before = (jnp.arange(ROWS)[:, None] > jnp.arange(ROWS)[None, :]).astype(bf16)
    counts = jnp.dot(before, both, preferred_element_type=f32)
    code = jnp.stack(
        [
            experts[:, k] * CAP + jnp.sum(jnp.where(named[k], counts, 0.0), axis=1).astype(i32)
            for k in range(2)
        ]
    )
    code_two = jnp.stack([code, cx(code, 2)])
    code_core = cx(code_two, 1)
    codes = jnp.concatenate([code_two[0], code_core[0], code_two[1], code_core[1]], axis=0)
    which, rank = codes // CAP, codes % CAP
    ids = jnp.where(which // EL == c, ((which - zi) % EL) * CAP + rank, -1).astype(i32)

    def dispatch(own, dep=None):
        far = cx(own, 2)
        near = cx(own, 1)
        both_far = cx(far, 1)
        packs = call(
            pack_body, [sds((4 * CAP, HALF), bf16)] * 4, name="pack"
        )(scalars, ids if dep is None else after(ids, *dep), own, near, far, both_far)
        return [packs[0]] + [zs(packs[s], s) for s in (1, 2, 3)]

    def sum_pieces(pieces, dep=None):
        total = pieces[0]
        if dep is not None:
            total = after(total, dep)
        for piece in pieces[1:]:
            total = total + piece.astype(f32)
        return total

    def over_tp(two):
        return (two[0].astype(f32) + yx(two[1]).astype(f32)).astype(bf16)

    def home(s, total):
        return total if s == 0 else zs(total, EL - s)

    def over_ctx(keep, send):
        got = cx(send, 1)
        far = (keep[1].astype(f32) + got[1].astype(f32)).astype(bf16)
        return keep[0].astype(f32) + got[0].astype(f32) + cx(far, 2).astype(f32)

    cot_h, cot_o = half(cotangent, y), half(cotangent, 1 - y)
    cot_rows = dispatch(cot_h)
    cot_pairs = [(rows, yx(rows)) for rows in cot_rows]

    positions = (c * ROWS + jnp.arange(ROWS, dtype=i32)).astype(f32)
    table = jnp.arange(128, dtype=i32)
    frequency = 10000.0 ** (-(table % 32).astype(f32) / 32)
    angles = positions[:, None] * frequency[None, :]
    cos = jnp.cos(angles)
    sin = jnp.sin(angles) * jnp.where(table % 64 < 32, -1.0, 1.0)[None, :]
    normed_one, queries, kv = call(
        qkv_body,
        [sds((ROWS, D), bf16), sds((ROWS, heads_width), bf16), sds((ROWS, 2 * heads_width), bf16)],
        us=5.0, name="qkv",
    )(
        scalars, tokens, gain_one[None, :], first, cos, sin,
        deps=[cot_pairs[0][1], *cot_rows[1:], expert_local],
    )
    kv_far = cx(kv, 2)
    kv_near = cx(kv, 1)
    kv_both = cx(kv_far, 1)
    kvs = (kv, kv_near, kv_far, kv_both)
    if small:
        expert_w = lax.all_to_all(
            after(expert_local, *cot_rows[1:]), "fsdp", 0, 0, tiled=True
        )
    before_attn = []
    seq_ids = segments[0]
    seg_col = seq_ids[:, None]
    seg_row = lax.dynamic_slice_in_dim(seq_ids, c * ROWS, ROWS, 0)[None, :]
    attended, z_own, z_oth, lse = call(
        attn_body,
        [
            sds((ROWS, heads_width), bf16),
            sds((ROWS, HALF), f32),
            sds((ROWS, HALF), bf16),
            sds((8, ROWS), f32),
        ],
        scratch=[
            pltpu.VMEM((4 * ROWS, 2 * heads_width), bf16),
            pltpu.VMEM((4 * ROWS, ROWS), f32),
            pltpu.VMEM((4 * ROWS, ROWS), f32),
            pltpu.VMEM((heads_width, ROWS), f32),
        ],
        us=17.0, name="attn",
    )(scalars, queries, *kvs, seg_col, seg_row, out_w, deps=before_attn)
    tok_h = half(tokens, y).astype(f32)
    middle = tok_h + z_own + yx(z_oth).astype(f32)

    def whole_rows(own):
        return halves(y, own, yx(own))

    def both_halves(sums):
        return sums + yx(sums)

    square = both_halves(jnp.sum(middle * middle, axis=1))
    scale_two = lax.rsqrt(square / D + eps)[:, None]
    normal_two = middle * scale_two
    normed_two = (normal_two * gain_two_h[None, :]).astype(bf16)

    normed_two_oth = yx(normed_two)
    rows_in = dispatch(normed_two, [normed_two_oth])
    shared_w = gathered(after(shared_shard, rows_in[3]), 1)[None]
    saved, backs, sums, router_part = None, [None] * 4, [], 0.0
    tied = [rows_in[0]] + [after(rows, *[pair[1] for pair in cot_pairs]) for rows in rows_in[1:]]
    pairs = [(rows, yx(rows)) for rows in tied]
    for i, s in enumerate((2, 1, 3, 0)):
        deps = [rows_in[1:], [pairs[3][1], pairs[0][1]], sums[:1], sums[1:2]][i]
        res = ffn(scalars, s, 4, *pairs[s], *cot_pairs[s], expert_w, extra, saved, deps)
        sums.append(over_tp(res[0]))
        backs[s] = home(s, sums[i])
        router_part = router_part + res[1][:, :E]
        saved = res[2:]
    ex_dgu, ex_y, ex_x, ex_de = [v.reshape(4 * ROWS, -1) for v in saved]
    ex_x = after(ex_x, backs[2])

    grad_w = [
        lax.dot_general(a, b, (((0,), (0,)), ((), ())), preferred_element_type=f32)
        for a, b in ((ex_x, ex_dgu[:, :hidden]), (ex_x, ex_dgu[:, hidden:]), (ex_de, ex_y))
    ]
    if small:
        grad_w = [g.astype(bf16).reshape(4, D // 4, hidden) for g in grad_w]
        grad_w = grad_ready = jnp.stack(grad_w, axis=1)
        grad_w = lax.all_to_all(
            grad_w, "fsdp", 0, 0, tiled=True
        )
    else:
        grad_ready = saved[0]
        grad_w = jnp.stack([g.reshape(F, D // F, hidden) for g in grad_w], axis=1)
        grad_w = lax.psum_scatter(
            grad_w, "fsdp", scatter_dimension=0, axis_index_groups=outer, tiled=True
        )
        grad_w = lax.all_to_all(grad_w, "fsdp", 0, 0, axis_index_groups=inner, tiled=True)

    sh_back, sh_dgu, sh_y = ffn(
        scalars, 0, 1, normed_two, normed_two_oth, cot_h, cot_o, shared_w, None, None,
        [grad_ready, backs[1], backs[3]],
    )
    sh_sum = sh_back[0].astype(f32) + yx(sh_back[1]).astype(f32)
    normed_full = halves(y, normed_two, normed_two_oth)
    shared_full = jnp.concatenate(
        [grad_of(normed_full, sh_dgu[0]), grad_of(cotangent, sh_y[0])], axis=1
    )
    shared_full = shared_full.astype(bf16) if small else shared_full
    shared_grad = lax.psum_scatter(
        shared_full,
        ("fsdp", "ctx"), scatter_dimension=0, tiled=True,
    ).astype(f32)

    keep_b, send_b, keep_o, send_o = call(
        unpack_body, [sds((2, ROWS, HALF), bf16)] * 4, us=0.0, name="unpack"
    )(scalars, ids, *backs, deps=[sh_sum])
    back_h = over_ctx(keep_b, send_b) + sh_sum[:, :HALF]
    scaled = back_h * gain_two_h[None, :]
    mean_two = both_halves(jnp.sum(scaled * normal_two, axis=1))[:, None] / D
    ffn_gain_part = jnp.sum(back_h * normal_two, axis=0)
    middle_grad = cot_h.astype(f32) + scale_two * (scaled - normal_two * mean_two)
    dz_own = middle_grad.astype(bf16)
    dz_oth = yx(dz_own)
    dq, dkv_keep, dkv_send = call(
        attn_back_body,
        [sds((ROWS, heads_width), bf16)] + [sds((2, ROWS, 2 * heads_width), bf16)] * 2,
        scratch=[
            pltpu.VMEM((4 * ROWS, 2 * heads_width), bf16),
            pltpu.VMEM((4 * ROWS, ROWS), f32),
            pltpu.VMEM((ROWS, heads_width), bf16),
            pltpu.VMEM((8, ROWS), f32),
            pltpu.VMEM((heads_width, ROWS), f32),
        ],
        us=0.0, name="attn_back",
    )(
        scalars, queries, *kvs, seg_col, seg_row, lse, attended, dz_own, dz_oth, out_w, cos, sin,
        deps=[shared_full],
    )
    dkv_near = cx(dkv_send, 1)
    kv_recv = cx((dkv_keep[1].astype(f32) + dkv_near[1].astype(f32)).astype(bf16), 2)
    dp, da_own, da_oth = call(
        proj_back_body,
        [sds((ROWS, 3 * heads_width), bf16), sds((ROWS, HALF), f32), sds((ROWS, HALF), bf16)],
        us=5.0, name="proj_back",
    )(scalars, dq, dkv_keep, dkv_near, kv_recv, first, cos, sin, deps=[grad_w])
    dense_pairs = [(normed_one, dp), (halves(y, dz_own, dz_oth), attended)]
    if small:
        dense_keep, dense_send = grad_blocks(back_offs, rows_own, dense_pairs)
        dense_part = reduce_near(dense_keep, dense_send)
    else:
        dense_keep = dense_part = dp
    da_h = after(da_own, dense_keep) + yx(da_oth).astype(f32)
    tok_full = tokens.astype(f32)
    scale_one = lax.rsqrt(jnp.mean(tok_full * tok_full, axis=1, keepdims=True) + eps)
    normal_one = tok_h * scale_one
    scaled_one = da_h * gain_one_h[None, :]
    mean_one = both_halves(jnp.sum(scaled_one * normal_one, axis=1))[:, None] / D
    attn_gain_part = jnp.sum(da_h * normal_one, axis=0)
    tokens_grad_h = middle_grad + scale_one * (scaled_one - normal_one * mean_one)

    tokens_grad = whole_rows(tokens_grad_h.astype(bf16)).astype(f32)

    layer_h = middle + over_ctx(keep_o, after(send_o, kv_recv)) + sh_sum[:, HALF:]
    layer_out = whole_rows(after(layer_h, tokens_grad_h).astype(bf16))
    grad_w = after(grad_w, tokens_grad_h, dense_part)
    expert_gate_up_grad = grad_w[:, :2].astype(f32)
    expert_down_grad = grad_w[:, 2].astype(f32).transpose(0, 2, 1)
    if small:
        dense_grad = reduce_far(dense_part, bf16)
    else:
        dense_grad = dense_reduce(dense_pairs)
    qkv_grad = dense_grad[:, : 3 * heads_width].reshape(rows_own, 3, heads_width).transpose(1, 0, 2)
    out_grad = dense_grad[:, 3 * heads_width :].T
    shared_gate_up_grad = jnp.stack(
        [shared_grad[:, :shared_hidden], shared_grad[:, shared_hidden : 2 * shared_hidden]]
    )
    shared_down_grad = shared_grad[:, 2 * shared_hidden :].T

    def placed(part):
        first = y == 0
        return jnp.concatenate([jnp.where(first, part, 0.0), jnp.where(first, 0.0, part)])

    tail = jnp.concatenate(
        [router_part, placed(attn_gain_part)[:, None], placed(ffn_gain_part)[:, None]], axis=1
    )
    tail = after(tail, dense_part).reshape(F * C, rows_own * (E + 2))
    tail = jnp.sum(lax.all_to_all(tail, ("fsdp", "ctx"), 0, 0, tiled=True), axis=0)
    tail = after(tail, dense_grad, expert_gate_up_grad, expert_down_grad)
    tail = tail.reshape(rows_own, E + 2)
    tail = tail + yx(tail)
    return (
        layer_out,
        tokens_grad,
        tail[:, E],
        qkv_grad,
        out_grad,
        tail[:, E + 1],
        tail[:, :E],
        expert_gate_up_grad,
        expert_down_grad,
        shared_gate_up_grad,
        shared_down_grad,
    )


def solution(mesh):
    return jax.shard_map(
        per_device,
        mesh=mesh,
        in_specs=(
            P(("fsdp", "ctx"), None),
            P("fsdp", None),
            P(("fsdp", "ctx"), None),
            P(("fsdp", "ctx")),
            P(None, ("fsdp", "ctx"), "tp"),
            P("tp", ("fsdp", "ctx")),
            P(("fsdp", "ctx")),
            P(("fsdp", "ctx"), None),
            P("ctx", None, "fsdp", "tp"),
            P("ctx", "tp", "fsdp"),
            P(None, ("fsdp", "ctx"), "tp"),
            P("tp", ("fsdp", "ctx")),
            P(("fsdp", "ctx"), None),
        ),
        out_specs=(
            P(("fsdp", "ctx"), None),
            P(("fsdp", "ctx"), None),
            P(("fsdp", "ctx")),
            P(None, ("fsdp", "ctx"), "tp"),
            P("tp", ("fsdp", "ctx")),
            P(("fsdp", "ctx")),
            P(("fsdp", "ctx"), None),
            P("ctx", None, "fsdp", "tp"),
            P("ctx", "tp", "fsdp"),
            P(None, ("fsdp", "ctx"), "tp"),
            P("tp", ("fsdp", "ctx")),
        ),
        check_vma=False,
    )
```

```python
import functools

import jax
import jax.numpy as jnp
from jax import lax
from jax.experimental import pallas as pl
from jax.experimental.pallas import tpu as pltpu
from jax.sharding import PartitionSpec as P

D = 768
HALF = D // 2
HD = 64
E = 16
ROWS = 512
CAP = 128
NEG = -1e30
eps = 1e-06
bf16 = jnp.bfloat16
f32 = jnp.float32
VMEM_LIMIT = 56 * 1024 * 1024


def mm(a, b):
    return lax.dot_general(a, b, (((1,), (0,)), ((), ())), preferred_element_type=f32)


def mm_t(a, b):
    return lax.dot_general(a, b, (((1,), (1,)), ((), ())), preferred_element_type=f32)


def t_mm(a, b):
    return lax.dot_general(a, b, (((0,), (0,)), ((), ())), preferred_element_type=f32)


def sds(shape, dtype):
    return jax.ShapeDtypeStruct(shape, dtype)


SMEM = pl.BlockSpec(memory_space=pltpu.SMEM)
VM = pl.BlockSpec(memory_space=pltpu.VMEM)


def call(body, outs, scratch=(), us=1.0, name=None):
    def run(scalars, *args, deps=()):
        count = 1 + len(args)

        def inner(*refs):
            body(*refs[:count], *refs[count + len(deps) :])

        return pl.pallas_call(
            inner,
            out_shape=outs,
            in_specs=[SMEM] + [VM] * len(args) + [pl.BlockSpec(memory_space=pl.ANY)] * len(deps),
            out_specs=jax.tree.map(lambda _: VM, outs),
            scratch_shapes=list(scratch),
            compiler_params=pltpu.CompilerParams(vmem_limit_bytes=VMEM_LIMIT),
            cost_estimate=pl.CostEstimate(
                flops=int(us * 1.1e9), bytes_accessed=0, transcendentals=0
            ),
            name=name,
        )(scalars, *args, *deps)

    return run


def after(v, *deps):
    return lax.optimization_barrier((v,) + deps)[0]


def partner(v, lane):
    return jnp.where(lane % 64 < 32, pltpu.roll(v, 96, 1), pltpu.roll(v, 32, 1))


def lane_id(rows):
    return lax.broadcasted_iota(jnp.int32, (rows, 128), 1)


def qkv_body(sc, tok, gain, w, cos, sin, a_o, q_o, kv_o):
    x = tok[...].astype(f32)
    scale = lax.rsqrt(jnp.mean(x * x, axis=1, keepdims=True) + eps)
    a = (x * scale * gain[...]).astype(bf16)
    a_o[...] = a
    n = q_o.shape[1]
    lane = lane_id(ROWS)
    for g in range(3 * n // 128):
        v = mm(a, w[:, g * 128 : (g + 1) * 128])
        lo = g * 128
        if lo < n:
            r = v * cos[...] + partner(v, lane) * sin[...]
            q_o[:, lo : lo + 128] = (r.astype(bf16).astype(f32) * (HD**-0.5)).astype(bf16)
        elif lo < 2 * n:
            r = v * cos[...] + partner(v, lane) * sin[...]
            kv_o[:, lo - n : lo - n + 128] = r.astype(bf16)
        else:
            kv_o[:, lo - n : lo - n + 128] = v.astype(bf16)


def block_bias(c, kb, segc, segq):
    off = pl.multiple_of(kb * ROWS, ROWS)
    kpos = off + lax.broadcasted_iota(jnp.int32, (ROWS, ROWS), 0)
    qpos = c * ROWS + lax.broadcasted_iota(jnp.int32, (ROWS, ROWS), 1)
    ok = (segc[pl.ds(off, ROWS), :] == segq[...]) & (kpos <= qpos)
    return jnp.where(ok, 0.0, NEG)


def attn_body(sc, q, k0, k1, k2, k3, segc, segq, wo, o_o, zown_o, zoth_o, lse_o, kvs, bias, st, ot):
    c, y = sc[0], sc[1]
    nb = c + 1
    n = q.shape[1]
    for r, ref in enumerate((k0, k1, k2, k3)):
        kvs[pl.ds(pl.multiple_of((c ^ r) * ROWS, ROWS), ROWS), :] = ref[...]

    def bias_step(kb, carry):
        bias[pl.ds(pl.multiple_of(kb * ROWS, ROWS), ROWS), :] = block_bias(c, kb, segc, segq)
        return carry

    lax.fori_loop(0, nb, bias_step, 0)
    for h in range(n // HD):
        lo = h * HD
        qh = q[:, lo : lo + HD]

        def score_step(kb, m, lo=lo, qh=qh):
            rows = pl.ds(pl.multiple_of(kb * ROWS, ROWS), ROWS)
            s = mm_t(kvs[rows, lo : lo + HD], qh) + bias[rows, :]
            st[rows, :] = s
            return jnp.maximum(m, jnp.max(s, axis=0, keepdims=True))

        m = lax.fori_loop(0, nb, score_step, jnp.full((1, ROWS), NEG, f32))

        def value_step(kb, carry, lo=lo, m=m):
            total, acc = carry
            rows = pl.ds(pl.multiple_of(kb * ROWS, ROWS), ROWS)
            p = jnp.exp(st[rows, :] - m)
            total = total + jnp.sum(p, axis=0, keepdims=True)
            return total, acc + t_mm(kvs[rows, n + lo : n + lo + HD], p.astype(bf16))

        total, acc = lax.fori_loop(
            0, nb, value_step, (jnp.zeros((1, ROWS), f32), jnp.zeros((HD, ROWS), f32))
        )
        ot[lo : lo + HD, :] = acc / total
        lse_o[h : h + 1, :] = m + jnp.log(total)
    o = ot[...].T.astype(bf16)
    o_o[...] = o
    own = pl.ds(pl.multiple_of(y * HALF, HALF), HALF)
    oth = pl.ds(pl.multiple_of((1 - y) * HALF, HALF), HALF)
    zoth_o[...] = mm_t(o, wo[oth, :]).astype(bf16)
    zown_o[...] = mm_t(o, wo[own, :])


def attn_back_body(
    sc, q, k0, k1, k2, k3, segc, segq, lse, o, zown, zoth, wo, cos, sin, dq_o, keep_o, send_o,
    kvs, bias, do_s, delta, dqt,
):
    c, y = sc[0], sc[1]
    nb = c + 1
    n = q.shape[1]
    heads = n // HD
    for r, ref in enumerate((k0, k1, k2, k3)):
        kvs[pl.ds(pl.multiple_of((c ^ r) * ROWS, ROWS), ROWS), :] = ref[...]

    def bias_step(kb, carry):
        bias[pl.ds(pl.multiple_of(kb * ROWS, ROWS), ROWS), :] = block_bias(c, kb, segc, segq)
        return carry

    lax.fori_loop(0, nb, bias_step, 0)
    own = pl.ds(pl.multiple_of(y * HALF, HALF), HALF)
    oth = pl.ds(pl.multiple_of((1 - y) * HALF, HALF), HALF)
    do = (mm(zown[...], wo[own, :]) + mm(zoth[...], wo[oth, :])).astype(bf16)
    do_s[...] = do
    pick = (
        lax.broadcasted_iota(jnp.int32, (8, n), 1) // HD
        == lax.broadcasted_iota(jnp.int32, (8, n), 0)
    ).astype(f32)
    delta[...] = lax.dot_general(
        pick,
        do.astype(f32) * o[...].astype(f32),
        (((1,), (1,)), ((), ())),
        precision=lax.Precision.HIGHEST,
        preferred_element_type=f32,
    )

    def put(kb, cols, value):
        at = kb ^ c

        @pl.when(at % 2 == 0)
        def _():
            keep_o[at // 2, :, cols] = value

        @pl.when(at % 2 == 1)
        def _():
            send_o[at // 2, :, cols] = value

    def zero_step(kb, carry):
        put(kb, slice(None), jnp.zeros((ROWS, 2 * n), bf16))
        return carry

    lax.fori_loop(nb, 4, zero_step, 0)
    for pair in range(heads // 2):
        at = pair * 128

        def step(kb, carry, at=at, pair=pair):
            rows = pl.ds(pl.multiple_of(kb * ROWS, ROWS), ROWS)
            dks, dvs, dqs = [], [], []
            for i in range(2):
                lo = at + i * HD
                h = 2 * pair + i
                kh = kvs[rows, lo : lo + HD]
                vh = kvs[rows, n + lo : n + lo + HD]
                qh = q[:, lo : lo + HD]
                dh = do_s[:, lo : lo + HD]
                p = jnp.exp(mm_t(kh, qh) + bias[rows, :] - lse[h : h + 1, :])
                ds = (p * (mm_t(vh, dh) - delta[h : h + 1, :])).astype(bf16)
                dvs.append(mm(p.astype(bf16), dh))
                dks.append(mm(ds, qh))
                dqs.append(carry[i] + t_mm(kh, ds))
            put(kb, slice(at, at + 128), jnp.concatenate(dks, axis=1).astype(bf16))
            put(kb, slice(n + at, n + at + 128), jnp.concatenate(dvs, axis=1).astype(bf16))
            return tuple(dqs)

        zero = jnp.zeros((HD, ROWS), f32)
        dqs = lax.fori_loop(0, nb, step, (zero, zero))
        dqt[at : at + HD, :] = dqs[0]
        dqt[at + HD : at + 128, :] = dqs[1]
    lane = lane_id(ROWS)
    for g in range(n // 128):
        v = dqt[g * 128 : (g + 1) * 128, :].T * (HD**-0.5)
        dq_o[:, g * 128 : (g + 1) * 128] = (v * cos[...] - partner(v, lane) * sin[...]).astype(bf16)


def proj_back_body(sc, dq, keep, near, recv, w, cos, sin, dp_o, own_o, oth_o):
    y = sc[1]
    n = dq.shape[1]
    lane = lane_id(ROWS)
    dp_o[:, :n] = dq[...]
    for g in range(2 * n // 128):
        cols = slice(g * 128, (g + 1) * 128)
        v = keep[0, :, cols].astype(f32) + near[0, :, cols].astype(f32) + recv[:, cols].astype(f32)
        if g < n // 128:
            v = v * cos[...] - partner(v, lane) * sin[...]
        dp_o[:, n + g * 128 : n + (g + 1) * 128] = v.astype(bf16)
    own = pl.ds(pl.multiple_of(y * HALF, HALF), HALF)
    oth = pl.ds(pl.multiple_of((1 - y) * HALF, HALF), HALF)
    oth_o[...] = mm_t(dp_o[...], w[oth, : 3 * n]).astype(bf16)
    own_o[...] = mm_t(dp_o[...], w[own, : 3 * n])


def slots_onehot(ids, r):
    i = lax.broadcasted_iota(jnp.int32, (4 * CAP, ROWS), 0)
    hit = (i == ids[2 * r : 2 * r + 1, :]) | (i == ids[2 * r + 1 : 2 * r + 2, :])
    return jnp.where(hit, 1.0, 0.0).astype(bf16)


def pack_body(sc, ids, b0, b1, b2, b3, p0, p1, p2, p3):
    for r, ref in enumerate((b0, b1, b2, b3)):
        rows = mm(slots_onehot(ids, r), ref[...]).astype(bf16)
        for s, out in enumerate((p0, p1, p2, p3)):
            out[r * CAP : (r + 1) * CAP, :] = rows[s * CAP : (s + 1) * CAP, :]


def unpack_body(sc, ids, p0, p1, p2, p3, keep_b, send_b, keep_o, send_o):
    for r in (1, 3, 0, 2):
        rows = jnp.concatenate(
            [p[r * CAP : (r + 1) * CAP, :] for p in (p0, p1, p2, p3)], axis=0
        )
        tok = t_mm(slots_onehot(ids, r), rows).astype(bf16)
        for at, pair in ((0, (keep_b, send_b)), (HALF, (keep_o, send_o))):
            pair[r % 2][r // 2] = tok[:, at : at + HALF]


def halves(y, a, b):
    first = y == 0
    return jnp.concatenate([jnp.where(first, a, b), jnp.where(first, b, a)], axis=1)


def ffn_body(routed, sc, xa, xb, wa, wb, weights, rt, *refs):
    if routed:
        refs = refs[len(refs) - 8 :]
        back_o, rg_o, dgu_o, y_o, x_o, de_o, acc_o, acc_b = refs
    else:
        back_o, dgu_o, y_o, acc_o, acc_b = refs[len(refs) - 5 :]
    y, e = sc[1], sc[2]
    x = halves(y, xa[...], xb[...])
    w = halves(y, wa[...], wb[...])
    hidden = weights.shape[3]
    if routed:
        lane = lane_id(ROWS)
        logits = jnp.where(lane < E, mm(x, rt[...]), NEG)
        ex = jnp.exp(logits - jnp.max(logits, axis=1, keepdims=True))
        probs = ex / jnp.sum(ex, axis=1, keepdims=True)
        gate = jnp.sum(jnp.where(lane == e, probs, 0.0), axis=1, keepdims=True)
        x_o[0] = x
        de_o[0] = (w.astype(f32) * gate).astype(bf16)
    acc_o[...] = jnp.zeros_like(acc_o)
    acc_b[...] = jnp.zeros_like(acc_b)
    tile = 512

    def columns(which, lo):
        cols = pl.ds(pl.multiple_of(lo, tile), tile)
        return jnp.concatenate(
            [weights[j, which, :, cols] for j in range(weights.shape[0])], axis=0
        )

    def step(j, dots):
        lo = pl.multiple_of(j * tile, tile)
        hi = pl.multiple_of(hidden + j * tile, tile)
        g = mm(x, columns(0, lo))
        u = mm(x, columns(1, lo))
        h = mm(w, columns(2, lo))
        sg = 1.0 / (1.0 + jnp.exp(-g))
        act = g * sg
        yv = (act * u).astype(bf16)
        if routed:
            dots = dots + jnp.sum(yv.astype(f32) * h, axis=1, keepdims=True)
            h = h * gate
        dg = (h * u * (sg + act * (1.0 - sg))).astype(bf16)
        du = (h * act).astype(bf16)
        y_o[0, :, pl.ds(lo, tile)] = yv
        dgu_o[0, :, pl.ds(lo, tile)] = dg
        dgu_o[0, :, pl.ds(hi, tile)] = du
        acc_o[...] += mm_t(yv, columns(2, lo))
        acc_b[...] += mm_t(dg, columns(0, lo)) + mm_t(du, columns(1, lo))
        return dots

    dots = lax.fori_loop(0, hidden // tile, step, jnp.zeros((ROWS, 1), f32))
    if routed:
        coef = (dots * gate) * (jnp.where(lane == e, 1.0, 0.0) - probs)
        coef = jnp.where(lane < E, coef, 0.0).astype(bf16)
        acc_b[...] += mm_t(coef, rt[...])
        rg_o[...] = t_mm(x, coef)
    for i, at in enumerate((y, 1 - y)):
        cols = pl.ds(pl.multiple_of(at * HALF, HALF), HALF)
        out = acc_o[:, cols]
        if routed:
            out = out * gate
        back_o[i, :, :HALF] = acc_b[:, cols].astype(bf16)
        back_o[i, :, HALF:] = out.astype(bf16)


def ffn(scalars, s, groups, xa, xb, wa, wb, weights, rt, prev, deps=()):
    routed = rt is not None
    hidden = weights.shape[3]
    full = lambda shape: pl.BlockSpec(shape, lambda i, n=len(shape): (0,) * n)
    part = lambda width: pl.BlockSpec((1, ROWS, width), lambda i: (s, 0, 0))
    two = (2, ROWS, D)
    outs = [sds(two, bf16)]
    out_specs = [full(two)]
    if routed:
        outs.append(sds((D, 128), f32))
        out_specs.append(full((D, 128)))
    widths = [2 * hidden, hidden] + ([D, D] if routed else [])
    base = len(outs)
    for width in widths:
        outs.append(sds((groups, ROWS, width), bf16))
        out_specs.append(part(width))
    args = [xa, xb, wa, wb, weights] + ([rt] if routed else [])
    in_specs = [SMEM] + [full(a.shape) for a in args]
    aliases = {}
    if not routed:
        args.append(scalars)
        in_specs.append(SMEM)
    for arr in deps:
        args.append(arr)
        in_specs.append(pl.BlockSpec(memory_space=pl.ANY))
    if prev is not None:
        for i, arr in enumerate(prev):
            aliases[1 + len(args)] = base + i
            args.append(arr)
            in_specs.append(pl.BlockSpec(memory_space=pl.ANY))
    return pl.pallas_call(
        functools.partial(ffn_body, routed),
        grid=(1,),
        out_shape=outs,
        in_specs=in_specs,
        out_specs=out_specs,
        scratch_shapes=[pltpu.VMEM((ROWS, D), f32), pltpu.VMEM((ROWS, D), f32)],
        input_output_aliases=aliases,
        compiler_params=pltpu.CompilerParams(vmem_limit_bytes=VMEM_LIMIT),
        cost_estimate=pl.CostEstimate(flops=int(16e9) if routed else 0, bytes_accessed=0, transcendentals=0),
        name="expert_ffn" if routed else "shared_ffn",
    )(scalars, *args)


def grad_blocks(offs, rows, pairs):
    tile = 384
    total = sum(b.shape[1] for _, b in pairs)

    def body(sc, *refs):
        keep, send, acc = refs[-3:]
        lo = 0
        for i in range(len(pairs)):
            a, b = refs[2 * i], refs[2 * i + 1]
            turned = a[...].T
            for j in range(0, b.shape[1], tile):
                width = min(tile, b.shape[1] - j)
                acc[:, :width] = mm(turned, b[:, j : j + width])
                for k in range(16):
                    at = pl.ds(pl.multiple_of(sc[k], 16), rows)
                    out = send if (k // 4) % 2 else keep
                    out[k // 8, k % 4, :, lo : lo + width] = acc[at, :width].astype(bf16)
                lo += width

    shape = sds((2, 4, rows, total), bf16)
    args = [m for pair in pairs for m in pair]
    return call(body, [shape, shape], scratch=[pltpu.VMEM((D, tile), f32)], us=3.0, name="grad_blocks")(
        offs, *args
    )


def per_device(
    tokens,
    segments,
    experts,
    attn_gain,
    qkv_proj,
    out_proj,
    ffn_gain,
    router_proj,
    expert_gate_up,
    expert_down,
    shared_gate_up,
    shared_down,
    cotangent,
):
    F, C = lax.axis_size("fsdp"), lax.axis_size("ctx")
    f, c, y = lax.axis_index("fsdp"), lax.axis_index("ctx"), lax.axis_index("tp")
    EL = expert_gate_up.shape[0]
    small = F == EL and C == 4
    heads_width = qkv_proj.shape[2]
    hidden = expert_down.shape[1]
    shared_hidden = shared_down.shape[0]
    zi = f % EL
    i32 = jnp.int32

    def yx(v):
        return lax.ppermute(v, "tp", [(0, 1), (1, 0)])

    def cx(v, flip):
        return lax.ppermute(v, "ctx", [(i, i ^ flip) for i in range(C)])

    def zs(v, s):
        return lax.ppermute(
            v, "fsdp", [(i, i // EL * EL + (i % EL + s) % EL) for i in range(F)]
        )

    scalars = jnp.stack([c, y, EL * c + zi]).astype(i32)
    rows_own = D // (F * C)
    rc = jnp.arange(4, dtype=i32)
    if small:
        dense_offs = (
            (((f - rc)[None, :] % 4) * 4 + (c ^ rc)[:, None]).reshape(16) * rows_own
        ).astype(i32)
        back_offs = (
            (((f + rc)[None, :] % 4) * 4 + (c ^ rc)[:, None]).reshape(16) * rows_own
        ).astype(i32)

    def gathered(shard, axis=0):
        return lax.all_gather(shard, ("fsdp", "ctx"), axis=axis, tiled=True)

    def reduce_near(keep, send):
        kind = keep.dtype
        near = cx(send, 1)
        far = cx((keep[1].astype(f32) + near[1].astype(f32)).astype(kind), 2)
        return keep[0].astype(f32) + near[0].astype(f32) + far.astype(f32)

    def reduce_far(part, kind, z_after=None, sum_after=None):
        pieces = [part[s].astype(kind) for s in (1, 2, 3)]
        if z_after is not None:
            pieces = [after(piece, z_after) for piece in pieces]
        total = part[0] if sum_after is None else after(part[0], sum_after)
        for s, piece in zip((1, 2, 3), pieces):
            total = total + zs(piece, s).astype(f32)
        return total

    def grad_of(a, b):
        return lax.dot_general(a, b, (((0,), (0,)), ((), ())), preferred_element_type=f32)

    def dense_reduce(pairs):
        full = jnp.concatenate([grad_of(a, b) for a, b in pairs], axis=1)
        return lax.psum_scatter(full, ("fsdp", "ctx"), scatter_dimension=0, tiled=True)

    def half(v, which):
        return lax.dynamic_slice_in_dim(v, which * HALF, HALF, v.ndim - 1)

    qkv_shard = jnp.concatenate(
        [
            qkv_proj.transpose(1, 0, 2).reshape(rows_own, 3 * heads_width),
            router_proj,
            attn_gain[:, None],
            ffn_gain[:, None],
            jnp.zeros((rows_own, 128 - E - 2), bf16),
        ],
        axis=1,
    )
    first = gathered(jnp.concatenate([qkv_shard, out_proj.T], axis=1))
    extra = first[:, 3 * heads_width : 3 * heads_width + 128]
    out_w = first[:, 3 * heads_width + 128 :]
    gains = extra[:, E : E + 2].astype(f32)
    gain_one, gain_two = gains[:, 0], gains[:, 1]
    gain_two_h = half(gain_two, y)
    gain_one_h = half(gain_one, y)
    shared_shard = jnp.concatenate([shared_gate_up, shared_down.T[None]])
    expert_local = jnp.concatenate(
        [expert_gate_up, expert_down.transpose(0, 2, 1)[:, None]], axis=1
    )
    if small:
        expert_w = None
    else:
        inner = [[g * EL + i for i in range(EL)] for g in range(F // EL)]
        outer = [[g * EL + i for g in range(F // EL)] for i in range(EL)]
        mine = lax.all_to_all(
            expert_local, "fsdp", 0, 0, axis_index_groups=inner, tiled=True
        )
        mine = lax.all_gather(mine, "fsdp", axis=0, axis_index_groups=outer, tiled=True)
        expert_w = mine.transpose(1, 0, 2, 3).reshape(1, 3, D, hidden)

    lanes = jnp.arange(E, dtype=i32)[None, :]
    named = [(experts[:, k : k + 1] == lanes) for k in range(2)]
    both = (named[0] | named[1]).astype(bf16)
    before = (jnp.arange(ROWS)[:, None] > jnp.arange(ROWS)[None, :]).astype(bf16)
    counts = jnp.dot(before, both, preferred_element_type=f32)
    code = jnp.stack(
        [
            experts[:, k] * CAP + jnp.sum(jnp.where(named[k], counts, 0.0), axis=1).astype(i32)
            for k in range(2)
        ]
    )
    code_two = jnp.stack([code, cx(code, 2)])
    code_core = cx(code_two, 1)
    codes = jnp.concatenate([code_two[0], code_core[0], code_two[1], code_core[1]], axis=0)
    which, rank = codes // CAP, codes % CAP
    ids = jnp.where(which // EL == c, ((which - zi) % EL) * CAP + rank, -1).astype(i32)

    def dispatch(own, dep=None):
        far = cx(own, 2)
        near = cx(own, 1)
        both_far = cx(far, 1)
        packs = call(
            pack_body, [sds((4 * CAP, HALF), bf16)] * 4, name="pack"
        )(scalars, ids if dep is None else after(ids, *dep), own, near, far, both_far)
        return [packs[0]] + [zs(packs[s], s) for s in (1, 2, 3)]

    def sum_pieces(pieces, dep=None):
        total = pieces[0]
        if dep is not None:
            total = after(total, dep)
        for piece in pieces[1:]:
            total = total + piece.astype(f32)
        return total

    def over_tp(two):
        return (two[0].astype(f32) + yx(two[1]).astype(f32)).astype(bf16)

    def home(s, total):
        return total if s == 0 else zs(total, EL - s)

    def over_ctx(keep, send):
        got = cx(send, 1)
        far = (keep[1].astype(f32) + got[1].astype(f32)).astype(bf16)
        return keep[0].astype(f32) + got[0].astype(f32) + cx(far, 2).astype(f32)

    cot_h, cot_o = half(cotangent, y), half(cotangent, 1 - y)
    cot_rows = dispatch(cot_h)
    cot_pairs = [(rows, yx(rows)) for rows in cot_rows]

    positions = (c * ROWS + jnp.arange(ROWS, dtype=i32)).astype(f32)
    table = jnp.arange(128, dtype=i32)
    frequency = 10000.0 ** (-(table % 32).astype(f32) / 32)
    angles = positions[:, None] * frequency[None, :]
    cos = jnp.cos(angles)
    sin = jnp.sin(angles) * jnp.where(table % 64 < 32, -1.0, 1.0)[None, :]
    normed_one, queries, kv = call(
        qkv_body,
        [sds((ROWS, D), bf16), sds((ROWS, heads_width), bf16), sds((ROWS, 2 * heads_width), bf16)],
        us=5.0, name="qkv",
    )(
        scalars, tokens, gain_one[None, :], first, cos, sin,
        deps=[cot_pairs[0][1], *cot_rows[1:], expert_local],
    )
    kv_far = cx(kv, 2)
    kv_near = cx(kv, 1)
    kv_both = cx(kv_far, 1)
    kvs = (kv, kv_near, kv_far, kv_both)
    if small:
        expert_w = lax.all_to_all(
            after(expert_local, *cot_rows[1:]), "fsdp", 0, 0, tiled=True
        )
    before_attn = []
    seq_ids = segments[0]
    seg_col = seq_ids[:, None]
    seg_row = lax.dynamic_slice_in_dim(seq_ids, c * ROWS, ROWS, 0)[None, :]
    attended, z_own, z_oth, lse = call(
        attn_body,
        [
            sds((ROWS, heads_width), bf16),
            sds((ROWS, HALF), f32),
            sds((ROWS, HALF), bf16),
            sds((8, ROWS), f32),
        ],
        scratch=[
            pltpu.VMEM((4 * ROWS, 2 * heads_width), bf16),
            pltpu.VMEM((4 * ROWS, ROWS), f32),
            pltpu.VMEM((4 * ROWS, ROWS), f32),
            pltpu.VMEM((heads_width, ROWS), f32),
        ],
        us=17.0, name="attn",
    )(scalars, queries, *kvs, seg_col, seg_row, out_w, deps=before_attn)
    tok_h = half(tokens, y).astype(f32)
    middle = tok_h + z_own + yx(z_oth).astype(f32)

    def whole_rows(own):
        return halves(y, own, yx(own))

    def both_halves(sums):
        return sums + yx(sums)

    square = both_halves(jnp.sum(middle * middle, axis=1))
    scale_two = lax.rsqrt(square / D + eps)[:, None]
    normal_two = middle * scale_two
    normed_two = (normal_two * gain_two_h[None, :]).astype(bf16)

    normed_two_oth = yx(normed_two)
    rows_in = dispatch(normed_two, [normed_two_oth])
    shared_w = gathered(after(shared_shard, rows_in[3]), 1)[None]
    saved, backs, sums, router_part = None, [None] * 4, [], 0.0
    tied = [rows_in[0]] + [after(rows, *[pair[1] for pair in cot_pairs]) for rows in rows_in[1:]]
    pairs = [(rows, yx(rows)) for rows in tied]
    for i, s in enumerate((2, 1, 3, 0)):
        deps = [rows_in[1:], [pairs[3][1], pairs[0][1]], sums[:1], sums[1:2]][i]
        res = ffn(scalars, s, 4, *pairs[s], *cot_pairs[s], expert_w, extra, saved, deps)
        sums.append(over_tp(res[0]))
        backs[s] = home(s, sums[i])
        router_part = router_part + res[1][:, :E]
        saved = res[2:]
    ex_dgu, ex_y, ex_x, ex_de = [v.reshape(4 * ROWS, -1) for v in saved]
    ex_x = after(ex_x, backs[2])

    grad_w = [
        lax.dot_general(a, b, (((0,), (0,)), ((), ())), preferred_element_type=f32)
        for a, b in ((ex_x, ex_dgu[:, :hidden]), (ex_x, ex_dgu[:, hidden:]), (ex_de, ex_y))
    ]
    if small:
        grad_w = [g.astype(bf16).reshape(4, D // 4, hidden) for g in grad_w]
        grad_w = grad_ready = jnp.stack(grad_w, axis=1)
        grad_w = lax.all_to_all(
            grad_w, "fsdp", 0, 0, tiled=True
        )
    else:
        grad_ready = saved[0]
        grad_w = jnp.stack([g.reshape(F, D // F, hidden) for g in grad_w], axis=1)
        grad_w = lax.psum_scatter(
            grad_w, "fsdp", scatter_dimension=0, axis_index_groups=outer, tiled=True
        )
        grad_w = lax.all_to_all(grad_w, "fsdp", 0, 0, axis_index_groups=inner, tiled=True)

    sh_back, sh_dgu, sh_y = ffn(
        scalars, 0, 1, normed_two, normed_two_oth, cot_h, cot_o, shared_w, None, None,
        [grad_ready, backs[1], backs[3]],
    )
    sh_sum = sh_back[0].astype(f32) + yx(sh_back[1]).astype(f32)
    normed_full = halves(y, normed_two, normed_two_oth)
    shared_full = jnp.concatenate(
        [grad_of(normed_full, sh_dgu[0]), grad_of(cotangent, sh_y[0])], axis=1
    )
    shared_full = shared_full.astype(bf16) if small else shared_full
    shared_grad = lax.psum_scatter(
        shared_full,
        ("fsdp", "ctx"), scatter_dimension=0, tiled=True,
    ).astype(f32)

    keep_b, send_b, keep_o, send_o = call(
        unpack_body, [sds((2, ROWS, HALF), bf16)] * 4, us=0.0, name="unpack"
    )(scalars, ids, *backs, deps=[sh_sum])
    back_h = over_ctx(keep_b, send_b) + sh_sum[:, :HALF]
    scaled = back_h * gain_two_h[None, :]
    mean_two = both_halves(jnp.sum(scaled * normal_two, axis=1))[:, None] / D
    ffn_gain_part = jnp.sum(back_h * normal_two, axis=0)
    middle_grad = cot_h.astype(f32) + scale_two * (scaled - normal_two * mean_two)
    dz_own = middle_grad.astype(bf16)
    dz_oth = yx(dz_own)
    dq, dkv_keep, dkv_send = call(
        attn_back_body,
        [sds((ROWS, heads_width), bf16)] + [sds((2, ROWS, 2 * heads_width), bf16)] * 2,
        scratch=[
            pltpu.VMEM((4 * ROWS, 2 * heads_width), bf16),
            pltpu.VMEM((4 * ROWS, ROWS), f32),
            pltpu.VMEM((ROWS, heads_width), bf16),
            pltpu.VMEM((8, ROWS), f32),
            pltpu.VMEM((heads_width, ROWS), f32),
        ],
        us=0.0, name="attn_back",
    )(
        scalars, queries, *kvs, seg_col, seg_row, lse, attended, dz_own, dz_oth, out_w, cos, sin,
        deps=[shared_full],
    )
    dkv_near = cx(dkv_send, 1)
    kv_recv = cx((dkv_keep[1].astype(f32) + dkv_near[1].astype(f32)).astype(bf16), 2)
    dp, da_own, da_oth = call(
        proj_back_body,
        [sds((ROWS, 3 * heads_width), bf16), sds((ROWS, HALF), f32), sds((ROWS, HALF), bf16)],
        us=5.0, name="proj_back",
    )(scalars, dq, dkv_keep, dkv_near, kv_recv, first, cos, sin, deps=[grad_w])
    dense_pairs = [(normed_one, dp), (halves(y, dz_own, dz_oth), attended)]
    if small:
        dense_keep, dense_send = grad_blocks(back_offs, rows_own, dense_pairs)
        dense_part = reduce_near(dense_keep, dense_send)
    else:
        dense_keep = dense_part = dp
    da_h = after(da_own, dense_keep) + yx(da_oth).astype(f32)
    tok_full = tokens.astype(f32)
    scale_one = lax.rsqrt(jnp.mean(tok_full * tok_full, axis=1, keepdims=True) + eps)
    normal_one = tok_h * scale_one
    scaled_one = da_h * gain_one_h[None, :]
    mean_one = both_halves(jnp.sum(scaled_one * normal_one, axis=1))[:, None] / D
    attn_gain_part = jnp.sum(da_h * normal_one, axis=0)
    tokens_grad_h = middle_grad + scale_one * (scaled_one - normal_one * mean_one)

    tokens_grad = whole_rows(tokens_grad_h.astype(bf16)).astype(f32)

    layer_h = middle + over_ctx(keep_o, after(send_o, kv_recv)) + sh_sum[:, HALF:]
    layer_out = whole_rows(after(layer_h, tokens_grad_h).astype(bf16))
    grad_w = after(grad_w, tokens_grad_h, dense_part)
    expert_gate_up_grad = grad_w[:, :2].astype(f32)
    expert_down_grad = grad_w[:, 2].astype(f32).transpose(0, 2, 1)
    if small:
        dense_grad = reduce_far(dense_part, bf16)
    else:
        dense_grad = dense_reduce(dense_pairs)
    qkv_grad = dense_grad[:, : 3 * heads_width].reshape(rows_own, 3, heads_width).transpose(1, 0, 2)
    out_grad = dense_grad[:, 3 * heads_width :].T
    shared_gate_up_grad = jnp.stack(
        [shared_grad[:, :shared_hidden], shared_grad[:, shared_hidden : 2 * shared_hidden]]
    )
    shared_down_grad = shared_grad[:, 2 * shared_hidden :].T

    def placed(part):
        first = y == 0
        return jnp.concatenate([jnp.where(first, part, 0.0), jnp.where(first, 0.0, part)])

    tail = jnp.concatenate(
        [router_part, placed(attn_gain_part)[:, None], placed(ffn_gain_part)[:, None]], axis=1
    )
    tail = after(tail, dense_part).reshape(F * C, rows_own * (E + 2))
    tail = jnp.sum(lax.all_to_all(tail, ("fsdp", "ctx"), 0, 0, tiled=True), axis=0)
    tail = after(tail, dense_grad, expert_gate_up_grad, expert_down_grad)
    tail = tail.reshape(rows_own, E + 2)
    tail = tail + yx(tail)
    return (
        layer_out,
        tokens_grad,
        tail[:, E],
        qkv_grad,
        out_grad,
        tail[:, E + 1],
        tail[:, :E],
        expert_gate_up_grad,
        expert_down_grad,
        shared_gate_up_grad,
        shared_down_grad,
    )


def solution(mesh):
    return jax.shard_map(
        per_device,
        mesh=mesh,
        in_specs=(
            P(("fsdp", "ctx"), None),
            P("fsdp", None),
            P(("fsdp", "ctx"), None),
            P(("fsdp", "ctx")),
            P(None, ("fsdp", "ctx"), "tp"),
            P("tp", ("fsdp", "ctx")),
            P(("fsdp", "ctx")),
            P(("fsdp", "ctx"), None),
            P("ctx", None, "fsdp", "tp"),
            P("ctx", "tp", "fsdp"),
            P(None, ("fsdp", "ctx"), "tp"),
            P("tp", ("fsdp", "ctx")),
            P(("fsdp", "ctx"), None),
        ),
        out_specs=(
            P(("fsdp", "ctx"), None),
            P(("fsdp", "ctx"), None),
            P(("fsdp", "ctx")),
            P(None, ("fsdp", "ctx"), "tp"),
            P("tp", ("fsdp", "ctx")),
            P(("fsdp", "ctx")),
            P(("fsdp", "ctx"), None),
            P("ctx", None, "fsdp", "tp"),
            P("ctx", "tp", "fsdp"),
            P(None, ("fsdp", "ctx"), "tp"),
            P("tp", ("fsdp", "ctx")),
        ),
        check_vma=False,
    )
```
